128 devices in a mesh: ep: 32 (over y, x, core), tp: 4 (over z).
Axes of the slice: x: 4, y: 4, z: 4, core: 2. Of those that a mesh axis runs over, the one named last changes fastest.
Arguments:
- queries: bfloat16 [512, 128, 576], P(('ep', 'tp')), may hold values from -45 to 45
- kv_cache: bfloat16 [512, 512, 576], P(('ep', 'tp')), may hold values from -5 to 5
- new_latent: bfloat16 [512, 576], P(('ep', 'tp')), may hold values from -5 to 5
- lengths: int32 [512], P(('ep', 'tp')), may hold values from 2 to 512, as said below
- residual: bfloat16 [512, 7168], P('ep', 'tp'), may hold values from -6 to 6
- gain_first: bfloat16 [7168], P('tp'), may hold values from 0.099609375 to 1.8984375
- gain_second: bfloat16 [7168], P('tp'), may hold values from 0.099609375 to 1.8984375
- value_proj: bfloat16 [128, 512, 128], P('ep'), may hold values from -0.25 to 0.25
- out_proj: bfloat16 [16384, 7168], P('ep', 'tp'), may hold values from -0.046875 to 0.046875
- dense_gate: bfloat16 [7168, 12288], P('tp', 'ep'), may hold values from -0.0625 to 0.0625
- dense_up: bfloat16 [7168, 12288], P('tp', 'ep'), may hold values from -0.0625 to 0.0625
- dense_down: bfloat16 [12288, 7168], P('ep', 'tp'), may hold values from -0.0546875 to 0.0546875
- route_ids: int32 [512, 8], P('ep'), may hold values from 0 to 31, all different within a row; in each aligned block of 16 rows (0 to 15, 16 to 31, ...) at most 6 rows name the same one
- route_gates: float32 [512, 8], P('ep'), may hold values from 0.1 to 0.6
- expert_gate: bfloat16 [32, 7168, 1024], P('ep', None, 'tp'), may hold values from -0.0625 to 0.0625
- expert_up: bfloat16 [32, 7168, 1024], P('ep', None, 'tp'), may hold values from -0.0625 to 0.0625
- expert_down: bfloat16 [32, 1024, 7168], P('ep', 'tp'), may hold values from -0.1875 to 0.1875
Outputs:
- hidden_out: bfloat16 [512, 7168], P('ep', 'tp')
The draws below stay inside these ranges and needn't reach their ends.
Inputs may be any that keep to these rules, and one draw needn't show every extreme that they name: `lengths`: each device's first request has all 512 slots live. `route_ids`: in each aligned block of 16 rows no expert is named by more than 6 rows.
All inputs are finite; a program needn't handle non-finite values.
Results may differ from the reference program's by a relative error of at most 0.024.
Values may be sent and summed in bfloat16 or wider, within the bound.
No kernel may reach another device: no remote copies, remote signals or barrier semaphores. Data moves between devices by JAX's collectives and lax.ppermute only.
A program may use at most 128 MiB of HBM per device.

```python
import math
import jax
import jax.numpy as jnp
import numpy as np
from jax import lax

D = 7168
H = 128
LAT = 512
ROPE = 64
VD = 128
TOP = 8
FFW = 12288
HE = 1024
REQ_DEV = 4
SLOTS = 512
EXPERTS = 32
TOK_EP = 16
TOKENS = 512
CAP = 6
N_EP = 32
N_TP = 4


def shared_cache(key):
    base = jax.random.normal(key, (TOKENS, SLOTS, LAT + ROPE), jnp.float32)
    return jnp.clip(base, -5.0, 5.0)


def draw_kv_cache(key, part):
    base = shared_cache(key)
    return base.astype(jnp.bfloat16)


def draw_queries(key, part):
    key = jax.random.fold_in(key, 5)
    values = jnp.clip(jax.random.normal(key, (TOKENS, H, LAT + ROPE), jnp.float32), -5.0, 5.0)
    return values.astype(jnp.bfloat16)


def draw_lengths(key, part):
    key = jax.random.fold_in(key, 11)
    drawn = jax.random.randint(key, (TOKENS,), 2, SLOTS + 1)
    position = jnp.arange(TOKENS, dtype=jnp.int32)
    return jnp.where(position % REQ_DEV == 0, SLOTS, drawn).astype(jnp.int32)


def column_scale(low, ratio):
    place = jnp.arange(D, dtype=jnp.float32) / (D - 1)
    return low * ratio ** place


def draw_residual(key, part):
    key = jax.random.fold_in(key, 13)
    values = jnp.clip(jax.random.normal(key, (TOKENS, D), jnp.float32), -3.0, 3.0)
    scale = column_scale(0.25, 8.0)
    return (values * scale[None, :]).astype(jnp.bfloat16)


def shard_levels(stream_key, shape, pieces, low, largest):
    def one(dim, parts):
        steps = jax.random.uniform(jax.random.fold_in(jax.random.fold_in(stream_key, 6), dim), (parts,), jnp.float32, low / len(pieces), largest / len(pieces))
        return jnp.repeat(jnp.exp(steps), shape[dim] // parts).reshape((-1,) + (1,) * (len(shape) - dim - 1))

    level = one(*pieces[0])
    for cut in pieces[1:]:
        level = level * one(*cut)
    return level


def routed_block(stream_key, own, number, rows, amount, top, most, skew):
    order = jax.random.permutation(stream_key, amount)
    crowded, common = load_shares(amount, rows * top, most, skew, True), load_shares(amount, rows * top, most, skew, False)
    places = jnp.arange(amount)

    def named(sizes, rotation):
        used = int((sizes > 0).sum())
        fixed = max(1, used // 4)
        moved = fixed + (places - fixed + rotation * (used - fixed)) % max(1, amount - fixed)
        return jnp.zeros((amount,), jnp.int32).at[order[jnp.where(places < fixed, places, moved)]].set(jnp.asarray(sizes, jnp.int32))

    sizes = jnp.where(number % 4 == 0, named(crowded, number // 4), named(common, number - number // 4 - 1))
    mixed = jax.random.permutation(jax.random.fold_in(own, 3), amount)
    source_of, sink = mixed[0:amount // 2 * 2:2], mixed[1:amount // 2 * 2:2]
    slack = jnp.minimum(sizes[source_of] - 1, most - sizes[sink]) // 2
    slack = jnp.where((source_of == order[0]) | (sink == order[0]) | (sizes[sink] == 0), 0, jnp.maximum(slack, 0))
    moved = jax.random.randint(jax.random.fold_in(own, 4), (amount // 2,), 0, 1 << 20) % (slack + 1)
    sizes = sizes.at[source_of].add(-moved).at[sink].add(moved)
    items = jnp.searchsorted(jnp.cumsum(sizes), jnp.arange(rows * top), side="right").astype(jnp.int32)
    listing = items.reshape(top, rows).T
    listing = listing[jax.random.permutation(jax.random.fold_in(own, 1), rows)]
    rotation = jax.random.randint(jax.random.fold_in(own, 2), (rows, 1), 0, top)
    return jnp.take_along_axis(listing, (jnp.arange(top)[None, :] + rotation) % top, axis=1)


def load_shares(number_of, total, most, skew, full):
    portions = [(1 << 20) // math.isqrt(grade ** skew) + 1 for grade in range(1, number_of + 1)]
    largest = most if full else min(most, max(-(-total // number_of), total * portions[0] // sum(portions)))
    least = 1 if total - largest >= number_of - 1 else 0
    given, spare = [largest] + [least] * (number_of - 1), total - largest - least * (number_of - 1)
    while spare > 0:
        movable = [i for i in range(1, number_of) if given[i] < largest] or [i for i in range(1, number_of) if given[i] < most]
        mass, budget = sum([portions[i] for i in movable]), spare
        for i in movable:
            more = min(most - given[i], max(1, budget * portions[i] // mass), spare)
            given[i] = given[i] + more
            spare = spare - more
    return np.array(given)


def centred(key, shape, width, bound, cuts=(), kind=jnp.bfloat16):
    factor_of = shard_levels(key, shape, cuts, -0.22, 0.18) if cuts else 1.0
    values = jax.random.normal(key, shape, jnp.float32) * width * factor_of
    return jnp.minimum(jnp.maximum(values, -bound), bound).astype(kind)


def setup_inputs(seed: int = 0) -> dict:
    seeds = jax.random.split(jax.random.key(seed), 18)
    queries = draw_queries(jax.random.fold_in(seeds[17], 71), 0)
    kv_cache = draw_kv_cache(jax.random.fold_in(seeds[17], 71), 0)
    new_latent = centred(seeds[2], (TOKENS, LAT + ROPE), 1.0, 5.0, ((0, 128),))
    lengths = draw_lengths(jax.random.fold_in(seeds[17], 71), 0)
    residual = draw_residual(jax.random.fold_in(seeds[17], 71), 0)
    gain_first = jnp.clip(1.0 + 0.18 * jax.random.normal(seeds[5], (D,), jnp.float32), 0.099609375, 1.8984375).astype(jnp.bfloat16)
    gain_second = jnp.clip(1.0 + 0.18 * jax.random.normal(seeds[6], (D,), jnp.float32), 0.099609375, 1.8984375).astype(jnp.bfloat16)
    value_proj = centred(seeds[7], (H, LAT, VD), LAT ** -0.5, 0.25, ((0, 32),))
    out_proj = centred(seeds[8], (H * VD, D), (H * VD) ** -0.5, 0.046875, ((0, 32), (1, 4)))
    dense_gate = centred(seeds[9], (D, FFW), D ** -0.5, 0.0625, ((0, 4), (1, 32)))
    dense_up = centred(seeds[10], (D, FFW), D ** -0.5, 0.0625, ((0, 4), (1, 32)))
    dense_down = centred(seeds[11], (FFW, D), FFW ** -0.5, 0.0546875, ((0, 32), (1, 4)))
    route_ids_keys = jax.random.split(jax.random.fold_in(seeds[12], 1), TOKENS // TOK_EP)
    route_ids_turns = jax.random.permutation(jax.random.fold_in(seeds[12], 3), TOKENS // TOK_EP)
    route_ids = jax.vmap(lambda own, number: routed_block(jax.random.fold_in(seeds[12], 2), own, number, TOK_EP, EXPERTS, TOP, CAP, 2))(route_ids_keys, route_ids_turns).reshape((TOKENS, TOP))
    route_gates = jnp.clip(0.1 + 0.5 * jax.random.uniform(seeds[13], (TOKENS, TOP), jnp.float32) ** shard_levels(seeds[13], (TOKENS, TOP), ((0, 32),), -0.2, 0.2), 0.1, 0.6)
    expert_gate = centred(seeds[14], (EXPERTS, D, HE), D ** -0.5, 0.0625, ((0, 32), (2, 4)))
    expert_up = centred(seeds[15], (EXPERTS, D, HE), D ** -0.5, 0.0625, ((0, 32), (2, 4)))
    expert_down = centred(seeds[16], (EXPERTS, HE, D), HE ** -0.5, 0.1875, ((0, 32), (1, 4)))
    return dict(queries=queries, kv_cache=kv_cache, new_latent=new_latent, lengths=lengths, residual=residual, gain_first=gain_first, gain_second=gain_second, value_proj=value_proj, out_proj=out_proj, dense_gate=dense_gate, dense_up=dense_up, dense_down=dense_down, route_ids=route_ids, route_gates=route_gates, expert_gate=expert_gate, expert_up=expert_up, expert_down=expert_down)


EPS = 1e-06

def rms_norm(values, gain):
    mean_sq = lax.optimization_barrier(jnp.mean(values * values, axis=-1, keepdims=True))
    return (values * lax.rsqrt(mean_sq + EPS) * gain.astype(jnp.float32)).astype(jnp.bfloat16)

def attend(operands):
    query_blk, cache_blk, fresh_blk, length_blk = operands
    score_scale = (VD + ROPE) ** (-0.5)
    query_f32 = query_blk.astype(jnp.float32)
    cache_f32 = cache_blk.astype(jnp.float32)
    fresh_f32 = fresh_blk.astype(jnp.float32)
    scores = jnp.einsum('rhc,rjc->rhj', query_f32, cache_f32) * score_scale
    self_score = jnp.einsum('rhc,rc->rh', query_f32, fresh_f32) * score_scale
    live_mask = jnp.arange(SLOTS, dtype=jnp.int32)[None, :] < length_blk[:, None]
    scores = jnp.where(live_mask[:, None, :], scores, -jnp.inf)
    top_score = jnp.maximum(lax.optimization_barrier(jnp.max(scores, axis=-1)), self_score)
    expo = jnp.exp(scores - top_score[..., None])
    self_expo = jnp.exp(self_score - top_score)
    total = lax.optimization_barrier(jnp.sum(expo, axis=-1)) + self_expo
    weights = (expo / total[..., None]).astype(jnp.bfloat16)
    self_weight = (self_expo / total).astype(jnp.bfloat16)
    latent = jnp.einsum('rhj,rjc->rhc', weights.astype(jnp.float32), cache_f32[:, :, :LAT])
    latent = latent + self_weight.astype(jnp.float32)[..., None] * fresh_f32[:, None, :LAT]
    return latent.astype(jnp.bfloat16)

def expert_apply(operands):
    rows, w_gate, w_up, w_down = operands
    gate_act = jnp.dot(rows, w_gate, preferred_element_type=jnp.float32)
    up_act = jnp.dot(rows, w_up, preferred_element_type=jnp.float32)
    hidden = (jax.nn.silu(gate_act) * up_act).astype(jnp.bfloat16)
    return jnp.dot(hidden, w_down, preferred_element_type=jnp.float32).astype(jnp.bfloat16)

def reference(queries, kv_cache, new_latent, lengths, residual, gain_first, gain_second, value_proj, out_proj, dense_gate, dense_up, dense_down, route_ids, route_gates, expert_gate, expert_up, expert_down):
    groups = N_EP * N_TP
    per_group = TOKENS // groups
    latent = lax.map(attend, (queries.reshape(groups, per_group, H, LAT + ROPE), kv_cache.reshape(groups, per_group, SLOTS, LAT + ROPE), new_latent.reshape(groups, per_group, LAT + ROPE), lengths.reshape(groups, per_group)))
    latent = latent.reshape(TOKENS, H, LAT)
    head_values = jnp.einsum('rhc,hcv->rhv', latent.astype(jnp.float32), value_proj.astype(jnp.float32)).astype(jnp.bfloat16)
    attn_out = jnp.dot(head_values.reshape(TOKENS, H * VD), out_proj, preferred_element_type=jnp.float32)
    first = residual.astype(jnp.float32) + attn_out
    normed = rms_norm(first, gain_first)
    gate_act = jnp.dot(normed, dense_gate, preferred_element_type=jnp.float32)
    up_act = jnp.dot(normed, dense_up, preferred_element_type=jnp.float32)
    dense_hidden = (jax.nn.silu(gate_act) * up_act).astype(jnp.bfloat16)
    second = first + jnp.dot(dense_hidden, dense_down, preferred_element_type=jnp.float32)
    normed_b = rms_norm(second, gain_second)
    picks = TOK_EP * TOP
    group_ids = route_ids.reshape(N_EP, picks)
    onehot = (group_ids[..., None] == jnp.arange(EXPERTS, dtype=jnp.int32)).astype(jnp.int32)
    before = jnp.cumsum(onehot, axis=1) - onehot
    slot = lax.optimization_barrier(jnp.sum(before * onehot, axis=-1))
    group_index = jnp.arange(N_EP, dtype=jnp.int32)[:, None]
    row_pos = (group_index * CAP + slot).astype(jnp.int32).reshape(-1)
    token_index = (group_index * TOK_EP + jnp.arange(picks, dtype=jnp.int32)[None, :] // TOP).reshape(-1)
    flat_ids = group_ids.reshape(-1)
    buffers = jnp.zeros((EXPERTS, N_EP * CAP, D), jnp.bfloat16).at[flat_ids, row_pos].set(normed_b[token_index])
    outputs = lax.map(expert_apply, (buffers, expert_gate, expert_up, expert_down))
    picked = outputs[flat_ids, row_pos].astype(jnp.float32).reshape(TOKENS, TOP, D)
    moe_out = lax.optimization_barrier(jnp.sum(route_gates[..., None] * picked, axis=1))
    return (second + moe_out).astype(jnp.bfloat16)
```

```python
import jax
import jax.numpy as jnp
from jax import lax
from jax.sharding import Mesh, PartitionSpec as P

D = 7168
ROPE = 64
VD = 128
EPS = 1e-06
YX = ("y", "x")
NZ = 4
BF = jnp.bfloat16
F32 = jnp.float32


def zsend(values, shift):
    return lax.ppermute(values, "z", [(i, (i + shift) % NZ) for i in range(NZ)])


def swap_core(values):
    return lax.ppermute(values, "c", [(0, 1), (1, 0)])


def zgather(values):
    return [values] + [zsend(values, NZ - k) for k in (1, 2, 3)]


def zscatter(blocks, z):
    take = lambda q: lax.dynamic_index_in_dim(blocks, q, 0, keepdims=False)
    got = [zsend(take(lax.rem(z + k, NZ)), k) for k in (1, 2, 3)]
    total = take(z).astype(F32)
    for piece in got:
        total = total + piece.astype(F32)
    return total


def plane_scatter(rows_own, rows_other, weight):
    dot = lambda a: jnp.dot(a, weight, preferred_element_type=F32)
    arrived = swap_core(dot(rows_other).astype(BF))
    mine = (dot(rows_own) + arrived.astype(F32)).astype(BF)
    parts = lax.all_to_all(mine.reshape(16, 16, -1), YX, 0, 0, tiled=True)
    return jnp.sum(parts.astype(F32), axis=0)


def attend(queries, kv_cache, new_latent, lengths, latent_dim):
    score_scale = (VD + ROPE) ** (-0.5)
    slot_count = kv_cache.shape[1]
    scores = jnp.einsum("rhc,rjc->rhj", queries, kv_cache, preferred_element_type=F32) * score_scale
    self_score = jnp.einsum("rhc,rc->rh", queries, new_latent, preferred_element_type=F32) * score_scale
    live_mask = lax.broadcasted_iota(jnp.int32, (1, slot_count), 1) < lengths[:, None]
    scores = jnp.where(live_mask[:, None, :], scores, -jnp.inf)
    top_score = jnp.maximum(jnp.max(scores, axis=-1), self_score)
    expo = jnp.exp(scores - top_score[..., None])
    self_expo = jnp.exp(self_score - top_score)
    total = jnp.sum(expo, axis=-1) + self_expo
    weights = (expo / total[..., None]).astype(BF)
    self_weight = (self_expo / total).astype(BF)
    latent = jnp.einsum("rhj,rjc->rhc", weights, kv_cache[:, :, :latent_dim], preferred_element_type=F32)
    latent = latent + self_weight.astype(F32)[..., None] * new_latent[:, None, :latent_dim].astype(F32)
    return latent.astype(BF)


def sum_columns(total):
    hi = lax.reduce_precision(total, 8, 7)
    lane = lax.broadcasted_iota(jnp.int32, (1, 128), 1)
    return jnp.where(lane == 0, hi[:, None], jnp.where(lane == 1, (total - hi)[:, None], 0.0))


def shards(
    queries, kv_cache, new_latent, lengths, residual, gain_first, gain_second, value_proj, out_proj,
    dense_gate, dense_up, dense_down, route_ids, route_gates, expert_gate, expert_up, expert_down,
):
    z = lax.axis_index("z")
    c = lax.axis_index("c")
    latent_dim = value_proj.shape[1]
    quarter = residual.shape[1]

    pick = lambda w, k, axis: lax.dynamic_slice_in_dim(w, lax.rem(z + k, NZ) * quarter, quarter, axis)
    gate_parts = [pick(expert_gate[0], 0, 0)] + [zsend(pick(expert_gate[0], NZ - k, 0), NZ - k) for k in (1, 2, 3)]
    up_parts = [pick(expert_up[0], 0, 0)] + [zsend(pick(expert_up[0], NZ - k, 0), NZ - k) for k in (1, 2, 3)]
    down_parts = [pick(expert_down[0], 0, 1)] + [zsend(pick(expert_down[0], NZ - k, 1), NZ - k) for k in (1, 2, 3)]

    latent = attend(queries, kv_cache, new_latent, lengths, latent_dim)
    latent = latent.reshape(4, 16, 2, 4, latent_dim)
    mine = lax.dynamic_index_in_dim(latent, c, 2, keepdims=False)
    theirs = lax.dynamic_index_in_dim(latent, 1 - c, 2, keepdims=False)
    theirs = swap_core(theirs)
    both = jnp.stack([mine, theirs], axis=0)
    both = both.transpose(2, 3, 0, 1, 4).reshape(16, 32, latent_dim)
    moved = lax.all_to_all(both, YX, 0, 0, tiled=True).reshape(16, 4, 8, latent_dim)
    head_vals = jnp.einsum("nhpc,hcv->nphv", moved, value_proj, preferred_element_type=F32).astype(BF)
    head_vals = head_vals.reshape(128, -1)
    rows = jnp.stack(zgather(head_vals), axis=0).reshape(NZ, 16, 2, 4, -1)
    rows = rows.transpose(2, 1, 0, 3, 4).reshape(2, 256, -1)
    attn_out = plane_scatter(rows[0], rows[1], out_proj)
    attn_out = jnp.roll(attn_out, z * 4, axis=0)
    first = residual.astype(F32) + attn_out

    def spread(values):
        wide = jnp.broadcast_to(values[None], (16,) + values.shape)
        own = lax.all_to_all(wide, YX, 0, 0, tiled=True).reshape(256, -1)
        return own, swap_core(own)

    own, other = spread(first.astype(BF))
    gain_a = gain_first.astype(F32)

    def gate_up(piece):
        value = piece.astype(F32)
        normed = (value * gain_a).astype(BF)
        return jnp.concatenate(
            [
                jnp.dot(normed, dense_gate, preferred_element_type=F32),
                jnp.dot(normed, dense_up, preferred_element_type=F32),
                sum_columns(jnp.sum(value * value, axis=1)),
            ],
            axis=1,
        ).astype(BF)

    width = dense_gate.shape[1]
    partial = jnp.stack([gate_up(own).reshape(NZ, 64, -1), gate_up(other).reshape(NZ, 64, -1)], axis=1)
    summed = zscatter(partial.reshape(NZ, 128, -1), z)
    scale = lax.rsqrt((summed[:, 2 * width] + summed[:, 2 * width + 1]) / D + EPS)[:, None]
    gate_act = summed[:, :width] * scale
    hidden = (jax.nn.silu(gate_act) * (summed[:, width : 2 * width] * scale)).astype(BF)
    hidden = jnp.stack(zgather(hidden), axis=0)
    hidden = jnp.roll(hidden, z, axis=0).reshape(NZ, 2, 64, -1)
    second = first + plane_scatter(hidden[:, 0].reshape(256, -1), hidden[:, 1].reshape(256, -1), dense_down)

    tok_group, top_count = route_ids.shape
    group_count, slots, cap = 32, 8, 6
    flat_ids = route_ids.reshape(-1)
    onehot = (flat_ids[:, None] == lax.broadcasted_iota(jnp.int32, (1, group_count), 1)).astype(jnp.int32)
    before = jnp.cumsum(onehot, axis=0) - onehot
    slot = jnp.sum(before * onehot, axis=1)
    position = (flat_ids * slots + slot).reshape(tok_group, top_count)
    columns = lax.broadcasted_iota(jnp.int32, (1, 1, group_count * slots), 2)
    matches = position[:, :, None] == columns
    pick_matrix = jnp.sum(matches.astype(jnp.int32), axis=1).astype(BF)
    combine_matrix = jnp.sum(jnp.where(matches, route_gates[:, :, None], 0.0), axis=1)
    sendbuf = jnp.einsum("tp,td->pd", pick_matrix, second.astype(BF), preferred_element_type=F32).astype(BF)
    arrived = lax.all_to_all(sendbuf.reshape(group_count, slots, -1), ("y", "x", "c"), 0, 0, tiled=True)
    arrived = arrived[:, :cap].reshape(group_count * cap, -1)
    value = arrived.astype(F32)
    normed = (value * gain_second.astype(F32)).astype(BF)
    he = expert_gate.shape[2]

    def unroll(parts):
        return jnp.roll(jnp.stack(parts, axis=0), z, axis=0).transpose(1, 0, 2).reshape(parts[0].shape[0], -1)

    gate_partial = unroll([jnp.dot(normed, w, preferred_element_type=F32).astype(BF) for w in gate_parts])
    up_partial = unroll([jnp.dot(normed, w, preferred_element_type=F32).astype(BF) for w in up_parts])
    partial = jnp.concatenate([gate_partial, up_partial, sum_columns(jnp.sum(value * value, axis=1)).astype(BF)], axis=1)
    summed = zscatter(partial.reshape(NZ, group_count * cap // NZ, -1), z)
    hw = he * NZ
    scale = lax.rsqrt((summed[:, 2 * hw] + summed[:, 2 * hw + 1]) / D + EPS)[:, None]
    expert_hidden = (jax.nn.silu(summed[:, :hw] * scale) * (summed[:, hw : 2 * hw] * scale)).astype(BF)
    expert_hidden = jnp.roll(jnp.stack(zgather(expert_hidden), axis=0), z, axis=0).reshape(group_count * cap, NZ, he)
    expert_hidden = jnp.roll(expert_hidden, -z, axis=1)
    result = sum(jnp.dot(expert_hidden[:, k], down_parts[k], preferred_element_type=F32) for k in range(NZ))
    result = jnp.pad(result.astype(BF).reshape(group_count, cap, -1), ((0, 0), (0, slots - cap), (0, 0)))
    returned = lax.all_to_all(result, ("y", "x", "c"), 0, 0, tiled=True).reshape(group_count * slots, -1)
    moe_out = jnp.dot(combine_matrix, returned.astype(F32), precision=lax.Precision.HIGHEST)
    return (second + moe_out).astype(BF)


def solution(mesh):
    grid = Mesh(mesh.devices.reshape(4, 4, 2, 4), ("y", "x", "c", "z"))
    ep = ("y", "x", "c")
    both = ("y", "x", "c", "z")
    return jax.shard_map(
        shards,
        mesh=grid,
        in_specs=(
            P(both, None, None),
            P(both, None, None),
            P(both, None),
            P(both),
            P(ep, "z"),
            P("z"),
            P("z"),
            P(ep, None, None),
            P(ep, "z"),
            P("z", ep),
            P("z", ep),
            P(ep, "z"),
            P(ep, None),
            P(ep, None),
            P(ep, None, "z"),
            P(ep, None, "z"),
            P(ep, "z", None),
        ),
        out_specs=P(ep, "z"),
        check_vma=False,
    )
```

```python
import jax
import jax.numpy as jnp
from jax import lax
from jax.experimental import pallas as pl
from jax.experimental.pallas import tpu as pltpu
from jax.sharding import Mesh, PartitionSpec as P

D = 7168
ROPE = 64
VD = 128
EPS = 1e-06
YX = ("y", "x")
NZ = 4
BF = jnp.bfloat16
F32 = jnp.float32


def zsend(values, shift):
    return lax.ppermute(values, "z", [(i, (i + shift) % NZ) for i in range(NZ)])


def swap_core(values):
    return lax.ppermute(values, "c", [(0, 1), (1, 0)])


def zgather(values):
    return [values] + [zsend(values, NZ - k) for k in (1, 2, 3)]


def zscatter(blocks):
    got = [zsend(blocks[k], k) for k in (1, 2, 3)]
    total = blocks[0].astype(F32)
    for piece in got:
        total = total + piece.astype(F32)
    return total


def plane_scatter(kernel, z, blocks, weight):
    arrived = swap_core(plane_dot(kernel, z, blocks, weight, 1, BF))
    mine = (plane_dot(kernel, z, blocks, weight, 0, F32) + arrived.astype(F32)).astype(BF)
    parts = lax.all_to_all(mine.reshape(16, 16, -1), YX, 0, 0, tiled=True)
    return jnp.sum(parts.astype(F32), axis=0)


def attend(queries, kv_cache, new_latent, lengths, latent_dim):
    score_scale = (VD + ROPE) ** (-0.5)
    slot_count = kv_cache.shape[1]
    scores = jnp.einsum("rhc,rjc->rhj", queries, kv_cache, preferred_element_type=F32) * score_scale
    self_score = jnp.einsum("rhc,rc->rh", queries, new_latent, preferred_element_type=F32) * score_scale
    live_mask = lax.broadcasted_iota(jnp.int32, (1, slot_count), 1) < lengths[:, None]
    scores = jnp.where(live_mask[:, None, :], scores, -jnp.inf)
    top_score = jnp.maximum(jnp.max(scores, axis=-1), self_score)
    expo = jnp.exp(scores - top_score[..., None])
    self_expo = jnp.exp(self_score - top_score)
    total = jnp.sum(expo, axis=-1) + self_expo
    weights = (expo / total[..., None]).astype(BF)
    self_weight = (self_expo / total).astype(BF)
    latent = jnp.einsum("rhj,rjc->rhc", weights, kv_cache[:, :, :latent_dim], preferred_element_type=F32)
    latent = latent + self_weight.astype(F32)[..., None] * new_latent[:, None, :latent_dim].astype(F32)
    return latent.astype(BF)


def params():
    return pltpu.CompilerParams(dimension_semantics=("arbitrary",), vmem_limit_bytes=40 * 1024 * 1024)


def tail_of(squares):
    total = jnp.sum(squares, axis=1, keepdims=True)
    hi = total.astype(BF).astype(F32)
    lane = lax.broadcasted_iota(jnp.int32, (total.shape[0], 128), 1)
    return jnp.where(lane == 0, hi, jnp.where(lane == 1, total - hi, 0.0)).astype(BF)


def dense_in_kernel(z_ref, own, other, gain, gate, up, o0, o1, o2, o3, acc, squares, tail):
    step = pl.program_id(0)
    width = gate.shape[1]

    @pl.when(step == 0)
    def _():
        acc[...] = jnp.zeros_like(acc)
        squares[...] = jnp.zeros_like(squares)

    scale = gain[...].astype(F32)
    for rel, ref in enumerate((own, other)):
        value = ref[...].astype(F32)
        normed = (value * scale).astype(BF)
        acc[rel, :, :width] += jnp.dot(normed, gate[...], preferred_element_type=F32)
        acc[rel, :, width:] += jnp.dot(normed, up[...], preferred_element_type=F32)
        square = value * value
        squares[rel] += square[:, :128] + square[:, 128:]

    @pl.when(step == pl.num_programs(0) - 1)
    def _():
        z = z_ref[0]
        for rel in range(2):
            tail[rel] = tail_of(squares[rel])
        for k, out in enumerate((o0, o1, o2, o3)):
            at = pl.multiple_of(lax.rem(z + k, NZ) * 64, 64)
            for rel in range(2):
                rows = pl.ds(rel * 64, 64)
                out[rows, : 2 * width] = acc[rel, pl.ds(at, 64), :].astype(BF)
                out[rows, 2 * width :] = tail[rel, pl.ds(at, 64), :]


def dense_in(z, own, other, gain, gate, up):
    depth, width = gate.shape
    step = 256
    rows = own.shape[0]
    lhs = pl.BlockSpec((rows, step), lambda i, z: (0, i))
    weight = pl.BlockSpec((step, width), lambda i, z: (i, 0))
    lanes = 2 * width + 128
    return pl.pallas_call(
        dense_in_kernel,
        grid_spec=pltpu.PrefetchScalarGridSpec(
            num_scalar_prefetch=1,
            grid=(depth // step,),
            in_specs=[lhs, lhs, pl.BlockSpec((1, step), lambda i, z: (0, i)), weight, weight],
            out_specs=[pl.BlockSpec((rows // 2, lanes), lambda i, z: (0, 0))] * NZ,
            scratch_shapes=[
                pltpu.VMEM((2, rows, 2 * width), F32),
                pltpu.VMEM((2, rows, 128), F32),
                pltpu.VMEM((2, rows, 128), BF),
            ],
        ),
        out_shape=[jax.ShapeDtypeStruct((rows // 2, lanes), BF)] * NZ,
        compiler_params=params(),
        cost_estimate=pl.CostEstimate(flops=8 * rows * depth * width, bytes_accessed=4 * depth * (rows + width), transcendentals=0),
        name="dense_in",
    )(z, own, other, gain.reshape(1, -1), gate, up)


def silu(value):
    return value / (1.0 + jnp.exp(-value))


def expert_in_kernel(z_ref, x0, x1, x2, *refs):
    gates, ups, out, (gate_acc, up_acc) = refs[:4], refs[4:8], refs[8], refs[9:]
    step = pl.program_id(0)

    @pl.when(step == 0)
    def _():
        gate_acc[...] = jnp.zeros_like(gate_acc)
        up_acc[...] = jnp.zeros_like(up_acc)

    rows, wide = out.shape[0], x0.shape[0]
    row = lax.broadcasted_iota(jnp.int32, (rows, wide), 0)
    col = lax.broadcasted_iota(jnp.int32, (rows, wide), 1)
    block, place = (col >> 3) * 6, col & 7
    onehot = lambda hit: jnp.where(hit, 1.0, 0.0).astype(BF)
    keep = onehot((place < 6) & (row == block + place))
    rest = None
    quarters = []
    for m, ref in enumerate((x0, x1, x2)):
        x = ref[...]
        quarters.append(jnp.dot(keep, x, preferred_element_type=F32).astype(BF))
        pick = onehot((place >= 6) & (row == block + 3 * (place - 6) + m))
        term = jnp.dot(pick, x, preferred_element_type=F32)
        rest = term if rest is None else rest + term
    quarters.append(rest.astype(BF))
    for m in range(NZ):
        gate_acc[...] += jnp.dot(quarters[m], gates[m][...], preferred_element_type=F32)
        up_acc[...] += jnp.dot(quarters[m], ups[m][...], preferred_element_type=F32)

    @pl.when(step == pl.num_programs(0) - 1)
    def _():
        out[...] = (silu(gate_acc[...]) * up_acc[...]).astype(BF)


def expert_in(z, x, gate, up, rows):
    depth, width = gate.shape
    step = 256
    steps = depth // NZ // step
    xs = [pl.BlockSpec((x.shape[0], step), lambda i, z, m=m: (0, m * steps + i)) for m in range(3)]
    ws = [pl.BlockSpec((step, width), lambda i, z, m=m: (lax.rem(z[0] + m, NZ) * steps + i, 0)) for m in range(NZ)]
    return pl.pallas_call(
        expert_in_kernel,
        grid_spec=pltpu.PrefetchScalarGridSpec(
            num_scalar_prefetch=1,
            grid=(steps,),
            in_specs=xs + ws + ws,
            out_specs=pl.BlockSpec((rows, width), lambda i, z: (0, 0)),
            scratch_shapes=[pltpu.VMEM((rows, width), F32)] * 2,
        ),
        out_shape=jax.ShapeDtypeStruct((rows, width), BF),
        compiler_params=params(),
        cost_estimate=pl.CostEstimate(flops=4 * rows * depth * width, bytes_accessed=4 * depth * width, transcendentals=0),
        name="expert_in",
    )(z, x, x, x, *[gate] * 4, *[up] * 4)


def expert_out_kernel(z_ref, *refs):
    hidden, weights, out, wide = refs[:4], refs[4:8], refs[8], refs[9]

    @pl.when(pl.program_id(0) == 0)
    def _():
        shape = (wide.shape[1], hidden[0].shape[0])
        row = lax.broadcasted_iota(jnp.int32, shape, 0)
        col = lax.broadcasted_iota(jnp.int32, shape, 1)
        keep = ((row & 7) < 6) & (col == (row >> 3) * 6 + (row & 7))
        keep = jnp.where(keep, 1.0, 0.0).astype(BF)
        for k in range(NZ):
            wide[k] = jnp.dot(keep, hidden[k][...], preferred_element_type=F32).astype(BF)

    total = None
    for k in range(NZ):
        term = jnp.dot(wide[k], weights[k][...], preferred_element_type=F32)
        total = term if total is None else total + term
    out[...] = total.astype(BF)


def expert_out(z, hidden, down, got, wide):
    rows, width = hidden[0].shape
    columns = got[0].shape[1]
    step = 256
    steps = columns // step
    return pl.pallas_call(
        expert_out_kernel,
        grid_spec=pltpu.PrefetchScalarGridSpec(
            num_scalar_prefetch=1,
            grid=(steps,),
            in_specs=[pl.BlockSpec((rows, width), lambda i, z: (0, 0))] * NZ
            + [pl.BlockSpec((width, step), lambda i, z: (0, z[0] * steps + i))]
            + [pl.BlockSpec((width, step), lambda i, z: (0, i))] * 3,
            out_specs=pl.BlockSpec((wide, step), lambda i, z: (0, i)),
            scratch_shapes=[pltpu.VMEM((NZ, wide, width), BF)],
        ),
        out_shape=jax.ShapeDtypeStruct((wide, columns), BF),
        compiler_params=params(),
        cost_estimate=pl.CostEstimate(flops=8 * wide * width * columns, bytes_accessed=8 * width * columns, transcendentals=0),
        name="expert_out",
    )(z, *hidden, down, *got)


def dense_out_kernel(z_ref, h0, h1, h2, h3, weight, out, held, *, rel):
    @pl.when(pl.program_id(0) == 0)
    def _():
        z = z_ref[0]
        for k, ref in enumerate((h0, h1, h2, h3)):
            at = pl.multiple_of(lax.rem(z + k, NZ) * 64, 64)
            held[pl.ds(at, 64), :] = ref[...]

    out[...] = jnp.dot(held[...], weight[...], preferred_element_type=F32).astype(out.dtype)


def out_proj_kernel(z_ref, h0, h1, h2, h3, weight, out, held, *, rel):
    @pl.when(pl.program_id(0) == 0)
    def _():
        z = z_ref[0]
        rows, cols = held.shape[0], h0.shape[0]
        row = lax.broadcasted_iota(jnp.int32, (rows, cols), 0)
        col = lax.broadcasted_iota(jnp.int32, (rows, cols), 1)
        match = col == (row >> 4) * 8 + rel * 4 + (row & 3)
        total = None
        for k, ref in enumerate((h0, h1, h2, h3)):
            hit = match & (((row >> 2) & 3) == lax.rem(z + k, NZ))
            term = jnp.dot(jnp.where(hit, 1.0, 0.0).astype(BF), ref[...], preferred_element_type=F32)
            total = term if total is None else total + term
        held[...] = total.astype(BF)

    out[...] = jnp.dot(held[...], weight[...], preferred_element_type=F32).astype(out.dtype)


def plane_dot(kernel, z, blocks, weight, rel, dtype):
    depth, columns = weight.shape
    step = 256
    block_rows, at = (64, rel) if kernel is dense_out_kernel else (128, 0)
    return pl.pallas_call(
        lambda *refs: kernel(*refs, rel=rel),
        grid_spec=pltpu.PrefetchScalarGridSpec(
            num_scalar_prefetch=1,
            grid=(columns // step,),
            in_specs=[pl.BlockSpec((block_rows, depth), lambda i, z: (at, 0))] * NZ
            + [pl.BlockSpec((depth, step), lambda i, z: (0, i))],
            out_specs=pl.BlockSpec((256, step), lambda i, z: (0, i)),
            scratch_shapes=[pltpu.VMEM((256, depth), BF)],
        ),
        out_shape=jax.ShapeDtypeStruct((256, columns), dtype),
        compiler_params=params(),
        cost_estimate=pl.CostEstimate(flops=512 * depth * columns, bytes_accessed=2 * depth * columns, transcendentals=0),
        name=("dense_out" if kernel is dense_out_kernel else "out_proj") + ("_other" if rel else "_own"),
    )(z, *blocks, weight)


def shards(
    queries, kv_cache, new_latent, lengths, residual, gain_first, gain_second, value_proj, out_proj,
    dense_gate, dense_up, dense_down, route_ids, route_gates, expert_gate, expert_up, expert_down,
):
    z = lax.axis_index("z")
    c = lax.axis_index("c")
    latent_dim = value_proj.shape[1]
    quarter = residual.shape[1]

    zs = z.astype(jnp.int32).reshape(1)

    def pick(w, k, axis):
        return lax.dynamic_slice_in_dim(w, lax.rem(z + k, NZ) * quarter, quarter, axis)

    def cut(w, axis, which):
        return {k: pick(w, NZ - k, axis) for k in which}

    def tied(value, *groups):
        flat = [group[k] for group in groups for k in group]
        value, *flat = lax.optimization_barrier((value, *flat))
        at = iter(flat)
        return (value, *[{k: next(at) for k in group} for group in groups])

    def fetch(group):
        return {k: zsend(group[k], NZ - k) for k in group}

    down_a = fetch(cut(expert_down[0], 1, (1, 3)))
    down_cut = cut(expert_down[0], 1, (2,))
    gains = zgather(gain_second.reshape(1, -1))

    latent = attend(queries, kv_cache, new_latent, lengths, latent_dim)
    latent = latent.reshape(4, 16, 2, 4, latent_dim)
    mine = lax.dynamic_index_in_dim(latent, c, 2, keepdims=False)
    theirs = lax.dynamic_index_in_dim(latent, 1 - c, 2, keepdims=False)
    theirs = swap_core(theirs)
    both = jnp.stack([mine, theirs], axis=0)
    both = both.transpose(2, 3, 0, 1, 4).reshape(16, 32, latent_dim)
    moved = lax.all_to_all(both, YX, 0, 0, tiled=True).reshape(16, 4, 8, latent_dim)
    moved, down_a, down_cut = tied(moved, down_a, down_cut)
    head_vals = jnp.einsum("nhpc,hcv->nphv", moved, value_proj, preferred_element_type=F32).astype(BF)
    head_vals = head_vals.reshape(128, -1)
    rows = zgather(head_vals)
    rows, down_cut = tied(rows, down_cut)
    down_b = fetch(down_cut)
    attn_out = plane_scatter(out_proj_kernel, zs, rows, out_proj)
    attn_out, down_b = tied(attn_out, down_b)
    first = residual.astype(F32) + attn_out

    def spread(values):
        wide = jnp.broadcast_to(values[None], (16,) + values.shape)
        own = lax.all_to_all(wide, YX, 0, 0, tiled=True).reshape(256, -1)
        return own, swap_core(own)

    own, other = spread(first.astype(BF))
    width = dense_gate.shape[1]
    own, other = lax.optimization_barrier((own, other))
    blocks = dense_in(zs, own, other, gain_first, dense_gate, dense_up)
    summed = zscatter(blocks)
    scale = lax.rsqrt((summed[:, 2 * width] + summed[:, 2 * width + 1]) / D + EPS)[:, None]
    gate_act = summed[:, :width] * scale
    hidden = (jax.nn.silu(gate_act) * (summed[:, width : 2 * width] * scale)).astype(BF)
    second = first + plane_scatter(dense_out_kernel, zs, zgather(hidden), dense_down)

    tok_group, top_count = route_ids.shape
    group_count, slots, cap = 32, 8, 6
    flat_ids = route_ids.reshape(-1)
    onehot = (flat_ids[:, None] == lax.broadcasted_iota(jnp.int32, (1, group_count), 1)).astype(jnp.int32)
    before = jnp.cumsum(onehot, axis=0) - onehot
    slot = jnp.sum(before * onehot, axis=1)
    position = (flat_ids * slots + slot).reshape(tok_group, top_count)
    columns = lax.broadcasted_iota(jnp.int32, (1, 1, group_count * slots), 2)
    matches = position[:, :, None] == columns
    combine_matrix = jnp.sum(jnp.where(matches, route_gates[:, :, None], 0.0), axis=1)
    wide = zgather(second.astype(BF))
    total = sum(jnp.sum(jnp.square(q.astype(F32)), axis=1, keepdims=True) for q in wide)
    scale = lax.rsqrt(total / D + EPS)
    normed = [(q.astype(F32) * scale * g.astype(F32)).astype(BF) for q, g in zip(wide, gains)]
    column = lax.broadcasted_iota(jnp.int32, (group_count * slots, 1, 1), 0)
    block, place = column >> 3, column & 7
    ids = flat_ids.reshape(1, tok_group, top_count)
    at = slot.reshape(1, tok_group, top_count)
    hot = lambda want: jnp.sum(((ids == block) & (at == want)).astype(jnp.int32), axis=2).astype(BF)
    head = hot(jnp.where(place < cap, place, -1))
    sendbuf = []
    for m in range(3):
        tail = hot(jnp.where(place >= cap, 3 * (place - cap) + m, -1))
        both = jnp.concatenate([normed[m], normed[3]], axis=0)
        sendbuf.append(jnp.dot(jnp.concatenate([head, tail], axis=1), both, preferred_element_type=F32).astype(BF))
    sendbuf = jnp.concatenate(sendbuf, axis=1).reshape(group_count, slots, -1)
    arrived = lax.all_to_all(sendbuf, ("y", "x", "c"), 0, 0, tiled=True).reshape(group_count * slots, -1)
    expert_hidden = expert_in(zs, arrived, expert_gate[0], expert_up[0], group_count * cap)
    result = expert_out(zs, zgather(expert_hidden), expert_down[0], [down_a[1], down_b[2], down_a[3]], group_count * slots)
    result = result.reshape(group_count, slots, -1)
    returned = lax.all_to_all(result, ("y", "x", "c"), 0, 0, tiled=True).reshape(group_count * slots, -1)
    moe_out = jnp.dot(combine_matrix, returned.astype(F32), precision=lax.Precision.HIGHEST)
    return (second + moe_out).astype(BF)


def solution(mesh):
    grid = Mesh(mesh.devices.reshape(4, 4, 2, 4), ("y", "x", "c", "z"))
    ep = ("y", "x", "c")
    both = ("y", "x", "c", "z")
    return jax.shard_map(
        shards,
        mesh=grid,
        in_specs=(
            P(both, None, None),
            P(both, None, None),
            P(both, None),
            P(both),
            P(ep, "z"),
            P("z"),
            P("z"),
            P(ep, None, None),
            P(ep, "z"),
            P("z", ep),
            P("z", ep),
            P(ep, "z"),
            P(ep, None),
            P(ep, None),
            P(ep, None, "z"),
            P(ep, None, "z"),
            P(ep, "z", None),
        ),
        out_specs=P(ep, "z"),
        check_vma=False,
    )
```

```python
import jax
import jax.numpy as jnp
from jax import lax
from jax.experimental import pallas as pl
from jax.experimental.pallas import tpu as pltpu
from jax.sharding import Mesh, PartitionSpec as P

D = 7168
ROPE = 64
VD = 128
EPS = 1e-06
YX = ("y", "x")
NZ = 4
BF = jnp.bfloat16
F32 = jnp.float32


def zsend(values, shift):
    return lax.ppermute(values, "z", [(i, (i + shift) % NZ) for i in range(NZ)])


def swap_core(values):
    return lax.ppermute(values, "c", [(0, 1), (1, 0)])


def zgather(values):
    return [values] + [zsend(values, NZ - k) for k in (1, 2, 3)]


def zscatter(blocks):
    got = [zsend(blocks[k], k) for k in (1, 2, 3)]
    total = blocks[0].astype(F32)
    for piece in got:
        total = total + piece.astype(F32)
    return total


def plane_scatter(kernel, z, blocks, weight):
    arrived = swap_core(plane_dot(kernel, z, blocks, weight, 1))
    mine = plane_dot(kernel, z, blocks, weight, 0, arrived)
    return lax.all_to_all(mine.reshape(16, 16, -1), YX, 0, 0, tiled=True)


def onehot(hit):
    return jnp.where(hit, 1.0, 0.0).astype(BF)


def grid_of(shape):
    return lax.broadcasted_iota(jnp.int32, shape, 0), lax.broadcasted_iota(jnp.int32, shape, 1)


def exact(a, b):
    return jnp.dot(a, b, preferred_element_type=F32).astype(BF)


def attend_kernel(len_ref, c_ref, q_ref, kv_ref, new_ref, keep, send, latents):
    step = pl.program_id(0)
    heads = q_ref.shape[2]
    half = heads // 2
    lat = latents.shape[3]
    row, col = grid_of((heads, heads))
    core = jnp.where(row < half, c_ref[0], 1 - c_ref[0])
    order = onehot(col == ((row >> 2) & 15) * 8 + core * 4 + (row & 3))
    new = new_ref[...].astype(F32)
    score_scale = (VD + ROPE) ** (-0.5)
    for i in range(q_ref.shape[0]):
        r = step * q_ref.shape[0] + i
        q = lax.dot_general(order, q_ref[i], (((1,), (1,)), ((), ())), preferred_element_type=F32)
        fresh = jnp.sum(jnp.where(lax.broadcasted_iota(jnp.int32, new.shape, 0) == r, new, 0.0), axis=0, keepdims=True)
        scores = jnp.dot(q.astype(BF), kv_ref[i], preferred_element_type=F32) * score_scale
        self_score = jnp.sum(q * fresh, axis=1, keepdims=True) * score_scale
        live = lax.broadcasted_iota(jnp.int32, (1, scores.shape[1]), 1) < len_ref[r]
        scores = jnp.where(live, scores, -jnp.inf)
        top = jnp.maximum(jnp.max(scores, axis=1, keepdims=True), self_score)
        expo = jnp.exp(scores - top)
        self_expo = jnp.exp(self_score - top)
        total = jnp.sum(expo, axis=1, keepdims=True) + self_expo
        weights = (expo / total).astype(BF)
        self_weight = (self_expo / total).astype(BF).astype(F32)
        latent = lax.dot_general(weights, kv_ref[i, :lat, :], (((1,), (1,)), ((), ())), preferred_element_type=F32)
        latent = (latent + self_weight * fresh[:, :lat]).astype(BF)
        latents[0, r] = latent[:half]
        latents[1, r] = latent[half:]

    @pl.when(step == pl.num_programs(0) - 1)
    def _():
        rows = keep.shape[0]
        row, col = grid_of((rows, rows))
        order = onehot(col == ((row >> 2) & 3) * half + (row >> 4) * 4 + (row & 3))
        keep[...] = exact(order, latents[0].reshape(rows, lat))
        send[...] = exact(order, latents[1].reshape(rows, lat))


def attend(lengths, c, queries, kv_cache, new_latent, lat):
    reqs, heads, width = queries.shape
    slots = kv_cache.shape[1]
    rows = reqs * heads // 2
    out = pl.BlockSpec((rows, lat), lambda r, n, c: (0, 0))
    return pl.pallas_call(
        attend_kernel,
        grid_spec=pltpu.PrefetchScalarGridSpec(
            num_scalar_prefetch=2,
            grid=(reqs // 2,),
            in_specs=[
                pl.BlockSpec((2, width, heads), lambda r, n, c: (r, 0, 0)),
                pl.BlockSpec((2, width, slots), lambda r, n, c: (r, 0, 0)),
                pl.BlockSpec((reqs, width), lambda r, n, c: (0, 0)),
            ],
            out_specs=[out, out],
            scratch_shapes=[pltpu.VMEM((2, reqs, heads // 2, lat), BF)],
        ),
        out_shape=[jax.ShapeDtypeStruct((rows, lat), BF)] * 2,
        compiler_params=params(60),
        cost_estimate=pl.CostEstimate(flops=4 * reqs * heads * slots * width, bytes_accessed=2 * reqs * slots * width, transcendentals=reqs * heads * slots),
        name="attend",
    )(lengths, c, queries.transpose(0, 2, 1), kv_cache.transpose(0, 2, 1), new_latent)


def heads_kernel(x, values, out):
    rows, wide = out.shape[0], x.shape[0]
    row, col = grid_of((rows, wide))
    width = values.shape[2]
    for hh in range(values.shape[0]):
        latent = exact(onehot(col == row * 4 + hh), x[...])
        out[:, hh * width : (hh + 1) * width] = jnp.dot(latent, values[hh], preferred_element_type=F32).astype(BF)


def head_values(x, values):
    count, lat, width = values.shape
    rows = x.shape[0] // count
    return pl.pallas_call(
        heads_kernel,
        out_shape=jax.ShapeDtypeStruct((rows, count * width), BF),
        compiler_params=pltpu.CompilerParams(vmem_limit_bytes=16 * 1024 * 1024),
        cost_estimate=pl.CostEstimate(flops=2 * rows * count * lat * (width + x.shape[0]), bytes_accessed=2 * count * lat * width, transcendentals=0),
        name="head_values",
    )(x, values)


def first_kernel(parts, residual, first, wide):
    total = residual[...].astype(F32)
    for i in range(parts.shape[0]):
        total = total + parts[i].astype(F32)
    first[...] = total
    for i in range(parts.shape[0]):
        wide[i] = total.astype(BF)


def first_sum(parts, residual):
    return pl.pallas_call(
        first_kernel,
        out_shape=[jax.ShapeDtypeStruct(residual.shape, F32), jax.ShapeDtypeStruct(parts.shape, BF)],
        compiler_params=pltpu.CompilerParams(vmem_limit_bytes=16 * 1024 * 1024),
        cost_estimate=pl.CostEstimate(flops=parts.size, bytes_accessed=4 * parts.size, transcendentals=0),
        name="first_sum",
    )(parts, residual)


def second_kernel(parts, first, gain, second, scaled):
    total = first[...]
    for i in range(parts.shape[0]):
        total = total + parts[i].astype(F32)
    second[...] = total
    width = total.shape[1]
    scaled[:, :width] = (total * gain[...].astype(F32)).astype(BF)
    square = total * total
    lanes = square[:, :128]
    for j in range(1, width // 128):
        lanes = lanes + square[:, j * 128 : (j + 1) * 128]
    scaled[:, width:] = tail_of(lanes)


def second_sum(parts, first, gain):
    rows, width = first.shape
    return pl.pallas_call(
        second_kernel,
        out_shape=[jax.ShapeDtypeStruct(first.shape, F32), jax.ShapeDtypeStruct((rows, width + 128), BF)],
        compiler_params=pltpu.CompilerParams(vmem_limit_bytes=16 * 1024 * 1024),
        cost_estimate=pl.CostEstimate(flops=parts.size, bytes_accessed=2 * parts.size, transcendentals=0),
        name="second_sum",
    )(parts, first, gain.reshape(1, -1))


def route_kernel(picks, hots, combs, *, top):
    count = picks.shape[0]
    experts = 32
    ids, gates = picks[:, :top], picks[:, top : 2 * top]
    core = picks[:1, 2 * top : 2 * top + 1]
    expert = lax.broadcasted_iota(jnp.int32, (count, experts), 1).astype(F32)
    named = jnp.zeros((count, experts), F32)
    gate = jnp.zeros((count, experts), F32)
    for k in range(top):
        hit = ids[:, k : k + 1] == expert
        named = named + jnp.where(hit, 1.0, 0.0)
        gate = gate + jnp.where(hit, gates[:, k : k + 1], 0.0)
    row, col = grid_of((count, count))
    earlier = onehot((col < row) & ((col >> 4) == (row >> 4)))
    place = jnp.dot(earlier, named.astype(BF), preferred_element_type=F32)
    token = lax.broadcasted_iota(jnp.int32, (count, experts), 0)
    place = place + jnp.where(token >= 16, 6.0, 0.0)
    place = jnp.where(named > 0.5, place, 100.0)
    across = lambda rows, chip_of, values: lax.dot_general(
        onehot(grid_of((rows, experts))[1].astype(F32) == chip_of(grid_of((rows, experts))[0]).astype(F32) * 2.0 + core),
        values.astype(BF),
        (((1,), (1,)), ((), ())),
        preferred_element_type=F32,
    )
    rows = hots.shape[1]
    at = across(rows, lambda r: r >> 4, place)
    p = lax.broadcasted_iota(jnp.int32, (rows, 1), 0) & 15
    head = onehot(at == jnp.where(p < 12, p, -1).astype(F32))
    for m in range(3):
        tail = onehot(at == jnp.where(p >= 12, 3 * (p - 12) + m, -1).astype(F32))
        hots[m] = jnp.concatenate([head, tail], axis=1)
    rows = combs.shape[2]
    at = across(rows, lambda r: r >> 3, place)
    p = lax.broadcasted_iota(jnp.int32, (rows, 1), 0) & 7
    high = gate.astype(BF)
    for j, part in enumerate((high, gate - high.astype(F32))):
        value = across(rows, lambda r: r >> 3, part)
        for m in range(3):
            want = p if m == 0 else jnp.where((p & 1) == m - 1, 8 + (p >> 1), -1)
            combs[j, m] = jnp.where(at == want.astype(F32), value, 0.0).astype(BF)


def route(picks, top):
    count = picks.shape[0]
    return pl.pallas_call(
        lambda *refs: route_kernel(*refs, top=top),
        out_shape=[jax.ShapeDtypeStruct((3, 256, 2 * count), BF), jax.ShapeDtypeStruct((2, 3, 128, count), BF)],
        compiler_params=pltpu.CompilerParams(vmem_limit_bytes=16 * 1024 * 1024),
        cost_estimate=pl.CostEstimate(flops=1 << 22, bytes_accessed=1 << 18, transcendentals=0),
        name="route",
    )(picks)


def combine_kernel(returned, combs, second, own, other):
    width = own.shape[1]
    half = width // 2
    sums = []
    for m in range(3):
        x = returned[:, :width] if m == 0 else returned[:, width:]
        sums.append(
            sum(lax.dot_general(combs[j, m], x, (((0,), (0,)), ((), ())), preferred_element_type=F32) for j in range(2))
        )
    rows = own.shape[0]
    for m in range(2):
        lanes = slice(m * half, (m + 1) * half)
        total = sums[0][:, lanes] + sums[1 + m]
        own[:, lanes] = second[:, lanes] + total[:rows]
        other[:, lanes] = total[rows:]


def combine(returned, combs, second):
    return pl.pallas_call(
        combine_kernel,
        out_shape=[jax.ShapeDtypeStruct(second.shape, F32)] * 2,
        compiler_params=pltpu.CompilerParams(vmem_limit_bytes=16 * 1024 * 1024),
        cost_estimate=pl.CostEstimate(flops=12 * 32 * 128 * 1792, bytes_accessed=1 << 20, transcendentals=0),
        name="combine",
    )(returned, combs, second)


def pack_kernel(w0, w1, w2, w3, hot, out, *, width):
    total = None
    refs = (w0, w1, w2, w3)
    for ref in refs:
        part = jnp.sum(ref[:, width:].astype(F32), axis=1, keepdims=True)
        total = part if total is None else total + part
    scale = lax.rsqrt(total / D + EPS)
    normed = lambda ref: (ref[:, :width].astype(F32) * scale).astype(BF)
    step = pl.program_id(0)
    for m in range(3):

        @pl.when(step == m)
        def _():
            both = jnp.concatenate([normed(refs[m]), normed(w3)], axis=0)
            out[...] = exact(hot[0], both)


def pack(wide, hot, width):
    rows, depth = hot.shape[1:]
    whole = lambda ref: pl.BlockSpec(ref.shape, lambda i: (0, 0))
    return pl.pallas_call(
        lambda *refs: pack_kernel(*refs, width=width),
        grid=(3,),
        in_specs=[whole(w) for w in wide] + [pl.BlockSpec((1, rows, depth), lambda i: (i, 0, 0))],
        out_specs=pl.BlockSpec((rows, width), lambda i: (0, i)),
        out_shape=jax.ShapeDtypeStruct((rows, 3 * width), BF),
        compiler_params=params(),
        cost_estimate=pl.CostEstimate(flops=6 * rows * width * depth, bytes_accessed=6 * rows * width, transcendentals=0),
        name="pack",
    )(*wide, hot)


def params(mib=16):
    return pltpu.CompilerParams(dimension_semantics=("arbitrary",), vmem_limit_bytes=mib * 1024 * 1024)


def tail_of(squares):
    total = jnp.sum(squares, axis=1, keepdims=True)
    hi = total.astype(BF).astype(F32)
    lane = lax.broadcasted_iota(jnp.int32, (total.shape[0], 128), 1)
    return jnp.where(lane == 0, hi, jnp.where(lane == 1, total - hi, 0.0)).astype(BF)


def dense_in_kernel(z_ref, own, other, gain, gate, up, o0, o1, o2, o3, acc, squares, tail):
    step = pl.program_id(0)
    width = gate.shape[1]

    @pl.when(step == 0)
    def _():
        acc[...] = jnp.zeros_like(acc)
        squares[...] = jnp.zeros_like(squares)

    scale = gain[...].astype(F32)
    for rel, ref in enumerate((own, other)):
        value = ref[...].astype(F32)
        normed = (value * scale).astype(BF)
        acc[rel, :, :width] += jnp.dot(normed, gate[...], preferred_element_type=F32)
        acc[rel, :, width:] += jnp.dot(normed, up[...], preferred_element_type=F32)
        square = value * value
        for j in range(square.shape[1] // 128):
            squares[rel] += square[:, j * 128 : (j + 1) * 128]

    @pl.when(step == pl.num_programs(0) - 1)
    def _():
        z = z_ref[0]
        for rel in range(2):
            tail[rel] = tail_of(squares[rel])
        for k, out in enumerate((o0, o1, o2, o3)):
            at = pl.multiple_of(lax.rem(z + k, NZ) * 64, 64)
            for rel in range(2):
                rows = pl.ds(rel * 64, 64)
                out[rows, : 2 * width] = acc[rel, pl.ds(at, 64), :].astype(BF)
                out[rows, 2 * width :] = tail[rel, pl.ds(at, 64), :]


def dense_in(z, own, other, gain, gate, up):
    depth, width = gate.shape
    step = depth // 2
    rows = own.shape[0]
    lhs = pl.BlockSpec((rows, step), lambda i, z: (0, i))
    weight = pl.BlockSpec((step, width), lambda i, z: (i, 0))
    lanes = 2 * width + 128
    return pl.pallas_call(
        dense_in_kernel,
        grid_spec=pltpu.PrefetchScalarGridSpec(
            num_scalar_prefetch=1,
            grid=(depth // step,),
            in_specs=[lhs, lhs, pl.BlockSpec((1, step), lambda i, z: (0, i)), weight, weight],
            out_specs=[pl.BlockSpec((rows // 2, lanes), lambda i, z: (0, 0))] * NZ,
            scratch_shapes=[
                pltpu.VMEM((2, rows, 2 * width), F32),
                pltpu.VMEM((2, rows, 128), F32),
                pltpu.VMEM((2, rows, 128), BF),
            ],
        ),
        out_shape=[jax.ShapeDtypeStruct((rows // 2, lanes), BF)] * NZ,
        compiler_params=params(),
        cost_estimate=pl.CostEstimate(flops=8 * rows * depth * width, bytes_accessed=4 * depth * (rows + width), transcendentals=0),
        name="dense_in",
    )(z, own, other, gain.reshape(1, -1), gate, up)


def silu(value):
    return value / (1.0 + jnp.exp(-value))


def expert_in_kernel(z_ref, x0, x1, x2, *refs):
    gates, ups, out, (gate_acc, up_acc) = refs[:4], refs[4:8], refs[8], refs[9:]
    step = pl.program_id(0)

    @pl.when(step == 0)
    def _():
        gate_acc[...] = jnp.zeros_like(gate_acc)
        up_acc[...] = jnp.zeros_like(up_acc)

    rows, wide = out.shape[0], x0.shape[0]
    row, col = grid_of((wide, wide))
    place = row & 15
    third = sum(jnp.where(place >= n, 1, 0) for n in (3, 6, 9))
    source = jnp.where(place < 12, (row & ~15) + 12 + third, -1)
    rest = None
    quarters = []
    for m, ref in enumerate((x0, x1, x2)):
        quarters.append(ref[...])
        pick = onehot((col == source) & (place - 3 * third == m))
        term = jnp.dot(pick, ref[...], preferred_element_type=F32)
        rest = term if rest is None else rest + term
    quarters.append(rest.astype(BF))
    for m in range(NZ):
        gate_acc[...] += jnp.dot(quarters[m], gates[m][...], preferred_element_type=F32)
        up_acc[...] += jnp.dot(quarters[m], ups[m][...], preferred_element_type=F32)

    @pl.when(step == pl.num_programs(0) - 1)
    def _():
        hidden = (silu(gate_acc[...]) * up_acc[...]).astype(BF)
        row, col = grid_of((rows, wide))
        keep = ((col & 15) < 12) & (row == (col >> 4) * 12 + (col & 15))
        out[...] = exact(onehot(keep), hidden)


def expert_in(z, x, gate, up, rows):
    depth, width = gate.shape
    steps = 2
    step = depth // NZ // steps
    xs = [pl.BlockSpec((x.shape[0], step), lambda i, z, m=m: (0, m * steps + i)) for m in range(3)]
    ws = [pl.BlockSpec((step, width), lambda i, z, m=m: (lax.rem(z[0] + m, NZ) * steps + i, 0)) for m in range(NZ)]
    return pl.pallas_call(
        expert_in_kernel,
        grid_spec=pltpu.PrefetchScalarGridSpec(
            num_scalar_prefetch=1,
            grid=(steps,),
            in_specs=xs + ws + ws,
            out_specs=pl.BlockSpec((rows, width), lambda i, z: (0, 0)),
            scratch_shapes=[pltpu.VMEM((x.shape[0], width), F32)] * 2,
        ),
        out_shape=jax.ShapeDtypeStruct((rows, width), BF),
        compiler_params=params(),
        cost_estimate=pl.CostEstimate(flops=4 * rows * depth * width, bytes_accessed=4 * depth * width, transcendentals=0),
        name="expert_in",
    )(z, x, x, x, *[gate] * 4, *[up] * 4)


def expert_out_kernel(z_ref, *refs):
    hidden, weights, out, wide = refs[:4], refs[4:8], refs[8], refs[9]
    step = pl.program_id(0)
    rows = out.shape[0]

    @pl.when(step == 0)
    def _():
        row, col = grid_of((2 * rows, hidden[0].shape[0]))
        at = row & (rows - 1)
        slot = jnp.where(row < rows, at & 7, 8 + ((at & 7) >> 1))
        order = onehot(col == (at >> 3) * 12 + slot)
        for k in range(NZ):
            wide[k] = exact(order, hidden[k][...])

    half = weights[0].shape[1]
    mine = (lax.broadcasted_iota(jnp.int32, (rows, 128), 0) & 1) == step
    for n in range(0, half, 128):
        total = None
        for k in range(NZ):
            term = jnp.dot(wide[k], weights[k][:, n : n + 128], preferred_element_type=F32)
            total = term if total is None else total + term
        total = total.astype(BF)
        out[:, pl.ds(pl.multiple_of(step * half + n, 128), 128)] = total[:rows]
        lanes = slice(2 * half + n, 2 * half + n + 128)
        out[:, lanes] = jnp.where(mine, total[rows:], out[:, lanes])


def expert_out(z, hidden, down, got):
    rows, width = hidden[0].shape
    columns = got[0].shape[1]
    steps = 2
    step = columns // steps
    whole = (rows // 12 * 8, columns + step)
    return pl.pallas_call(
        expert_out_kernel,
        grid_spec=pltpu.PrefetchScalarGridSpec(
            num_scalar_prefetch=1,
            grid=(steps,),
            in_specs=[pl.BlockSpec((rows, width), lambda i, z: (0, 0))] * NZ
            + [pl.BlockSpec((width, step), lambda i, z: (0, z[0] * steps + i))]
            + [pl.BlockSpec((width, step), lambda i, z: (0, i))] * 3,
            out_specs=pl.BlockSpec(whole, lambda i, z: (0, 0)),
            scratch_shapes=[pltpu.VMEM((NZ, 2 * whole[0], width), BF)],
        ),
        out_shape=jax.ShapeDtypeStruct(whole, BF),
        compiler_params=params(),
        cost_estimate=pl.CostEstimate(flops=16 * whole[0] * width * columns, bytes_accessed=8 * width * columns, transcendentals=0),
        name="expert_out",
    )(z, *hidden, down, *got)


def dense_out_kernel(z_ref, h0, h1, h2, h3, weight, *refs, rel):
    *arrived, out, held = refs

    @pl.when(pl.program_id(0) == 0)
    def _():
        z = z_ref[0]
        for k, ref in enumerate((h0, h1, h2, h3)):
            at = pl.multiple_of(lax.rem(z + k, NZ) * 64, 64)
            held[pl.ds(at, 64), :] = ref[...]

    total = jnp.dot(held[...], weight[...], preferred_element_type=F32)
    for ref in arrived:
        total = total + ref[...].astype(F32)
    out[...] = total.astype(BF)


def out_proj_kernel(z_ref, h0, h1, h2, h3, weight, *refs, rel):
    *arrived, out, held = refs

    @pl.when(pl.program_id(0) == 0)
    def _():
        z = z_ref[0]
        rows, cols = held.shape[0], h0.shape[0]
        row = lax.broadcasted_iota(jnp.int32, (rows, cols), 0)
        col = lax.broadcasted_iota(jnp.int32, (rows, cols), 1)
        match = col == (row >> 4) * 8 + rel * 4 + (row & 3)
        total = None
        for k, ref in enumerate((h0, h1, h2, h3)):
            hit = match & (((row >> 2) & 3) == lax.rem(z + k, NZ))
            term = jnp.dot(jnp.where(hit, 1.0, 0.0).astype(BF), ref[...], preferred_element_type=F32)
            total = term if total is None else total + term
        held[...] = total.astype(BF)

    total = jnp.dot(held[...], weight[...], preferred_element_type=F32)
    for ref in arrived:
        total = total + ref[...].astype(F32)
    out[...] = total.astype(BF)


def plane_dot(kernel, z, blocks, weight, rel, *arrived):
    depth, columns = weight.shape
    step = columns // 2
    block_rows, at = (64, rel) if kernel is dense_out_kernel else (128, 0)
    return pl.pallas_call(
        lambda *refs: kernel(*refs, rel=rel),
        grid_spec=pltpu.PrefetchScalarGridSpec(
            num_scalar_prefetch=1,
            grid=(columns // step,),
            in_specs=[pl.BlockSpec((block_rows, depth), lambda i, z: (at, 0))] * NZ
            + [pl.BlockSpec((depth, step), lambda i, z: (0, i))]
            + [pl.BlockSpec((256, step), lambda i, z: (0, i))] * len(arrived),
            out_specs=pl.BlockSpec((256, step), lambda i, z: (0, i)),
            scratch_shapes=[pltpu.VMEM((256, depth), BF)],
        ),
        out_shape=jax.ShapeDtypeStruct((256, columns), BF),
        compiler_params=params(),
        cost_estimate=pl.CostEstimate(flops=512 * depth * columns, bytes_accessed=2 * depth * columns, transcendentals=0),
        name=("dense_out" if kernel is dense_out_kernel else "out_proj") + ("_other" if rel else "_own"),
    )(z, *blocks, weight, *arrived)


def shards(
    queries, kv_cache, new_latent, lengths, residual, gain_first, gain_second, value_proj, out_proj,
    dense_gate, dense_up, dense_down, route_ids, route_gates, expert_gate, expert_up, expert_down,
):
    z = lax.axis_index("z")
    c = lax.axis_index("c")
    latent_dim = value_proj.shape[1]
    quarter = residual.shape[1]

    zs = z.astype(jnp.int32).reshape(1)

    def pick(w, k, axis):
        return lax.dynamic_slice_in_dim(w, lax.rem(z + k, NZ) * quarter, quarter, axis)

    def cut(w, axis, which):
        return {k: pick(w, NZ - k, axis) for k in which}

    def tied(value, *groups):
        flat = [group[k] for group in groups for k in group]
        value, *flat = lax.optimization_barrier((value, *flat))
        at = iter(flat)
        return (value, *[{k: next(at) for k in group} for group in groups])

    def fetch(group):
        return {k: zsend(group[k], NZ - k) for k in group}

    only = lambda group, *which: {k: group[k] for k in which}
    picks = jnp.concatenate([route_ids.astype(F32), route_gates], axis=1)
    picks = jnp.concatenate([picks, swap_core(picks)], axis=0)
    picks = jnp.concatenate([picks, jnp.broadcast_to(c.astype(F32), (picks.shape[0], 1))], axis=1)
    hots, combs = route(picks, route_ids.shape[1])

    keep, send = attend(lengths, c.astype(jnp.int32).reshape(1), queries, kv_cache, new_latent, latent_dim)
    both = jnp.stack([keep.reshape(16, 16, -1), swap_core(send).reshape(16, 16, -1)], axis=1)
    moved = lax.all_to_all(both.reshape(16, 32, -1), YX, 0, 0, tiled=True)
    rows = zgather(head_values(moved.reshape(512, -1), value_proj))
    rows, down_cut = tied(rows, cut(expert_down[0], 1, (1, 2, 3)))
    down_a = fetch(only(down_cut, 1, 3))
    parts = plane_scatter(out_proj_kernel, zs, rows, out_proj)
    parts, down_a, down_cut = tied(parts, down_a, only(down_cut, 2))
    first, spread = first_sum(parts, residual)
    own = lax.all_to_all(spread, YX, 0, 0, tiled=True).reshape(256, -1)
    other = swap_core(own)
    width = dense_gate.shape[1]
    blocks = dense_in(zs, own, other, gain_first, dense_gate, dense_up)
    summed = zscatter(blocks)
    scale = lax.rsqrt((summed[:, 2 * width] + summed[:, 2 * width + 1]) / D + EPS)[:, None]
    gate_act = summed[:, :width] * scale
    hidden = (jax.nn.silu(gate_act) * (summed[:, width : 2 * width] * scale)).astype(BF)
    hidden = zgather(hidden)
    hidden, down_cut = tied(hidden, down_cut)
    down_b = fetch(down_cut)
    parts = plane_scatter(dense_out_kernel, zs, hidden, dense_down)
    parts, down_b = tied(parts, down_b)
    second, scaled = second_sum(parts, first, gain_second)

    scaled = jnp.concatenate([scaled, swap_core(scaled)], axis=0)
    wide = zgather(scaled)
    sendbuf = pack(wide, hots, quarter).reshape(16, 16, -1)
    arrived = lax.all_to_all(sendbuf, YX, 0, 0, tiled=True).reshape(256, -1)
    expert_hidden = expert_in(zs, arrived, expert_gate[0], expert_up[0], 192)
    result = expert_out(zs, zgather(expert_hidden), expert_down[0], [down_a[1], down_b[2], down_a[3]])
    returned = lax.all_to_all(result.reshape(16, 8, -1), YX, 0, 0, tiled=True).reshape(128, -1)
    total, theirs = combine(returned, combs, second)
    return (total + swap_core(theirs)).astype(BF)


def solution(mesh):
    grid = Mesh(mesh.devices.reshape(4, 4, 2, 4), ("y", "x", "c", "z"))
    ep = ("y", "x", "c")
    both = ("y", "x", "c", "z")
    return jax.shard_map(
        shards,
        mesh=grid,
        in_specs=(
            P(both, None, None),
            P(both, None, None),
            P(both, None),
            P(both),
            P(ep, "z"),
            P("z"),
            P("z"),
            P(ep, None, None),
            P(ep, "z"),
            P("z", ep),
            P("z", ep),
            P(ep, "z"),
            P(ep, None),
            P(ep, None),
            P(ep, None, "z"),
            P(ep, None, "z"),
            P(ep, "z", None),
        ),
        out_specs=P(ep, "z"),
        check_vma=False,
    )
```

```python
import jax
import jax.numpy as jnp
from jax import lax
from jax.experimental import pallas as pl
from jax.experimental.pallas import tpu as pltpu
from jax.sharding import Mesh, PartitionSpec as P

D = 7168
ROPE = 64
VD = 128
EPS = 1e-06
YX = ("y", "x")
NZ = 4
BF = jnp.bfloat16
F32 = jnp.float32


def zsend(values, shift):
    return lax.ppermute(values, "z", [(i, (i + shift) % NZ) for i in range(NZ)])


def swap_core(values):
    return lax.ppermute(values, "c", [(0, 1), (1, 0)])


def zgather(values):
    return [values] + [zsend(values, NZ - k) for k in (1, 2, 3)]


def zscatter(blocks):
    got = [zsend(blocks[k], k) for k in (1, 2, 3)]
    total = blocks[0].astype(F32)
    for piece in got:
        total = total + piece.astype(F32)
    return total


def plane_scatter(mine, other):
    mine = (mine + swap_core(other).astype(F32)).astype(BF)
    return lax.all_to_all(mine.reshape(16, 16, -1), YX, 0, 0, tiled=True)


def onehot(hit):
    return jnp.where(hit, 1.0, 0.0).astype(BF)


def grid_of(shape):
    return lax.broadcasted_iota(jnp.int32, shape, 0), lax.broadcasted_iota(jnp.int32, shape, 1)


def exact(a, b):
    return jnp.dot(a, b, preferred_element_type=F32).astype(BF)


def attend_kernel(len_ref, c_ref, q_ref, kv_ref, new_ref, out, latents):
    step = pl.program_id(0)
    lat = latents.shape[2]
    new = new_ref[...].astype(F32)
    score_scale = (VD + ROPE) ** (-0.5)
    down = (((0,), (0,)), ((), ()))
    for i in range(q_ref.shape[0]):
        r = step * q_ref.shape[0] + i
        q = q_ref[i]
        fresh = jnp.sum(jnp.where(lax.broadcasted_iota(jnp.int32, new.shape, 0) == r, new, 0.0), axis=0, keepdims=True)
        scores = lax.dot_general(q, kv_ref[i], down, preferred_element_type=F32) * score_scale
        own = lax.dot_general(q, new_ref[...], (((0,), (1,)), ((), ())), preferred_element_type=F32)
        own = jnp.where(lax.broadcasted_iota(jnp.int32, own.shape, 1) == r, own, 0.0)
        self_score = jnp.sum(own, axis=1, keepdims=True) * score_scale
        live = lax.broadcasted_iota(jnp.int32, (1, scores.shape[1]), 1) < len_ref[r]
        scores = jnp.where(live, scores, -jnp.inf)
        top = jnp.maximum(jnp.max(scores, axis=1, keepdims=True), self_score)
        expo = jnp.exp(scores - top)
        self_expo = jnp.exp(self_score - top)
        total = 1.0 / (jnp.sum(expo, axis=1, keepdims=True) + self_expo)
        weights = (expo * total).astype(BF)
        self_weight = (self_expo * total).astype(BF).astype(F32)
        latent = lax.dot_general(weights, kv_ref[i, :lat, :], (((1,), (1,)), ((), ())), preferred_element_type=F32)
        latents[r] = (latent + self_weight * fresh[:, :lat]).astype(BF)

    @pl.when(step == pl.num_programs(0) - 1)
    def _():
        rows = out.shape[0]
        heads = rows // latents.shape[0]
        held = latents[...].reshape(rows, lat)
        part = rows // 2
        for i in range(2):
            row, col = grid_of((part, rows))
            row = row + i * part
            core = jnp.where((row & 16) == 0, c_ref[0], 1 - c_ref[0])
            order = onehot(col == ((row >> 2) & 3) * heads + (row >> 5) * 8 + core * 4 + (row & 3))
            out[i * part : (i + 1) * part, :] = exact(order, held)


def attend(lengths, c, queries, kv_cache, new_latent, lat):
    reqs, heads, width = queries.shape
    slots = kv_cache.shape[1]
    rows = reqs * heads
    return pl.pallas_call(
        attend_kernel,
        grid_spec=pltpu.PrefetchScalarGridSpec(
            num_scalar_prefetch=2,
            grid=(reqs // 2,),
            in_specs=[
                pl.BlockSpec((2, width, heads), lambda r, n, c: (r, 0, 0)),
                pl.BlockSpec((2, width, slots), lambda r, n, c: (r, 0, 0)),
                pl.BlockSpec((reqs, width), lambda r, n, c: (0, 0)),
            ],
            out_specs=pl.BlockSpec((rows, lat), lambda r, n, c: (0, 0)),
            scratch_shapes=[pltpu.VMEM((reqs, heads, lat), BF)],
        ),
        out_shape=jax.ShapeDtypeStruct((rows, lat), BF),
        compiler_params=params(60),
        cost_estimate=pl.CostEstimate(flops=4 * reqs * heads * slots * width, bytes_accessed=2 * reqs * slots * width, transcendentals=reqs * heads * slots),
        name="attend",
    )(lengths, c, queries.transpose(0, 2, 1), kv_cache.transpose(0, 2, 1), new_latent)


def heads_kernel(x, got, values, out):
    width = values.shape[2]
    for hh in range(values.shape[0]):
        row, col = grid_of((out.shape[0], x.shape[0]))
        pick = onehot(((row & 4) == 0) & (col == (row >> 3) * 32 + (row & 3) * 4 + hh))
        latent = jnp.dot(pick, x[...], preferred_element_type=F32)
        row, col = grid_of((out.shape[0], got.shape[0]))
        pick = onehot(((row & 4) != 0) & (col == (row >> 3) * 16 + (row & 3) * 4 + hh))
        latent = latent + jnp.dot(pick, got[...], preferred_element_type=F32)
        latent = jnp.dot(latent.astype(BF), values[hh], preferred_element_type=F32)
        out[:, hh * width : (hh + 1) * width] = latent.astype(BF)


def head_values(x, got, values):
    count, lat, width = values.shape
    rows = x.shape[0] // count
    return pl.pallas_call(
        heads_kernel,
        out_shape=jax.ShapeDtypeStruct((rows, count * width), BF),
        compiler_params=pltpu.CompilerParams(vmem_limit_bytes=16 * 1024 * 1024),
        cost_estimate=pl.CostEstimate(flops=2 * rows * count * lat * (width + x.shape[0]), bytes_accessed=2 * count * lat * width, transcendentals=0),
        name="head_values",
    )(x, got, values)


def first_kernel(parts, residual, first, wide):
    total = residual[...].astype(F32)
    for i in range(parts.shape[0]):
        total = total + parts[i].astype(F32)
    first[...] = total
    for i in range(parts.shape[0]):
        wide[i] = total.astype(BF)


def first_sum(parts, residual):
    return pl.pallas_call(
        first_kernel,
        out_shape=[jax.ShapeDtypeStruct(residual.shape, F32), jax.ShapeDtypeStruct(parts.shape, BF)],
        compiler_params=pltpu.CompilerParams(vmem_limit_bytes=16 * 1024 * 1024),
        cost_estimate=pl.CostEstimate(flops=parts.size, bytes_accessed=24 * parts.size, transcendentals=0),
        name="first_sum",
    )(parts, residual)


def second_kernel(parts, first, gain, second, scaled):
    total = first[...]
    for i in range(parts.shape[0]):
        total = total + parts[i].astype(F32)
    second[...] = total
    width = total.shape[1]
    scaled[:, :width] = (total * gain[...].astype(F32)).astype(BF)
    square = total * total
    lanes = square[:, :128]
    for j in range(1, width // 128):
        lanes = lanes + square[:, j * 128 : (j + 1) * 128]
    scaled[:, width:] = tail_of(lanes)


def second_sum(parts, first, gain):
    rows, width = first.shape
    return pl.pallas_call(
        second_kernel,
        out_shape=[jax.ShapeDtypeStruct(first.shape, F32), jax.ShapeDtypeStruct((rows, width + 128), BF)],
        compiler_params=pltpu.CompilerParams(vmem_limit_bytes=16 * 1024 * 1024),
        cost_estimate=pl.CostEstimate(flops=parts.size, bytes_accessed=2 * parts.size, transcendentals=0),
        name="second_sum",
    )(parts, first, gain.reshape(1, -1))


def route_kernel(picks, hots, combs, *, top):
    count = picks.shape[0]
    experts = 32
    ids, gates = picks[:, :top], picks[:, top : 2 * top]
    core = picks[:1, 2 * top : 2 * top + 1]
    expert = lax.broadcasted_iota(jnp.int32, (count, experts), 1).astype(F32)
    named = jnp.zeros((count, experts), F32)
    gate = jnp.zeros((count, experts), F32)
    for k in range(top):
        hit = ids[:, k : k + 1] == expert
        named = named + jnp.where(hit, 1.0, 0.0)
        gate = gate + jnp.where(hit, gates[:, k : k + 1], 0.0)
    row, col = grid_of((count, count))
    earlier = onehot((col < row) & ((col >> 4) == (row >> 4)))
    place = jnp.dot(earlier, named.astype(BF), preferred_element_type=F32)
    token = lax.broadcasted_iota(jnp.int32, (count, experts), 0)
    place = place + jnp.where(token >= 16, 6.0, 0.0)
    place = jnp.where(named > 0.5, place, 100.0)
    across = lambda rows, chip_of, values: lax.dot_general(
        onehot(grid_of((rows, experts))[1].astype(F32) == chip_of(grid_of((rows, experts))[0]).astype(F32) * 2.0 + core),
        values.astype(BF),
        (((1,), (1,)), ((), ())),
        preferred_element_type=F32,
    )
    rows = combs.shape[2]
    at = across(rows, lambda r: r >> 3, place)
    p = lax.broadcasted_iota(jnp.int32, (rows, 1), 0) & 7
    hots[0] = onehot(at == p.astype(F32))
    hots[1] = onehot(at == (8 + (p >> 1)).astype(F32))
    high = gate.astype(BF)
    for j, part in enumerate((high, gate - high.astype(F32))):
        value = across(rows, lambda r: r >> 3, part)
        for m in range(3):
            want = p if m == 0 else jnp.where((p & 1) == m - 1, 8 + (p >> 1), -1)
            combs[j, m] = jnp.where(at == want.astype(F32), value, 0.0).astype(BF)


def route(picks, top):
    count = picks.shape[0]
    return pl.pallas_call(
        lambda *refs: route_kernel(*refs, top=top),
        out_shape=[jax.ShapeDtypeStruct((2, 128, count), BF), jax.ShapeDtypeStruct((2, 3, 128, count), BF)],
        compiler_params=pltpu.CompilerParams(vmem_limit_bytes=16 * 1024 * 1024),
        cost_estimate=pl.CostEstimate(flops=1 << 22, bytes_accessed=1 << 18, transcendentals=0),
        name="route",
    )(picks)


def combine_kernel(returned, combs, second, own, other):
    width = own.shape[1]
    half = width // 2
    sums = []
    for m in range(3):
        x = returned[:, :width] if m == 0 else returned[:, width:]
        sums.append(
            sum(lax.dot_general(combs[j, m], x, (((0,), (0,)), ((), ())), preferred_element_type=F32) for j in range(2))
        )
    rows = own.shape[0]
    for m in range(2):
        lanes = slice(m * half, (m + 1) * half)
        total = sums[0][:, lanes] + sums[1 + m]
        own[:, lanes] = second[:, lanes] + total[:rows]
        other[:, lanes] = total[rows:]


def combine(returned, combs, second):
    return pl.pallas_call(
        combine_kernel,
        out_shape=[jax.ShapeDtypeStruct(second.shape, F32)] * 2,
        compiler_params=pltpu.CompilerParams(vmem_limit_bytes=16 * 1024 * 1024),
        cost_estimate=pl.CostEstimate(flops=12 * 32 * 128 * 1792, bytes_accessed=1 << 20, transcendentals=0),
        name="combine",
    )(returned, combs, second)


def pack_kernel(x, hots, out, *, width):
    half = width // 2
    rows = out.shape[0]
    head = exact(hots[0], x[...])
    tail = exact(hots[1], x[...])
    out[:, :width] = head[:, :width]
    even = (lax.broadcasted_iota(jnp.int32, (rows, half), 0) & 1) == 0
    out[:, width : width + half] = jnp.where(even, tail[:, :half], tail[:, half:width])
    lane = lax.broadcasted_iota(jnp.int32, (rows, 128), 1)
    out[:, width + half :] = jnp.where(lane < 2, head[:, width:], tail[:, width:])


def pack(x, hots, width):
    rows = hots.shape[1]
    return pl.pallas_call(
        lambda *refs: pack_kernel(*refs, width=width),
        out_shape=jax.ShapeDtypeStruct((rows, width * 3 // 2 + 128), BF),
        compiler_params=pltpu.CompilerParams(vmem_limit_bytes=16 * 1024 * 1024),
        cost_estimate=pl.CostEstimate(flops=4 * rows * width * 32, bytes_accessed=3 * rows * width, transcendentals=0),
        name="pack",
    )(x, hots)


def params(mib=16):
    return pltpu.CompilerParams(dimension_semantics=("arbitrary",), vmem_limit_bytes=mib * 1024 * 1024)


def tail_of(squares):
    total = jnp.sum(squares, axis=1, keepdims=True)
    hi = total.astype(BF).astype(F32)
    lane = lax.broadcasted_iota(jnp.int32, (total.shape[0], 128), 1)
    return jnp.where(lane < 4, jnp.where((lane & 1) == 0, hi, total - hi), 0.0).astype(BF)


def dense_in_kernel(z_ref, x, gain, gate, up, o0, o1, o2, o3, acc, squares, tail):
    step = pl.program_id(0)
    width = gate.shape[1]

    @pl.when(step == 0)
    def _():
        acc[...] = jnp.zeros_like(acc)
        squares[...] = jnp.zeros_like(squares)

    value = x[...].astype(F32)
    normed = (value * gain[...].astype(F32)).astype(BF)
    acc[:, :width] += jnp.dot(normed, gate[...], preferred_element_type=F32)
    acc[:, width:] += jnp.dot(normed, up[...], preferred_element_type=F32)
    square = value * value
    for j in range(square.shape[1] // 128):
        squares[...] += square[:, j * 128 : (j + 1) * 128]

    @pl.when(step == pl.num_programs(0) - 1)
    def _():
        z = z_ref[0]
        tail[...] = tail_of(squares[...])
        part = acc.shape[0] // NZ
        for k, out in enumerate((o0, o1, o2, o3)):
            at = pl.ds(pl.multiple_of(lax.rem(z + k, NZ) * part, part), part)
            out[:, : 2 * width] = acc[at, :].astype(BF)
            out[:, 2 * width :] = tail[at, :]


def dense_in(z, x, gain, gate, up, name):
    depth, width = gate.shape
    step = depth // 2
    rows = x.shape[0]
    weight = pl.BlockSpec((step, width), lambda i, z: (i, 0))
    lanes = 2 * width + 128
    return pl.pallas_call(
        dense_in_kernel,
        grid_spec=pltpu.PrefetchScalarGridSpec(
            num_scalar_prefetch=1,
            grid=(depth // step,),
            in_specs=[
                pl.BlockSpec((rows, step), lambda i, z: (0, i)),
                pl.BlockSpec((1, step), lambda i, z: (0, i)),
                weight,
                weight,
            ],
            out_specs=[pl.BlockSpec((rows // NZ, lanes), lambda i, z: (0, 0))] * NZ,
            scratch_shapes=[
                pltpu.VMEM((rows, 2 * width), F32),
                pltpu.VMEM((rows, 128), F32),
                pltpu.VMEM((rows, 128), BF),
            ],
        ),
        out_shape=[jax.ShapeDtypeStruct((rows // NZ, lanes), BF)] * NZ,
        compiler_params=params(),
        cost_estimate=pl.CostEstimate(flops=4 * rows * depth * width, bytes_accessed=4 * depth * (rows + width), transcendentals=0),
        name=name,
    )(z, x, gain.reshape(1, -1), gate, up)


def silu(value):
    return value / (1.0 + jnp.exp(-value))


def expert_in_kernel(z_ref, *refs):
    heads, tails, sums, gates, ups = (refs[4 * j : 4 * j + 4] for j in range(5))
    out, gate_acc, up_acc = refs[20:]
    step = pl.program_id(0)

    @pl.when(step == 0)
    def _():
        gate_acc[...] = jnp.zeros_like(gate_acc)
        up_acc[...] = jnp.zeros_like(up_acc)

    rows = heads[0].shape[0]
    row, col = grid_of((rows // 2, rows))
    pick = onehot(col == 2 * row + step)
    for m in range(NZ):
        x = jnp.concatenate([heads[m][...], exact(pick, tails[m][...])], axis=0)
        gate_acc[...] += jnp.dot(x, gates[m][...], preferred_element_type=F32)
        up_acc[...] += jnp.dot(x, ups[m][...], preferred_element_type=F32)

    @pl.when(step == pl.num_programs(0) - 1)
    def _():
        lane = lax.broadcasted_iota(jnp.int32, (1, 128), 1)
        total = None
        for ref in sums:
            square = jnp.concatenate(
                [
                    jnp.where(lane < 2, ref[...].astype(F32), 0.0),
                    jnp.where((lane >= 2) & (lane < 4), jnp.dot(pick, ref[...], preferred_element_type=F32), 0.0),
                ],
                axis=0,
            )
            total = square if total is None else total + square
        scale = lax.rsqrt(jnp.sum(total, axis=1, keepdims=True) / D + EPS)
        out[...] = (silu(gate_acc[...] * scale) * (up_acc[...] * scale)).astype(BF)


def expert_in(z, xs, gate, up):
    depth, width = gate.shape
    steps = 2
    step = depth // NZ // steps
    rows = xs[0].shape[0]
    heads = [pl.BlockSpec((rows, step), lambda i, z: (0, i))] * NZ
    tails = [pl.BlockSpec((rows, step), lambda i, z: (0, 2))] * NZ
    sums = [pl.BlockSpec((rows, 128), lambda i, z: (0, 3 * step // 128))] * NZ
    ws = [pl.BlockSpec((step, width), lambda i, z, m=m: (lax.rem(z[0] + m, NZ) * steps + i, 0)) for m in range(NZ)]
    total = rows * 3 // 2
    return pl.pallas_call(
        expert_in_kernel,
        grid_spec=pltpu.PrefetchScalarGridSpec(
            num_scalar_prefetch=1,
            grid=(steps,),
            in_specs=heads + tails + sums + ws + ws,
            out_specs=pl.BlockSpec((total, width), lambda i, z: (0, 0)),
            scratch_shapes=[pltpu.VMEM((total, width), F32)] * 2,
        ),
        out_shape=jax.ShapeDtypeStruct((total, width), BF),
        compiler_params=params(),
        cost_estimate=pl.CostEstimate(flops=4 * total * depth * width, bytes_accessed=4 * depth * width, transcendentals=0),
        name="expert_in",
    )(z, *xs, *xs, *xs, *[gate] * 4, *[up] * 4)


def expert_out_kernel(z_ref, *refs):
    hidden, weights, out, wide = refs[:4], refs[4:8], refs[8], refs[9]
    step = pl.program_id(0)
    rows = out.shape[0]

    @pl.when(step == 0)
    def _():
        row, col = grid_of((rows, rows // 2))
        order = onehot(col == row >> 1)
        for k in range(NZ):
            wide[k, :rows] = hidden[k][:rows]
            wide[k, rows:] = exact(order, hidden[k][rows:])

    half = weights[0].shape[1]
    for n in range(0, half, 256):
        tile = min(256, half - n)
        total = None
        for k in range(NZ):
            term = jnp.dot(wide[k], weights[k][:, n : n + tile], preferred_element_type=F32)
            total = term if total is None else total + term
        total = total.astype(BF)
        out[:, pl.ds(pl.multiple_of(step * half + n, 128), tile)] = total[:rows]
        lanes = slice(2 * half + n, 2 * half + n + tile)
        mine = (lax.broadcasted_iota(jnp.int32, (rows, tile), 0) & 1) == step
        out[:, lanes] = jnp.where(mine, total[rows:], out[:, lanes])


def expert_out(z, hidden, down, got):
    rows, width = hidden[0].shape
    columns = got[0].shape[1]
    steps = 2
    step = columns // steps
    whole = (rows // 12 * 8, columns + step)
    return pl.pallas_call(
        expert_out_kernel,
        grid_spec=pltpu.PrefetchScalarGridSpec(
            num_scalar_prefetch=1,
            grid=(steps,),
            in_specs=[pl.BlockSpec((rows, width), lambda i, z: (0, 0))] * NZ
            + [pl.BlockSpec((width, step), lambda i, z: (0, z[0] * steps + i))]
            + [pl.BlockSpec((width, step), lambda i, z: (0, i))] * 3,
            out_specs=pl.BlockSpec(whole, lambda i, z: (0, 0)),
            scratch_shapes=[pltpu.VMEM((NZ, 2 * whole[0], width), BF)],
        ),
        out_shape=jax.ShapeDtypeStruct(whole, BF),
        compiler_params=params(),
        cost_estimate=pl.CostEstimate(flops=16 * whole[0] * width * columns, bytes_accessed=8 * width * columns, transcendentals=0),
        name="expert_out",
    )(z, *hidden, down, *got)


def dense_out_kernel(z_ref, h0, h1, h2, h3, weight, *refs, rel):
    out, held = refs

    @pl.when(pl.program_id(0) == 0)
    def _():
        z = z_ref[0]
        for k, ref in enumerate((h0, h1, h2, h3)):
            at = pl.multiple_of(lax.rem(z + k, NZ) * 64, 64)
            held[pl.ds(at, 64), :] = ref[...]

    total = jnp.dot(held[...], weight[...], preferred_element_type=F32)
    out[...] = total.astype(out.dtype)


def out_proj_kernel(z_ref, h0, h1, h2, h3, weight, *refs, rel):
    out, held = refs

    @pl.when(pl.program_id(0) == 0)
    def _():
        z = z_ref[0]
        rows, cols = held.shape[0], h0.shape[0]
        row = lax.broadcasted_iota(jnp.int32, (rows, cols), 0)
        col = lax.broadcasted_iota(jnp.int32, (rows, cols), 1)
        match = col == (row >> 4) * 8 + rel * 4 + (row & 3)
        total = None
        for k, ref in enumerate((h0, h1, h2, h3)):
            hit = match & (((row >> 2) & 3) == lax.rem(z + k, NZ))
            term = jnp.dot(jnp.where(hit, 1.0, 0.0).astype(BF), ref[...], preferred_element_type=F32)
            total = term if total is None else total + term
        held[...] = total.astype(BF)

    total = jnp.dot(held[...], weight[...], preferred_element_type=F32)
    out[...] = total.astype(out.dtype)


def plane_dot(kernel, z, blocks, weight, rel):
    depth, columns = weight.shape
    step = columns
    block_rows = blocks[0].shape[0]
    return pl.pallas_call(
        lambda *refs: kernel(*refs, rel=rel),
        grid_spec=pltpu.PrefetchScalarGridSpec(
            num_scalar_prefetch=1,
            grid=(columns // step,),
            in_specs=[pl.BlockSpec((block_rows, depth), lambda i, z: (0, 0))] * NZ
            + [pl.BlockSpec((depth, step), lambda i, z: (0, i))],
            out_specs=pl.BlockSpec((256, step), lambda i, z: (0, i)),
            scratch_shapes=[pltpu.VMEM((256, depth), BF)],
        ),
        out_shape=jax.ShapeDtypeStruct((256, columns), BF if rel else F32),
        compiler_params=params(),
        cost_estimate=pl.CostEstimate(flops=512 * depth * columns, bytes_accessed=2 * depth * columns, transcendentals=0),
        name=("dense_out" if kernel is dense_out_kernel else "out_proj") + ("_other" if rel else "_own"),
    )(z, *blocks, weight)


def shards(
    queries, kv_cache, new_latent, lengths, residual, gain_first, gain_second, value_proj, out_proj,
    dense_gate, dense_up, dense_down, route_ids, route_gates, expert_gate, expert_up, expert_down,
):
    z = lax.axis_index("z")
    c = lax.axis_index("c")
    latent_dim = value_proj.shape[1]
    quarter = residual.shape[1]

    zs = z.astype(jnp.int32).reshape(1)

    def pick(w, k, axis):
        return lax.dynamic_slice_in_dim(w, lax.rem(z + k, NZ) * quarter, quarter, axis)

    def cut(w, axis, which):
        return {k: pick(w, NZ - k, axis) for k in which}

    def tied(value, *groups):
        flat = [group[k] for group in groups for k in group]
        value, *flat = lax.optimization_barrier((value, *flat))
        at = iter(flat)
        return (value, *[{k: next(at) for k in group} for group in groups])

    def fetch(group):
        return {k: zsend(group[k], NZ - k) for k in group}

    only = lambda group, *which: {k: group[k] for k in which}
    picks = jnp.concatenate([route_ids.astype(F32), route_gates], axis=1)
    picks = jnp.concatenate([picks, swap_core(picks)], axis=0)
    picks = jnp.concatenate([picks, jnp.broadcast_to(c.astype(F32), (picks.shape[0], 1))], axis=1)
    hots, combs = route(picks, route_ids.shape[1])

    latents = attend(lengths, c.astype(jnp.int32).reshape(1), queries, kv_cache, new_latent, latent_dim)
    moved = lax.all_to_all(latents.reshape(16, 32, -1), YX, 0, 0, tiled=True)
    moved, down_cut = tied(moved, cut(expert_down[0], 1, (1, 2, 3)))
    got = swap_core(moved[:, 16:].reshape(256, -1))
    rows = zgather(head_values(moved.reshape(512, -1), got, value_proj))
    rows, down_cut = tied(rows, down_cut)
    down_a = fetch(only(down_cut, 1, 3))
    other = plane_dot(out_proj_kernel, zs, rows, out_proj, 1)
    parts = plane_scatter(plane_dot(out_proj_kernel, zs, rows, out_proj, 0), other)
    parts, down_a, down_cut = tied(parts, down_a, only(down_cut, 2))
    first, spread = first_sum(parts, residual)
    own = lax.all_to_all(spread, YX, 0, 0, tiled=True).reshape(256, -1)
    other = swap_core(own)
    width = dense_gate.shape[1]

    def activate(summed):
        scale = lax.rsqrt((summed[:, 2 * width] + summed[:, 2 * width + 1]) / D + EPS)[:, None]
        gate_act = summed[:, :width] * scale
        return (jax.nn.silu(gate_act) * (summed[:, width : 2 * width] * scale)).astype(BF)

    blocks_own = dense_in(zs, own, gain_first, dense_gate, dense_up, "dense_in_own")
    other, blocks_own = lax.optimization_barrier((other, blocks_own))
    blocks_other = dense_in(zs, other, gain_first, dense_gate, dense_up, "dense_in_other")
    hidden_own = activate(zscatter(blocks_own))
    summed, hidden_own = lax.optimization_barrier((zscatter(blocks_other), hidden_own))
    hidden_other = activate(summed)
    hidden_own, hidden_other = zgather(hidden_own), zgather(hidden_other)
    mine = plane_dot(dense_out_kernel, zs, hidden_own, dense_down, 0)
    mine, hidden_other = lax.optimization_barrier((mine, hidden_other))
    hidden_other, down_cut = tied(hidden_other, down_cut)
    down_b = fetch(down_cut)
    parts = plane_scatter(mine, plane_dot(dense_out_kernel, zs, hidden_other, dense_down, 1))
    parts, down_b = tied(parts, down_b)
    second, scaled = second_sum(parts, first, gain_second)

    scaled = jnp.concatenate([scaled, swap_core(scaled)], axis=0)
    far = zsend(scaled, 2)
    spread = lambda rows: lax.all_to_all(rows.reshape(16, 8, -1), YX, 0, 0, tiled=True).reshape(128, -1)
    near = spread(pack(scaled, hots, quarter))
    near, far = lax.optimization_barrier((near, far))
    ahead, behind = zsend(near, NZ - 1), zsend(near, 1)
    far = spread(pack(far, hots, quarter))
    expert_hidden = expert_in(zs, [near, ahead, far, behind], expert_gate[0], expert_up[0])
    result = expert_out(zs, zgather(expert_hidden), expert_down[0], [down_a[1], down_b[2], down_a[3]])
    returned = lax.all_to_all(result.reshape(16, 8, -1), YX, 0, 0, tiled=True).reshape(128, -1)
    total, theirs = combine(returned, combs, second)
    return (total + swap_core(theirs)).astype(BF)


def solution(mesh):
    grid = Mesh(mesh.devices.reshape(4, 4, 2, 4), ("y", "x", "c", "z"))
    ep = ("y", "x", "c")
    both = ("y", "x", "c", "z")
    return jax.shard_map(
        shards,
        mesh=grid,
        in_specs=(
            P(both, None, None),
            P(both, None, None),
            P(both, None),
            P(both),
            P(ep, "z"),
            P("z"),
            P("z"),
            P(ep, None, None),
            P(ep, "z"),
            P("z", ep),
            P("z", ep),
            P(ep, "z"),
            P(ep, None),
            P(ep, None),
            P(ep, None, "z"),
            P(ep, None, "z"),
            P(ep, "z", None),
        ),
        out_specs=P(ep, "z"),
        check_vma=False,
    )
```

```python
import jax
import jax.numpy as jnp
from jax import lax
from jax.experimental import pallas as pl
from jax.experimental.pallas import tpu as pltpu
from jax.sharding import Mesh, PartitionSpec as P

D = 7168
ROPE = 64
VD = 128
EPS = 1e-06
YX = ("y", "x")
NZ = 4
BF = jnp.bfloat16
F32 = jnp.float32


def zsend(values, shift):
    return lax.ppermute(values, "z", [(i, (i + shift) % NZ) for i in range(NZ)])


def swap_core(values):
    return lax.ppermute(values, "c", [(0, 1), (1, 0)])


def zgather(values):
    return [values] + [zsend(values, NZ - k) for k in (1, 2, 3)]


def zscatter(blocks):
    got = [zsend(blocks[k], k) for k in (1, 2, 3)]
    total = blocks[0].astype(F32)
    for piece in got:
        total = total + piece.astype(F32)
    return total


def plane_scatter(rows):
    return lax.all_to_all(rows.reshape(16, 16, -1), YX, 0, 0, tiled=True)


def onehot(hit):
    return jnp.where(hit, 1.0, 0.0).astype(BF)


def grid_of(shape):
    return lax.broadcasted_iota(jnp.int32, shape, 0), lax.broadcasted_iota(jnp.int32, shape, 1)


def exact(a, b):
    return jnp.dot(a, b, preferred_element_type=F32).astype(BF)


def attend_kernel(len_ref, c_ref, q_ref, kv_ref, new_ref, out, latents):
    step = pl.program_id(0)
    lat = latents.shape[2]
    new = new_ref[...].astype(F32)
    score_scale = (VD + ROPE) ** (-0.5)
    down = (((0,), (0,)), ((), ()))
    for i in range(q_ref.shape[0]):
        r = step * q_ref.shape[0] + i
        q = q_ref[i]
        fresh = jnp.sum(jnp.where(lax.broadcasted_iota(jnp.int32, new.shape, 0) == r, new, 0.0), axis=0, keepdims=True)
        scores = lax.dot_general(q, kv_ref[i], down, preferred_element_type=F32) * score_scale
        own = lax.dot_general(q, new_ref[...], (((0,), (1,)), ((), ())), preferred_element_type=F32)
        own = jnp.where(lax.broadcasted_iota(jnp.int32, own.shape, 1) == r, own, 0.0)
        self_score = jnp.sum(own, axis=1, keepdims=True) * score_scale
        live = lax.broadcasted_iota(jnp.int32, (1, scores.shape[1]), 1) < len_ref[r]
        scores = jnp.where(live, scores, -jnp.inf)
        top = jnp.maximum(jnp.max(scores, axis=1, keepdims=True), self_score)
        expo = jnp.exp(scores - top)
        self_expo = jnp.exp(self_score - top)
        total = 1.0 / (jnp.sum(expo, axis=1, keepdims=True) + self_expo)
        weights = (expo * total).astype(BF)
        self_weight = (self_expo * total).astype(BF).astype(F32)
        latent = lax.dot_general(weights, kv_ref[i, :lat, :], (((1,), (1,)), ((), ())), preferred_element_type=F32)
        latents[r] = (latent + self_weight * fresh[:, :lat]).astype(BF)

    @pl.when(step == pl.num_programs(0) - 1)
    def _():
        rows = out.shape[0]
        heads = rows // latents.shape[0]
        held = latents[...].reshape(rows, lat)
        part = rows // 2
        for i in range(2):
            row, col = grid_of((part, rows))
            row = row + i * part
            core = jnp.where((row & 16) == 0, c_ref[0], 1 - c_ref[0])
            order = onehot(col == ((row >> 2) & 3) * heads + (row >> 5) * 8 + core * 4 + (row & 3))
            out[i * part : (i + 1) * part, :] = exact(order, held)


def attend(lengths, c, queries, kv_cache, new_latent, lat):
    reqs, heads, width = queries.shape
    slots = kv_cache.shape[1]
    rows = reqs * heads
    return pl.pallas_call(
        attend_kernel,
        grid_spec=pltpu.PrefetchScalarGridSpec(
            num_scalar_prefetch=2,
            grid=(reqs // 2,),
            in_specs=[
                pl.BlockSpec((2, width, heads), lambda r, n, c: (r, 0, 0)),
                pl.BlockSpec((2, width, slots), lambda r, n, c: (r, 0, 0)),
                pl.BlockSpec((reqs, width), lambda r, n, c: (0, 0)),
            ],
            out_specs=pl.BlockSpec((rows, lat), lambda r, n, c: (0, 0)),
            scratch_shapes=[pltpu.VMEM((reqs, heads, lat), BF)],
        ),
        out_shape=jax.ShapeDtypeStruct((rows, lat), BF),
        compiler_params=params(60),
        cost_estimate=pl.CostEstimate(flops=4 * reqs * heads * slots * width, bytes_accessed=2 * reqs * slots * width, transcendentals=reqs * heads * slots),
        name="attend",
    )(lengths, c, queries.transpose(0, 2, 1), kv_cache.transpose(0, 2, 1), new_latent)


def heads_kernel(x, own, got, out):
    rows = x.shape[0]
    row, col = grid_of((rows, rows))
    head, chip, r = row >> 6, (row >> 2) & 15, row & 3
    latent = exact(onehot(col == chip * 32 + (head >> 2) * 16 + r * 4 + (head & 3)), x[...])
    part, width = out.shape[0], own.shape[2]
    for head in range(2 * own.shape[0]):
        values = (own, got)[head // own.shape[0]]
        value = jnp.dot(latent[head * part : (head + 1) * part], values[head % own.shape[0]], preferred_element_type=F32)
        out[:, head * width : (head + 1) * width] = value.astype(BF)


def head_values(x, own, got):
    count, lat, width = own.shape
    rows = x.shape[0] // count // 2
    return pl.pallas_call(
        heads_kernel,
        out_shape=jax.ShapeDtypeStruct((rows, 2 * count * width), BF),
        compiler_params=pltpu.CompilerParams(vmem_limit_bytes=16 * 1024 * 1024),
        cost_estimate=pl.CostEstimate(flops=2 * x.shape[0] * lat * (width + x.shape[0]), bytes_accessed=4 * count * lat * width, transcendentals=0),
        name="head_values",
    )(x, own, got)


def first_kernel(parts, residual, first, wide):
    total = residual[...].astype(F32)
    for i in range(parts.shape[0]):
        total = total + parts[i].astype(F32)
    first[...] = total
    for i in range(parts.shape[0]):
        wide[i] = total.astype(BF)


def first_sum(parts, residual):
    return pl.pallas_call(
        first_kernel,
        out_shape=[jax.ShapeDtypeStruct(residual.shape, F32), jax.ShapeDtypeStruct(parts.shape, BF)],
        compiler_params=pltpu.CompilerParams(vmem_limit_bytes=16 * 1024 * 1024),
        cost_estimate=pl.CostEstimate(flops=parts.size, bytes_accessed=200 * parts.size, transcendentals=0),
        name="first_sum",
    )(parts, residual)


def second_kernel(parts, first, gain, second, scaled):
    total = first[...]
    for i in range(parts.shape[0]):
        total = total + parts[i].astype(F32)
    second[...] = total
    width = total.shape[1]
    scaled[:, :width] = (total * gain[...].astype(F32)).astype(BF)
    square = total * total
    lanes = square[:, :128]
    for j in range(1, width // 128):
        lanes = lanes + square[:, j * 128 : (j + 1) * 128]
    scaled[:, width:] = tail_of(lanes)


def second_sum(parts, first, gain):
    rows, width = first.shape
    return pl.pallas_call(
        second_kernel,
        out_shape=[jax.ShapeDtypeStruct(first.shape, F32), jax.ShapeDtypeStruct((rows, width + 128), BF)],
        compiler_params=pltpu.CompilerParams(vmem_limit_bytes=16 * 1024 * 1024),
        cost_estimate=pl.CostEstimate(flops=parts.size, bytes_accessed=2 * parts.size, transcendentals=0),
        name="second_sum",
    )(parts, first, gain)


def route_kernel(picks, hots, combs, *, top):
    count = picks.shape[0]
    experts = 32
    ids, gates = picks[:, :top], picks[:, top : 2 * top]
    core = picks[:1, 2 * top : 2 * top + 1]
    expert = lax.broadcasted_iota(jnp.int32, (count, experts), 1).astype(F32)
    named = jnp.zeros((count, experts), F32)
    gate = jnp.zeros((count, experts), F32)
    for k in range(top):
        hit = ids[:, k : k + 1] == expert
        named = named + jnp.where(hit, 1.0, 0.0)
        gate = gate + jnp.where(hit, gates[:, k : k + 1], 0.0)
    row, col = grid_of((count, count))
    earlier = onehot((col < row) & ((col >> 4) == (row >> 4)))
    place = jnp.dot(earlier, named.astype(BF), preferred_element_type=F32)
    token = lax.broadcasted_iota(jnp.int32, (count, experts), 0)
    place = place + jnp.where(token >= 16, 6.0, 0.0)
    place = jnp.where(named > 0.5, place, 100.0)
    across = lambda rows, chip_of, values: lax.dot_general(
        onehot(grid_of((rows, experts))[1].astype(F32) == chip_of(grid_of((rows, experts))[0]).astype(F32) * 2.0 + core),
        values.astype(BF),
        (((1,), (1,)), ((), ())),
        preferred_element_type=F32,
    )
    rows = combs.shape[2]
    at = across(rows, lambda r: r >> 3, place)
    p = lax.broadcasted_iota(jnp.int32, (rows, 1), 0) & 7
    hots[0] = onehot(at == p.astype(F32))
    hots[1] = onehot(at == (8 + (p >> 1)).astype(F32))
    high = gate.astype(BF)
    for j, part in enumerate((high, gate - high.astype(F32))):
        value = across(rows, lambda r: r >> 3, part)
        for m in range(3):
            want = p if m == 0 else jnp.where((p & 1) == m - 1, 8 + (p >> 1), -1)
            combs[j, m] = jnp.where(at == want.astype(F32), value, 0.0).astype(BF)


def route(picks, top):
    count = picks.shape[0]
    return pl.pallas_call(
        lambda *refs: route_kernel(*refs, top=top),
        out_shape=[jax.ShapeDtypeStruct((2, 128, count), BF), jax.ShapeDtypeStruct((2, 3, 128, count), BF)],
        compiler_params=pltpu.CompilerParams(vmem_limit_bytes=16 * 1024 * 1024),
        cost_estimate=pl.CostEstimate(flops=1 << 22, bytes_accessed=1 << 18, transcendentals=0),
        name="route",
    )(picks)


def combine_kernel(returned, combs, second, own, other):
    width = own.shape[1]
    half = width // 2
    sums = []
    for m in range(3):
        x = returned[:, :width] if m == 0 else returned[:, width:]
        sums.append(
            sum(lax.dot_general(combs[j, m], x, (((0,), (0,)), ((), ())), preferred_element_type=F32) for j in range(2))
        )
    rows = own.shape[0]
    for m in range(2):
        lanes = slice(m * half, (m + 1) * half)
        total = sums[0][:, lanes] + sums[1 + m]
        own[:, lanes] = second[:, lanes] + total[:rows]
        other[:, lanes] = total[rows:]


def combine(returned, combs, second):
    return pl.pallas_call(
        combine_kernel,
        out_shape=[jax.ShapeDtypeStruct(second.shape, F32)] * 2,
        compiler_params=pltpu.CompilerParams(vmem_limit_bytes=16 * 1024 * 1024),
        cost_estimate=pl.CostEstimate(flops=12 * 32 * 128 * 1792, bytes_accessed=1 << 20, transcendentals=0),
        name="combine",
    )(returned, combs, second)


def pack_kernel(x, hots, out, *, width):
    half = width // 2
    rows = out.shape[0]
    head = exact(hots[0], x[...])
    tail = exact(hots[1], x[...])
    out[:, :width] = head[:, :width]
    even = (lax.broadcasted_iota(jnp.int32, (rows, half), 0) & 1) == 0
    out[:, width : width + half] = jnp.where(even, tail[:, :half], tail[:, half:width])
    lane = lax.broadcasted_iota(jnp.int32, (rows, 128), 1)
    out[:, width + half :] = jnp.where(lane < 2, head[:, width:], tail[:, width:])


def pack(x, hots, width):
    rows = hots.shape[1]
    return pl.pallas_call(
        lambda *refs: pack_kernel(*refs, width=width),
        out_shape=jax.ShapeDtypeStruct((rows, width * 3 // 2 + 128), BF),
        compiler_params=pltpu.CompilerParams(vmem_limit_bytes=16 * 1024 * 1024),
        cost_estimate=pl.CostEstimate(flops=4 * rows * width * 32, bytes_accessed=3 * rows * width, transcendentals=0),
        name="pack",
    )(x, hots)


def params(mib=16):
    return pltpu.CompilerParams(dimension_semantics=("arbitrary",), vmem_limit_bytes=mib * 1024 * 1024)


def tail_of(squares):
    total = jnp.sum(squares, axis=1, keepdims=True)
    hi = total.astype(BF).astype(F32)
    lane = lax.broadcasted_iota(jnp.int32, (total.shape[0], 128), 1)
    return jnp.where(lane < 4, jnp.where((lane & 1) == 0, hi, total - hi), 0.0).astype(BF)


def dense_in_kernel(z_ref, x, gain, gate, gate_got, up, up_got, o0, o1, o2, o3, acc, squares, tail):
    step = pl.program_id(0)
    width = gate.shape[1]

    @pl.when(step == 0)
    def _():
        acc[...] = jnp.zeros_like(acc)
        squares[...] = jnp.zeros_like(squares)

    value = x[...].astype(F32)
    normed = (value * gain[...].astype(F32)).astype(BF)
    for j, weight in enumerate((gate, gate_got, up, up_got)):
        acc[:, j * width : (j + 1) * width] += jnp.dot(normed, weight[...], preferred_element_type=F32)
    square = value * value
    for j in range(square.shape[1] // 128):
        squares[...] += square[:, j * 128 : (j + 1) * 128]

    @pl.when(step == pl.num_programs(0) - 1)
    def _():
        z = z_ref[0]
        tail[...] = tail_of(squares[...])
        part = acc.shape[0] // NZ
        for k, out in enumerate((o0, o1, o2, o3)):
            at = pl.ds(pl.multiple_of(lax.rem(z + k, NZ) * part, part), part)
            out[:, : 4 * width] = acc[at, :].astype(BF)
            out[:, 4 * width :] = tail[at, :]


def dense_in(z, x, gain, weights):
    depth, width = weights[0].shape
    step = depth // 2
    rows = x.shape[0]
    lanes = 4 * width + 128
    return pl.pallas_call(
        dense_in_kernel,
        grid_spec=pltpu.PrefetchScalarGridSpec(
            num_scalar_prefetch=1,
            grid=(depth // step,),
            in_specs=[
                pl.BlockSpec((rows, step), lambda i, z: (0, i)),
                pl.BlockSpec((1, step), lambda i, z: (0, i)),
            ]
            + [pl.BlockSpec((step, width), lambda i, z: (i, 0))] * 4,
            out_specs=[pl.BlockSpec((rows // NZ, lanes), lambda i, z: (0, 0))] * NZ,
            scratch_shapes=[
                pltpu.VMEM((rows, 4 * width), F32),
                pltpu.VMEM((rows, 128), F32),
                pltpu.VMEM((rows, 128), BF),
            ],
        ),
        out_shape=[jax.ShapeDtypeStruct((rows // NZ, lanes), BF)] * NZ,
        compiler_params=params(),
        cost_estimate=pl.CostEstimate(flops=8 * rows * depth * width, bytes_accessed=2 * depth * (rows + 4 * width), transcendentals=0),
        name="dense_in",
    )(z, x, gain, *weights)


def silu(value):
    return value / (1.0 + jnp.exp(-value))


def expert_in_kernel(z_ref, *refs):
    heads, tails, sums, gates, ups = (refs[4 * j : 4 * j + 4] for j in range(5))
    out, gate_acc, up_acc = refs[20:]
    step = pl.program_id(0)

    @pl.when(step == 0)
    def _():
        gate_acc[...] = jnp.zeros_like(gate_acc)
        up_acc[...] = jnp.zeros_like(up_acc)

    rows = heads[0].shape[0]
    row, col = grid_of((rows // 2, rows))
    pick = onehot(col == 2 * row + step)
    for m in range(NZ):
        x = jnp.concatenate([heads[m][...], exact(pick, tails[m][...])], axis=0)
        gate_acc[...] += jnp.dot(x, gates[m][...], preferred_element_type=F32)
        up_acc[...] += jnp.dot(x, ups[m][...], preferred_element_type=F32)

    @pl.when(step == pl.num_programs(0) - 1)
    def _():
        lane = lax.broadcasted_iota(jnp.int32, (1, 128), 1)
        total = None
        for ref in sums:
            square = jnp.concatenate(
                [
                    jnp.where(lane < 2, ref[...].astype(F32), 0.0),
                    jnp.where((lane >= 2) & (lane < 4), jnp.dot(pick, ref[...], preferred_element_type=F32), 0.0),
                ],
                axis=0,
            )
            total = square if total is None else total + square
        scale = lax.rsqrt(jnp.sum(total, axis=1, keepdims=True) / D + EPS)
        out[...] = (silu(gate_acc[...] * scale) * (up_acc[...] * scale)).astype(BF)


def expert_in(z, xs, gate, up):
    depth, width = gate.shape
    steps = 2
    step = depth // NZ // steps
    rows = xs[0].shape[0]
    heads = [pl.BlockSpec((rows, step), lambda i, z: (0, i))] * NZ
    tails = [pl.BlockSpec((rows, step), lambda i, z: (0, 2))] * NZ
    sums = [pl.BlockSpec((rows, 128), lambda i, z: (0, 3 * step // 128))] * NZ
    ws = [pl.BlockSpec((step, width), lambda i, z, m=m: (lax.rem(z[0] + m, NZ) * steps + i, 0)) for m in range(NZ)]
    total = rows * 3 // 2
    return pl.pallas_call(
        expert_in_kernel,
        grid_spec=pltpu.PrefetchScalarGridSpec(
            num_scalar_prefetch=1,
            grid=(steps,),
            in_specs=heads + tails + sums + ws + ws,
            out_specs=pl.BlockSpec((total, width), lambda i, z: (0, 0)),
            scratch_shapes=[pltpu.VMEM((total, width), F32)] * 2,
        ),
        out_shape=jax.ShapeDtypeStruct((total, width), BF),
        compiler_params=params(),
        cost_estimate=pl.CostEstimate(flops=4 * total * depth * width, bytes_accessed=4 * depth * width, transcendentals=0),
        name="expert_in",
    )(z, *xs, *xs, *xs, *[gate] * 4, *[up] * 4)


def expert_out_kernel(z_ref, *refs):
    hidden, weights, out, wide = refs[:4], refs[4:8], refs[8], refs[9]
    step = pl.program_id(0)
    rows = out.shape[0]

    @pl.when(step == 0)
    def _():
        row, col = grid_of((rows, rows // 2))
        order = onehot(col == row >> 1)
        for k in range(NZ):
            wide[k, :rows] = hidden[k][:rows]
            wide[k, rows:] = exact(order, hidden[k][rows:])

    half = weights[0].shape[1]
    for n in range(0, half, 256):
        tile = min(256, half - n)
        total = None
        for k in range(NZ):
            term = jnp.dot(wide[k], weights[k][:, n : n + tile], preferred_element_type=F32)
            total = term if total is None else total + term
        total = total.astype(BF)
        out[:, pl.ds(pl.multiple_of(step * half + n, 128), tile)] = total[:rows]
        lanes = slice(2 * half + n, 2 * half + n + tile)
        mine = (lax.broadcasted_iota(jnp.int32, (rows, tile), 0) & 1) == step
        out[:, lanes] = jnp.where(mine, total[rows:], out[:, lanes])


def expert_out(z, hidden, down, got):
    rows, width = hidden[0].shape
    columns = got[0].shape[1]
    steps = 2
    step = columns // steps
    whole = (rows // 12 * 8, columns + step)
    return pl.pallas_call(
        expert_out_kernel,
        grid_spec=pltpu.PrefetchScalarGridSpec(
            num_scalar_prefetch=1,
            grid=(steps,),
            in_specs=[pl.BlockSpec((rows, width), lambda i, z: (0, 0))] * NZ
            + [pl.BlockSpec((width, step), lambda i, z: (0, z[0] * steps + i))]
            + [pl.BlockSpec((width, step), lambda i, z: (0, i))] * 3,
            out_specs=pl.BlockSpec(whole, lambda i, z: (0, 0)),
            scratch_shapes=[pltpu.VMEM((NZ, 2 * whole[0], width), BF)],
        ),
        out_shape=jax.ShapeDtypeStruct(whole, BF),
        compiler_params=params(),
        cost_estimate=pl.CostEstimate(flops=16 * whole[0] * width * columns, bytes_accessed=8 * width * columns, transcendentals=0),
        name="expert_out",
    )(z, *hidden, down, *got)


def two_dots(rows, own, got, out):
    depth = own.shape[0]
    total = jnp.dot(rows[:, :depth], own[...], preferred_element_type=F32)
    total = total + jnp.dot(rows[:, depth:], got[...], preferred_element_type=F32)
    out[...] = total.astype(BF)


def dense_out_kernel(z_ref, h0, h1, h2, h3, own, got, out, held):
    @pl.when(pl.program_id(0) == 0)
    def _():
        z = z_ref[0]
        for k, ref in enumerate((h0, h1, h2, h3)):
            at = pl.multiple_of(lax.rem(z + k, NZ) * 64, 64)
            held[pl.ds(at, 64), :] = ref[...]

    two_dots(held, own, got, out)


def out_proj_kernel(z_ref, h0, h1, h2, h3, own, got, out, held):
    @pl.when(pl.program_id(0) == 0)
    def _():
        z = z_ref[0]
        row, col = grid_of((held.shape[0], h0.shape[0]))
        match = col == (row >> 4) * 4 + (row & 3)
        total = None
        for k, ref in enumerate((h0, h1, h2, h3)):
            hit = match & (((row >> 2) & 3) == lax.rem(z + k, NZ))
            term = jnp.dot(onehot(hit), ref[...], preferred_element_type=F32)
            total = term if total is None else total + term
        held[...] = total.astype(BF)

    two_dots(held, own, got, out)


def plane_dot(kernel, z, blocks, own, got, name):
    depth, columns = own.shape
    step = columns // 2
    weight = pl.BlockSpec((depth, step), lambda i, z: (0, i))
    return pl.pallas_call(
        kernel,
        grid_spec=pltpu.PrefetchScalarGridSpec(
            num_scalar_prefetch=1,
            grid=(columns // step,),
            in_specs=[pl.BlockSpec(blocks[0].shape, lambda i, z: (0, 0))] * NZ + [weight, weight],
            out_specs=pl.BlockSpec((256, step), lambda i, z: (0, i)),
            scratch_shapes=[pltpu.VMEM((256, 2 * depth), BF)],
        ),
        out_shape=jax.ShapeDtypeStruct((256, columns), BF),
        compiler_params=params(),
        cost_estimate=pl.CostEstimate(flops=1024 * depth * columns, bytes_accessed=4 * depth * columns, transcendentals=0),
        name=name,
    )(z, *blocks, own, got)


def shards(
    queries, kv_cache, new_latent, lengths, residual, gain_first, gain_second, value_proj, out_proj,
    dense_gate, dense_up, dense_down, route_ids, route_gates, expert_gate, expert_up, expert_down,
):
    z = lax.axis_index("z")
    c = lax.axis_index("c")
    latent_dim = value_proj.shape[1]
    quarter = residual.shape[1]

    zs = z.astype(jnp.int32).reshape(1)

    def pick(w, k, axis):
        return lax.dynamic_slice_in_dim(w, lax.rem(z + k, NZ) * quarter, quarter, axis)

    def cut(w, axis, which):
        return {k: pick(w, NZ - k, axis) for k in which}

    def tied(value, *groups):
        flat = [group[k] for group in groups for k in group]
        value, *flat = lax.optimization_barrier((value, *flat))
        at = iter(flat)
        return (value, *[{k: next(at) for k in group} for group in groups])

    def fetch(group):
        return {k: zsend(group[k], NZ - k) for k in group}

    only = lambda group, *which: {k: group[k] for k in which}
    picks = jnp.concatenate([route_ids.astype(F32), route_gates], axis=1)
    picks = jnp.concatenate([picks, swap_core(picks)], axis=0)
    picks = jnp.concatenate([picks, jnp.broadcast_to(c.astype(F32), (picks.shape[0], 1))], axis=1)
    hots, combs = route(picks, route_ids.shape[1])
    gain_a, gain_b = gain_first.reshape(1, -1), gain_second.reshape(1, -1)

    latents = attend(lengths, c.astype(jnp.int32).reshape(1), queries, kv_cache, new_latent, latent_dim)
    moved = lax.all_to_all(latents.reshape(16, 32, -1), YX, 0, 0, tiled=True)
    moved, value_got = lax.optimization_barrier((moved, swap_core(value_proj)))
    moved, gain_a, gain_b, hots, combs = lax.optimization_barrier((moved, gain_a, gain_b, hots, combs))
    moved, down_cut = tied(moved, cut(expert_down[0], 1, (1, 2, 3)))
    moved, mine = lax.optimization_barrier((moved, out_proj))
    out_got = swap_core(mine)
    rows = zgather(head_values(moved.reshape(512, -1), value_proj, value_got))
    rows, out_got, *mine = lax.optimization_barrier((rows, out_got, dense_gate, dense_up, dense_down))
    dense_got = [swap_core(weight) for weight in mine]
    rows, down_cut = tied(rows, down_cut)
    down_a = fetch(only(down_cut, 1, 3))
    parts = plane_scatter(plane_dot(out_proj_kernel, zs, rows, out_proj, out_got, "out_proj"))
    parts, down_a, down_cut = tied(parts, down_a, only(down_cut, 2))
    parts, *dense_got = lax.optimization_barrier((parts, *dense_got))
    first, spread = first_sum(parts, residual)
    own = lax.all_to_all(spread, YX, 0, 0, tiled=True).reshape(256, -1)
    width = 2 * dense_gate.shape[1]

    def activate(summed):
        scale = lax.rsqrt((summed[:, 2 * width] + summed[:, 2 * width + 1]) / D + EPS)[:, None]
        gate_act = summed[:, :width] * scale
        return (jax.nn.silu(gate_act) * (summed[:, width : 2 * width] * scale)).astype(BF)

    blocks = dense_in(zs, own, gain_a, [dense_gate, dense_got[0], dense_up, dense_got[1]])
    hidden = zgather(activate(zscatter(blocks)))
    hidden, down_cut = tied(hidden, down_cut)
    down_b = fetch(down_cut)
    parts = plane_scatter(plane_dot(dense_out_kernel, zs, hidden, dense_down, dense_got[2], "dense_out"))
    parts, down_b = tied(parts, down_b)
    second, scaled = second_sum(parts, first, gain_b)

    scaled = jnp.concatenate([scaled, swap_core(scaled)], axis=0)
    far = zsend(scaled, 2)
    spread = lambda rows: lax.all_to_all(rows.reshape(16, 8, -1), YX, 0, 0, tiled=True).reshape(128, -1)
    near = spread(pack(scaled, hots, quarter))
    near, far = lax.optimization_barrier((near, far))
    ahead, behind = zsend(near, NZ - 1), zsend(near, 1)
    far = spread(pack(far, hots, quarter))
    expert_hidden = expert_in(zs, [near, ahead, far, behind], expert_gate[0], expert_up[0])
    result = expert_out(zs, zgather(expert_hidden), expert_down[0], [down_a[1], down_b[2], down_a[3]])
    returned = lax.all_to_all(result.reshape(16, 8, -1), YX, 0, 0, tiled=True).reshape(128, -1)
    total, theirs = combine(returned, combs, second)
    return (total + swap_core(theirs)).astype(BF)


def solution(mesh):
    grid = Mesh(mesh.devices.reshape(4, 4, 2, 4), ("y", "x", "c", "z"))
    ep = ("y", "x", "c")
    both = ("y", "x", "c", "z")
    return jax.shard_map(
        shards,
        mesh=grid,
        in_specs=(
            P(both, None, None),
            P(both, None, None),
            P(both, None),
            P(both),
            P(ep, "z"),
            P("z"),
            P("z"),
            P(ep, None, None),
            P(ep, "z"),
            P("z", ep),
            P("z", ep),
            P(ep, "z"),
            P(ep, None),
            P(ep, None),
            P(ep, None, "z"),
            P(ep, None, "z"),
            P(ep, "z", None),
        ),
        out_specs=P(ep, "z"),
        check_vma=False,
    )
```

```python
import jax
import jax.numpy as jnp
from jax import lax
from jax.experimental import pallas as pl
from jax.experimental.pallas import tpu as pltpu
from jax.sharding import Mesh, PartitionSpec as P

D = 7168
ROPE = 64
VD = 128
EPS = 1e-06
YX = ("y", "x")
NZ = 4
BF = jnp.bfloat16
F32 = jnp.float32


def zsend(values, shift):
    return lax.ppermute(values, "z", [(i, (i + shift) % NZ) for i in range(NZ)])


def swap_core(values):
    return lax.ppermute(values, "c", [(0, 1), (1, 0)])


def zgather(values):
    return [values] + [zsend(values, NZ - k) for k in (1, 2, 3)]


def zscatter(blocks):
    got = [zsend(blocks[k], k) for k in (1, 2, 3)]
    total = blocks[0].astype(F32)
    for piece in got:
        total = total + piece.astype(F32)
    return total


def plane_scatter(rows):
    return lax.all_to_all(rows.reshape(16, 16, -1), YX, 0, 0, tiled=True)


def onehot(hit):
    return jnp.where(hit, 1.0, 0.0).astype(BF)


def grid_of(shape):
    return lax.broadcasted_iota(jnp.int32, shape, 0), lax.broadcasted_iota(jnp.int32, shape, 1)


def exact(a, b):
    return jnp.dot(a, b, preferred_element_type=F32).astype(BF)


def attend_kernel(len_ref, c_ref, q_ref, kv_ref, new_ref, out, latents):
    step = pl.program_id(0)
    lat = latents.shape[2]
    new = new_ref[...].astype(F32)
    score_scale = (VD + ROPE) ** (-0.5)
    down = (((0,), (0,)), ((), ()))
    for i in range(q_ref.shape[0]):
        r = step * q_ref.shape[0] + i
        q = q_ref[i]
        fresh = jnp.sum(jnp.where(lax.broadcasted_iota(jnp.int32, new.shape, 0) == r, new, 0.0), axis=0, keepdims=True)
        scores = lax.dot_general(q, kv_ref[i], down, preferred_element_type=F32) * score_scale
        own = lax.dot_general(q, new_ref[...], (((0,), (1,)), ((), ())), preferred_element_type=F32)
        own = jnp.where(lax.broadcasted_iota(jnp.int32, own.shape, 1) == r, own, 0.0)
        self_score = jnp.sum(own, axis=1, keepdims=True) * score_scale
        live = lax.broadcasted_iota(jnp.int32, (1, scores.shape[1]), 1) < len_ref[r]
        scores = jnp.where(live, scores, -jnp.inf)
        top = jnp.maximum(jnp.max(scores, axis=1, keepdims=True), self_score)
        expo = jnp.exp(scores - top)
        self_expo = jnp.exp(self_score - top)
        total = 1.0 / (jnp.sum(expo, axis=1, keepdims=True) + self_expo)
        weights = (expo * total).astype(BF)
        self_weight = (self_expo * total).astype(BF).astype(F32)
        latent = lax.dot_general(weights, kv_ref[i, :lat, :], (((1,), (1,)), ((), ())), preferred_element_type=F32)
        latents[r] = (latent + self_weight * fresh[:, :lat]).astype(BF)

    @pl.when(step == pl.num_programs(0) - 1)
    def _():
        rows = out.shape[0]
        heads = rows // latents.shape[0]
        held = latents[...].reshape(rows, lat)
        part = rows // 2
        for i in range(2):
            row, col = grid_of((part, rows))
            row = row + i * part
            core = jnp.where((row & 16) == 0, c_ref[0], 1 - c_ref[0])
            order = onehot(col == ((row >> 2) & 3) * heads + (row >> 5) * 8 + core * 4 + (row & 3))
            out[i * part : (i + 1) * part, :] = exact(order, held)


def attend(lengths, c, queries, kv_cache, new_latent, lat):
    reqs, heads, width = queries.shape
    slots = kv_cache.shape[1]
    rows = reqs * heads
    return pl.pallas_call(
        attend_kernel,
        grid_spec=pltpu.PrefetchScalarGridSpec(
            num_scalar_prefetch=2,
            grid=(reqs // 2,),
            in_specs=[
                pl.BlockSpec((2, width, heads), lambda r, n, c: (r, 0, 0)),
                pl.BlockSpec((2, width, slots), lambda r, n, c: (r, 0, 0)),
                pl.BlockSpec((reqs, width), lambda r, n, c: (0, 0)),
            ],
            out_specs=pl.BlockSpec((rows, lat), lambda r, n, c: (0, 0)),
            scratch_shapes=[pltpu.VMEM((reqs, heads, lat), BF)],
        ),
        out_shape=jax.ShapeDtypeStruct((rows, lat), BF),
        compiler_params=params(60),
        cost_estimate=pl.CostEstimate(flops=4 * reqs * heads * slots * width, bytes_accessed=2 * reqs * slots * width, transcendentals=reqs * heads * slots),
        name="attend",
    )(lengths, c, queries.transpose(0, 2, 1), kv_cache.transpose(0, 2, 1), new_latent)


def heads_kernel(x, own, got, out):
    rows = x.shape[0]
    row, col = grid_of((rows, rows))
    head, chip, r = row >> 6, (row >> 2) & 15, row & 3
    latent = exact(onehot(col == chip * 32 + (head >> 2) * 16 + r * 4 + (head & 3)), x[...])
    part, width = out.shape[0], own.shape[2]
    for head in range(2 * own.shape[0]):
        values = (own, got)[head // own.shape[0]]
        value = jnp.dot(latent[head * part : (head + 1) * part], values[head % own.shape[0]], preferred_element_type=F32)
        out[:, head * width : (head + 1) * width] = value.astype(BF)


def head_values(x, own, got):
    count, lat, width = own.shape
    rows = x.shape[0] // count // 2
    return pl.pallas_call(
        heads_kernel,
        out_shape=jax.ShapeDtypeStruct((rows, 2 * count * width), BF),
        compiler_params=pltpu.CompilerParams(vmem_limit_bytes=16 * 1024 * 1024),
        cost_estimate=pl.CostEstimate(flops=2 * x.shape[0] * lat * (width + x.shape[0]), bytes_accessed=4 * count * lat * width, transcendentals=0),
        name="head_values",
    )(x, own, got)


def first_kernel(parts, residual, first, wide):
    total = residual[...].astype(F32)
    for i in range(parts.shape[0]):
        total = total + parts[i].astype(F32)
    first[...] = total
    for i in range(parts.shape[0]):
        wide[i] = total.astype(BF)


def first_sum(parts, residual):
    return pl.pallas_call(
        first_kernel,
        out_shape=[jax.ShapeDtypeStruct(residual.shape, F32), jax.ShapeDtypeStruct(parts.shape, BF)],
        compiler_params=pltpu.CompilerParams(vmem_limit_bytes=16 * 1024 * 1024),
        cost_estimate=pl.CostEstimate(flops=parts.size, bytes_accessed=200 * parts.size, transcendentals=0),
        name="first_sum",
    )(parts, residual)


def second_kernel(parts, first, gain, second, scaled):
    total = first[...]
    for i in range(parts.shape[0]):
        total = total + parts[i].astype(F32)
    second[...] = total
    width = total.shape[1]
    scaled[:, :width] = (total * gain[...].astype(F32)).astype(BF)
    square = total * total
    lanes = square[:, :128]
    for j in range(1, width // 128):
        lanes = lanes + square[:, j * 128 : (j + 1) * 128]
    scaled[:, width:] = tail_of(lanes)


def second_sum(parts, first, gain):
    rows, width = first.shape
    return pl.pallas_call(
        second_kernel,
        out_shape=[jax.ShapeDtypeStruct(first.shape, F32), jax.ShapeDtypeStruct((rows, width + 128), BF)],
        compiler_params=pltpu.CompilerParams(vmem_limit_bytes=16 * 1024 * 1024),
        cost_estimate=pl.CostEstimate(flops=parts.size, bytes_accessed=2 * parts.size, transcendentals=0),
        name="second_sum",
    )(parts, first, gain)


def route_kernel(picks, hots, combs, *, top):
    count = picks.shape[0]
    experts = 32
    ids, gates = picks[:, :top], picks[:, top : 2 * top]
    core = picks[:1, 2 * top : 2 * top + 1]
    expert = lax.broadcasted_iota(jnp.int32, (count, experts), 1).astype(F32)
    named = jnp.zeros((count, experts), F32)
    gate = jnp.zeros((count, experts), F32)
    for k in range(top):
        hit = ids[:, k : k + 1] == expert
        named = named + jnp.where(hit, 1.0, 0.0)
        gate = gate + jnp.where(hit, gates[:, k : k + 1], 0.0)
    row, col = grid_of((count, count))
    earlier = onehot((col < row) & ((col >> 4) == (row >> 4)))
    place = jnp.dot(earlier, named.astype(BF), preferred_element_type=F32)
    token = lax.broadcasted_iota(jnp.int32, (count, experts), 0)
    place = place + jnp.where(token >= 16, 6.0, 0.0)
    place = jnp.where(named > 0.5, place, 100.0)
    across = lambda rows, chip_of, values: lax.dot_general(
        onehot(grid_of((rows, experts))[1].astype(F32) == chip_of(grid_of((rows, experts))[0]).astype(F32) * 2.0 + core),
        values.astype(BF),
        (((1,), (1,)), ((), ())),
        preferred_element_type=F32,
    )
    rows = combs.shape[2]
    at = across(rows, lambda r: r >> 3, place)
    p = lax.broadcasted_iota(jnp.int32, (rows, 1), 0) & 7
    hots[0] = onehot(at == p.astype(F32))
    hots[1] = onehot(at == (8 + (p >> 1)).astype(F32))
    high = gate.astype(BF)
    for j, part in enumerate((high, gate - high.astype(F32))):
        value = across(rows, lambda r: r >> 3, part)
        for m in range(3):
            want = p if m == 0 else jnp.where((p & 1) == m - 1, 8 + (p >> 1), -1)
            combs[j, m] = jnp.where(at == want.astype(F32), value, 0.0).astype(BF)


def route(picks, top):
    count = picks.shape[0]
    return pl.pallas_call(
        lambda *refs: route_kernel(*refs, top=top),
        out_shape=[jax.ShapeDtypeStruct((2, 128, count), BF), jax.ShapeDtypeStruct((2, 3, 128, count), BF)],
        compiler_params=pltpu.CompilerParams(vmem_limit_bytes=16 * 1024 * 1024),
        cost_estimate=pl.CostEstimate(flops=1 << 22, bytes_accessed=1 << 18, transcendentals=0),
        name="route",
    )(picks)


def combine_kernel(returned, combs, second, own, other):
    width = own.shape[1]
    half = width // 2
    sums = []
    for m in range(3):
        x = returned[:, :width] if m == 0 else returned[:, width:]
        sums.append(
            sum(lax.dot_general(combs[j, m], x, (((0,), (0,)), ((), ())), preferred_element_type=F32) for j in range(2))
        )
    rows = own.shape[0]
    for m in range(2):
        lanes = slice(m * half, (m + 1) * half)
        total = sums[0][:, lanes] + sums[1 + m]
        own[:, lanes] = second[:, lanes] + total[:rows]
        other[:, lanes] = total[rows:]


def combine(returned, combs, second):
    return pl.pallas_call(
        combine_kernel,
        out_shape=[jax.ShapeDtypeStruct(second.shape, F32)] * 2,
        compiler_params=pltpu.CompilerParams(vmem_limit_bytes=16 * 1024 * 1024),
        cost_estimate=pl.CostEstimate(flops=12 * 32 * 128 * 1792, bytes_accessed=1 << 20, transcendentals=0),
        name="combine",
    )(returned, combs, second)


def pack_kernel(x, hots, out, *, width):
    half = width // 2
    rows = out.shape[0]
    head = exact(hots[0], x[...])
    tail = exact(hots[1], x[...])
    out[:, :width] = head[:, :width]
    even = (lax.broadcasted_iota(jnp.int32, (rows, half), 0) & 1) == 0
    out[:, width : width + half] = jnp.where(even, tail[:, :half], tail[:, half:width])
    lane = lax.broadcasted_iota(jnp.int32, (rows, 128), 1)
    out[:, width + half :] = jnp.where(lane < 2, head[:, width:], tail[:, width:])


def pack(x, hots, width):
    rows = hots.shape[1]
    return pl.pallas_call(
        lambda *refs: pack_kernel(*refs, width=width),
        out_shape=jax.ShapeDtypeStruct((rows, width * 3 // 2 + 128), BF),
        compiler_params=pltpu.CompilerParams(vmem_limit_bytes=16 * 1024 * 1024),
        cost_estimate=pl.CostEstimate(flops=4 * rows * width * 32, bytes_accessed=3 * rows * width, transcendentals=0),
        name="pack",
    )(x, hots)


def params(mib=16):
    return pltpu.CompilerParams(dimension_semantics=("arbitrary",), vmem_limit_bytes=mib * 1024 * 1024)


def tail_of(squares):
    total = jnp.sum(squares, axis=1, keepdims=True)
    hi = total.astype(BF).astype(F32)
    lane = lax.broadcasted_iota(jnp.int32, (total.shape[0], 128), 1)
    return jnp.where(lane < 4, jnp.where((lane & 1) == 0, hi, total - hi), 0.0).astype(BF)


def dense_in_kernel(z_ref, x, gain, gate, gate_got, up, up_got, o0, o1, o2, o3, acc, squares, tail):
    step = pl.program_id(0)
    width = gate.shape[1]

    @pl.when(step == 0)
    def _():
        acc[...] = jnp.zeros_like(acc)
        squares[...] = jnp.zeros_like(squares)

    value = x[...].astype(F32)
    normed = (value * gain[...].astype(F32)).astype(BF)
    for j, weight in enumerate((gate, gate_got, up, up_got)):
        acc[:, j * width : (j + 1) * width] += jnp.dot(normed, weight[...], preferred_element_type=F32)
    square = value * value
    for j in range(square.shape[1] // 128):
        squares[...] += square[:, j * 128 : (j + 1) * 128]

    @pl.when(step == pl.num_programs(0) - 1)
    def _():
        z = z_ref[0]
        tail[...] = tail_of(squares[...])
        part = acc.shape[0] // NZ
        for k, out in enumerate((o0, o1, o2, o3)):
            at = pl.ds(pl.multiple_of(lax.rem(z + k, NZ) * part, part), part)
            out[:, : 4 * width] = acc[at, :].astype(BF)
            out[:, 4 * width :] = tail[at, :]


def dense_in(z, x, gain, weights):
    depth, width = weights[0].shape
    step = depth // 2
    rows = x.shape[0]
    lanes = 4 * width + 128
    return pl.pallas_call(
        dense_in_kernel,
        grid_spec=pltpu.PrefetchScalarGridSpec(
            num_scalar_prefetch=1,
            grid=(depth // step,),
            in_specs=[
                pl.BlockSpec((rows, step), lambda i, z: (0, i)),
                pl.BlockSpec((1, step), lambda i, z: (0, i)),
            ]
            + [pl.BlockSpec((step, width), lambda i, z: (i, 0))] * 4,
            out_specs=[pl.BlockSpec((rows // NZ, lanes), lambda i, z: (0, 0))] * NZ,
            scratch_shapes=[
                pltpu.VMEM((rows, 4 * width), F32),
                pltpu.VMEM((rows, 128), F32),
                pltpu.VMEM((rows, 128), BF),
            ],
        ),
        out_shape=[jax.ShapeDtypeStruct((rows // NZ, lanes), BF)] * NZ,
        compiler_params=params(),
        cost_estimate=pl.CostEstimate(flops=8 * rows * depth * width, bytes_accessed=2 * depth * (rows + 4 * width), transcendentals=0),
        name="dense_in",
    )(z, x, gain, *weights)


def silu(value):
    return value / (1.0 + jnp.exp(-value))


def expert_in_kernel(z_ref, *refs):
    heads, tails, sums, gates, ups = (refs[4 * j : 4 * j + 4] for j in range(5))
    out, gate_acc, up_acc = refs[20:]
    step = pl.program_id(0)

    @pl.when(step == 0)
    def _():
        gate_acc[...] = jnp.zeros_like(gate_acc)
        up_acc[...] = jnp.zeros_like(up_acc)

    rows = heads[0].shape[0]
    row, col = grid_of((rows // 2, rows))
    pick = onehot(col == 2 * row + step)
    for m in range(NZ):
        x = jnp.concatenate([heads[m][...], exact(pick, tails[m][...])], axis=0)
        gate_acc[...] += jnp.dot(x, gates[m][...], preferred_element_type=F32)
        up_acc[...] += jnp.dot(x, ups[m][...], preferred_element_type=F32)

    @pl.when(step == pl.num_programs(0) - 1)
    def _():
        lane = lax.broadcasted_iota(jnp.int32, (1, 128), 1)
        total = None
        for ref in sums:
            square = jnp.concatenate(
                [
                    jnp.where(lane < 2, ref[...].astype(F32), 0.0),
                    jnp.where((lane >= 2) & (lane < 4), jnp.dot(pick, ref[...], preferred_element_type=F32), 0.0),
                ],
                axis=0,
            )
            total = square if total is None else total + square
        scale = lax.rsqrt(jnp.sum(total, axis=1, keepdims=True) / D + EPS)
        out[...] = (silu(gate_acc[...] * scale) * (up_acc[...] * scale)).astype(BF)


def expert_in(z, xs, gate, up):
    depth, width = gate.shape
    steps = 2
    step = depth // NZ // steps
    rows = xs[0].shape[0]
    heads = [pl.BlockSpec((rows, step), lambda i, z: (0, i))] * NZ
    tails = [pl.BlockSpec((rows, step), lambda i, z: (0, 2))] * NZ
    sums = [pl.BlockSpec((rows, 128), lambda i, z: (0, 3 * step // 128))] * NZ
    ws = [pl.BlockSpec((step, width), lambda i, z, m=m: (lax.rem(z[0] + m, NZ) * steps + i, 0)) for m in range(NZ)]
    total = rows * 3 // 2
    return pl.pallas_call(
        expert_in_kernel,
        grid_spec=pltpu.PrefetchScalarGridSpec(
            num_scalar_prefetch=1,
            grid=(steps,),
            in_specs=heads + tails + sums + ws + ws,
            out_specs=pl.BlockSpec((total, width), lambda i, z: (0, 0)),
            scratch_shapes=[pltpu.VMEM((total, width), F32)] * 2,
        ),
        out_shape=jax.ShapeDtypeStruct((total, width), BF),
        compiler_params=params(),
        cost_estimate=pl.CostEstimate(flops=4 * total * depth * width, bytes_accessed=4 * depth * width, transcendentals=0),
        name="expert_in",
    )(z, *xs, *xs, *xs, *[gate] * 4, *[up] * 4)


def expert_out_kernel(z_ref, *refs):
    hidden, weights, out, wide = refs[:4], refs[4:8], refs[8], refs[9]
    step = pl.program_id(0)
    rows = out.shape[0]

    @pl.when(step == 0)
    def _():
        row, col = grid_of((rows, rows // 2))
        order = onehot(col == row >> 1)
        for k in range(NZ):
            wide[k, :rows] = hidden[k][:rows]
            wide[k, rows:] = exact(order, hidden[k][rows:])

    half = weights[0].shape[1]
    for n in range(0, half, 256):
        tile = min(256, half - n)
        total = None
        for k in range(NZ):
            term = jnp.dot(wide[k], weights[k][:, n : n + tile], preferred_element_type=F32)
            total = term if total is None else total + term
        total = total.astype(BF)
        out[:, pl.ds(pl.multiple_of(step * half + n, 128), tile)] = total[:rows]
        lanes = slice(2 * half + n, 2 * half + n + tile)
        mine = (lax.broadcasted_iota(jnp.int32, (rows, tile), 0) & 1) == step
        out[:, lanes] = jnp.where(mine, total[rows:], out[:, lanes])


def expert_out(z, hidden, down, got):
    rows, width = hidden[0].shape
    columns = got[0].shape[1]
    steps = 2
    step = columns // steps
    whole = (rows // 12 * 8, columns + step)
    return pl.pallas_call(
        expert_out_kernel,
        grid_spec=pltpu.PrefetchScalarGridSpec(
            num_scalar_prefetch=1,
            grid=(steps,),
            in_specs=[pl.BlockSpec((rows, width), lambda i, z: (0, 0))] * NZ
            + [pl.BlockSpec((width, step), lambda i, z: (0, z[0] * steps + i))]
            + [pl.BlockSpec((width, step), lambda i, z: (0, i))] * 3,
            out_specs=pl.BlockSpec(whole, lambda i, z: (0, 0)),
            scratch_shapes=[pltpu.VMEM((NZ, 2 * whole[0], width), BF)],
        ),
        out_shape=jax.ShapeDtypeStruct(whole, BF),
        compiler_params=params(),
        cost_estimate=pl.CostEstimate(flops=16 * whole[0] * width * columns, bytes_accessed=8 * width * columns, transcendentals=0),
        name="expert_out",
    )(z, *hidden, down, *got)


def two_dots(rows, own, got, out):
    depth = own.shape[0]
    total = jnp.dot(rows[:, :depth], own[...], preferred_element_type=F32)
    total = total + jnp.dot(rows[:, depth:], got[...], preferred_element_type=F32)
    out[...] = total.astype(BF)


def dense_out_kernel(z_ref, h0, h1, h2, h3, own, got, out, held):
    @pl.when(pl.program_id(0) == 0)
    def _():
        z = z_ref[0]
        for k, ref in enumerate((h0, h1, h2, h3)):
            at = pl.multiple_of(lax.rem(z + k, NZ) * 64, 64)
            held[pl.ds(at, 64), :] = ref[...]

    two_dots(held, own, got, out)


def out_proj_kernel(z_ref, h0, h1, h2, h3, own, got, out, held):
    @pl.when(pl.program_id(0) == 0)
    def _():
        z = z_ref[0]
        row, col = grid_of((held.shape[0], h0.shape[0]))
        match = col == (row >> 4) * 4 + (row & 3)
        total = None
        for k, ref in enumerate((h0, h1, h2, h3)):
            hit = match & (((row >> 2) & 3) == lax.rem(z + k, NZ))
            term = jnp.dot(onehot(hit), ref[...], preferred_element_type=F32)
            total = term if total is None else total + term
        held[...] = total.astype(BF)

    two_dots(held, own, got, out)


def plane_dot(kernel, z, blocks, own, got, name):
    depth, columns = own.shape
    step = columns // 2
    weight = pl.BlockSpec((depth, step), lambda i, z: (0, i))
    return pl.pallas_call(
        kernel,
        grid_spec=pltpu.PrefetchScalarGridSpec(
            num_scalar_prefetch=1,
            grid=(columns // step,),
            in_specs=[pl.BlockSpec(blocks[0].shape, lambda i, z: (0, 0))] * NZ + [weight, weight],
            out_specs=pl.BlockSpec((256, step), lambda i, z: (0, i)),
            scratch_shapes=[pltpu.VMEM((256, 2 * depth), BF)],
        ),
        out_shape=jax.ShapeDtypeStruct((256, columns), BF),
        compiler_params=params(),
        cost_estimate=pl.CostEstimate(flops=1024 * depth * columns, bytes_accessed=4 * depth * columns, transcendentals=0),
        name=name,
    )(z, *blocks, own, got)


def shards(
    queries, kv_cache, new_latent, lengths, residual, gain_first, gain_second, value_proj, out_proj,
    dense_gate, dense_up, dense_down, route_ids, route_gates, expert_gate, expert_up, expert_down,
):
    z = lax.axis_index("z")
    c = lax.axis_index("c")
    latent_dim = value_proj.shape[1]
    quarter = residual.shape[1]

    zs = z.astype(jnp.int32).reshape(1)

    def pick(w, k, axis):
        return lax.dynamic_slice_in_dim(w, lax.rem(z + k, NZ) * quarter, quarter, axis)

    def cut(w, axis, which):
        return {k: pick(w, NZ - k, axis) for k in which}

    def tied(value, *groups):
        flat = [group[k] for group in groups for k in group]
        value, *flat = lax.optimization_barrier((value, *flat))
        at = iter(flat)
        return (value, *[{k: next(at) for k in group} for group in groups])

    def fetch(group):
        return {k: zsend(group[k], NZ - k) for k in group}

    only = lambda group, *which: {k: group[k] for k in which}
    picks = jnp.concatenate([route_ids.astype(F32), route_gates], axis=1)
    picks = jnp.concatenate([picks, swap_core(picks)], axis=0)
    picks = jnp.concatenate([picks, jnp.broadcast_to(c.astype(F32), (picks.shape[0], 1))], axis=1)
    hots, combs = route(picks, route_ids.shape[1])
    gain_a, gain_b = gain_first.reshape(1, -1), gain_second.reshape(1, -1)

    latents = attend(lengths, c.astype(jnp.int32).reshape(1), queries, kv_cache, new_latent, latent_dim)
    moved = lax.all_to_all(latents.reshape(16, 32, -1), YX, 0, 0, tiled=True)
    moved, value_got = lax.optimization_barrier((moved, swap_core(value_proj)))
    moved, gain_a, gain_b, hots, combs = lax.optimization_barrier((moved, gain_a, gain_b, hots, combs))
    moved, down_cut = tied(moved, cut(expert_down[0], 1, (1, 2, 3)))
    moved, mine = lax.optimization_barrier((moved, out_proj))
    out_got = swap_core(mine)
    rows = zgather(head_values(moved.reshape(512, -1), value_proj, value_got))
    rows, out_got, *mine = lax.optimization_barrier((rows, out_got, dense_gate, dense_up, dense_down))
    dense_got = [swap_core(weight) for weight in mine]
    rows, down_cut = tied(rows, down_cut)
    down_a = fetch(only(down_cut, 1, 3))
    parts = plane_scatter(plane_dot(out_proj_kernel, zs, rows, out_proj, out_got, "out_proj"))
    parts, down_a, down_cut = tied(parts, down_a, only(down_cut, 2))
    parts, *dense_got = lax.optimization_barrier((parts, *dense_got))
    first, spread = first_sum(parts, residual)
    own = lax.all_to_all(spread, YX, 0, 0, tiled=True).reshape(256, -1)
    width = 2 * dense_gate.shape[1]

    def activate(summed):
        scale = lax.rsqrt((summed[:, 2 * width] + summed[:, 2 * width + 1]) / D + EPS)[:, None]
        gate_act = summed[:, :width] * scale
        return (jax.nn.silu(gate_act) * (summed[:, width : 2 * width] * scale)).astype(BF)

    blocks = dense_in(zs, own, gain_a, [dense_gate, dense_got[0], dense_up, dense_got[1]])
    hidden = zgather(activate(zscatter(blocks)))
    hidden, down_cut = tied(hidden, down_cut)
    down_b = fetch(down_cut)
    parts = plane_scatter(plane_dot(dense_out_kernel, zs, hidden, dense_down, dense_got[2], "dense_out"))
    parts, down_b = tied(parts, down_b)
    second, scaled = second_sum(parts, first, gain_b)

    across = lambda rows, flip: lax.ppermute(
        rows, ("c", "z"), [(c0 * NZ + z0, (c0 ^ flip) * NZ + (z0 + 2) % NZ) for c0 in range(2) for z0 in range(NZ)]
    )
    far = jnp.concatenate([across(scaled, 0), across(scaled, 1)], axis=0)
    scaled = jnp.concatenate([scaled, swap_core(scaled)], axis=0)
    spread = lambda rows: lax.all_to_all(rows.reshape(16, 8, -1), YX, 0, 0, tiled=True).reshape(128, -1)
    near, far = lax.optimization_barrier((pack(scaled, hots, quarter), far))
    near = spread(near)
    near, far = lax.optimization_barrier((near, far))
    ahead, behind = zsend(near, NZ - 1), zsend(near, 1)
    far = spread(pack(far, hots, quarter))
    expert_hidden = expert_in(zs, [near, ahead, far, behind], expert_gate[0], expert_up[0])
    result = expert_out(zs, zgather(expert_hidden), expert_down[0], [down_a[1], down_b[2], down_a[3]])
    returned = lax.all_to_all(result.reshape(16, 8, -1), YX, 0, 0, tiled=True).reshape(128, -1)
    total, theirs = combine(returned, combs, second)
    return (total + swap_core(theirs)).astype(BF)


def solution(mesh):
    grid = Mesh(mesh.devices.reshape(4, 4, 2, 4), ("y", "x", "c", "z"))
    ep = ("y", "x", "c")
    both = ("y", "x", "c", "z")
    return jax.shard_map(
        shards,
        mesh=grid,
        in_specs=(
            P(both, None, None),
            P(both, None, None),
            P(both, None),
            P(both),
            P(ep, "z"),
            P("z"),
            P("z"),
            P(ep, None, None),
            P(ep, "z"),
            P("z", ep),
            P("z", ep),
            P(ep, "z"),
            P(ep, None),
            P(ep, None),
            P(ep, None, "z"),
            P(ep, None, "z"),
            P(ep, "z", None),
        ),
        out_specs=P(ep, "z"),
        check_vma=False,
    )
```

```python
import jax
import jax.numpy as jnp
from jax import lax
from jax.experimental import pallas as pl
from jax.experimental.pallas import tpu as pltpu
from jax.sharding import Mesh, PartitionSpec as P

D = 7168
ROPE = 64
VD = 128
EPS = 1e-06
YX = ("y", "x")
NZ = 4
BF = jnp.bfloat16
F32 = jnp.float32


def zsend(values, shift):
    return lax.ppermute(values, "z", [(i, (i + shift) % NZ) for i in range(NZ)])


def swap_core(values):
    return lax.ppermute(values, "c", [(0, 1), (1, 0)])


def zgather(values):
    return [values] + [zsend(values, NZ - k) for k in (1, 2, 3)]


def zscatter(blocks):
    got = [zsend(blocks[k], k) for k in (1, 2, 3)]
    total = blocks[0].astype(F32)
    for piece in got:
        total = total + piece.astype(F32)
    return total


def plane_scatter(rows):
    return lax.all_to_all(rows.reshape(16, 16, -1), YX, 0, 0, tiled=True)


def onehot(hit):
    return jnp.where(hit, 1.0, 0.0).astype(BF)


def grid_of(shape):
    return lax.broadcasted_iota(jnp.int32, shape, 0), lax.broadcasted_iota(jnp.int32, shape, 1)


def exact(a, b):
    return jnp.dot(a, b, preferred_element_type=F32).astype(BF)


def attend_kernel(len_ref, c_ref, q_ref, kv_ref, new_ref, out, latents):
    step = pl.program_id(0)
    lat = latents.shape[2]
    new = new_ref[...].astype(F32)
    score_scale = (VD + ROPE) ** (-0.5)
    down = (((0,), (0,)), ((), ()))
    for i in range(q_ref.shape[0]):
        r = step * q_ref.shape[0] + i
        q = q_ref[i]
        fresh = jnp.sum(jnp.where(lax.broadcasted_iota(jnp.int32, new.shape, 0) == r, new, 0.0), axis=0, keepdims=True)
        scores = lax.dot_general(q, kv_ref[i], down, preferred_element_type=F32) * score_scale
        own = lax.dot_general(q, new_ref[...], (((0,), (1,)), ((), ())), preferred_element_type=F32)
        own = jnp.where(lax.broadcasted_iota(jnp.int32, own.shape, 1) == r, own, 0.0)
        self_score = jnp.sum(own, axis=1, keepdims=True) * score_scale
        live = lax.broadcasted_iota(jnp.int32, (1, scores.shape[1]), 1) < len_ref[r]
        scores = jnp.where(live, scores, -jnp.inf)
        top = jnp.maximum(jnp.max(scores, axis=1, keepdims=True), self_score)
        expo = jnp.exp(scores - top)
        self_expo = jnp.exp(self_score - top)
        total = 1.0 / (jnp.sum(expo, axis=1, keepdims=True) + self_expo)
        weights = (expo * total).astype(BF)
        self_weight = (self_expo * total).astype(BF).astype(F32)
        latent = lax.dot_general(weights, kv_ref[i, :lat, :], (((1,), (1,)), ((), ())), preferred_element_type=F32)
        latents[r] = (latent + self_weight * fresh[:, :lat]).astype(BF)

    @pl.when(step == pl.num_programs(0) - 1)
    def _():
        rows = out.shape[0]
        heads = rows // latents.shape[0]
        held = latents[...].reshape(rows, lat)
        part = rows // 2
        for i in range(2):
            row, col = grid_of((part, rows))
            row = row + i * part
            core = jnp.where((row & 16) == 0, c_ref[0], 1 - c_ref[0])
            order = onehot(col == ((row >> 2) & 3) * heads + (row >> 5) * 8 + core * 4 + (row & 3))
            out[i * part : (i + 1) * part, :] = exact(order, held)


def attend(lengths, c, queries, kv_cache, new_latent, lat):
    reqs, heads, width = queries.shape
    slots = kv_cache.shape[1]
    rows = reqs * heads
    return pl.pallas_call(
        attend_kernel,
        grid_spec=pltpu.PrefetchScalarGridSpec(
            num_scalar_prefetch=2,
            grid=(reqs // 2,),
            in_specs=[
                pl.BlockSpec((2, width, heads), lambda r, n, c: (r, 0, 0)),
                pl.BlockSpec((2, width, slots), lambda r, n, c: (r, 0, 0)),
                pl.BlockSpec((reqs, width), lambda r, n, c: (0, 0)),
            ],
            out_specs=pl.BlockSpec((rows, lat), lambda r, n, c: (0, 0)),
            scratch_shapes=[pltpu.VMEM((reqs, heads, lat), BF)],
        ),
        out_shape=jax.ShapeDtypeStruct((rows, lat), BF),
        compiler_params=params(60),
        cost_estimate=pl.CostEstimate(flops=4 * reqs * heads * slots * width, bytes_accessed=2 * reqs * slots * width, transcendentals=reqs * heads * slots),
        name="attend",
    )(lengths, c, queries.transpose(0, 2, 1), kv_cache.transpose(0, 2, 1), new_latent)


def heads_kernel(x, own, got, out):
    rows = x.shape[0]
    row, col = grid_of((rows, rows))
    head, chip, r = row >> 6, (row >> 2) & 15, row & 3
    latent = exact(onehot(col == chip * 32 + (head >> 2) * 16 + r * 4 + (head & 3)), x[...])
    part, width = out.shape[0], own.shape[2]
    for head in range(2 * own.shape[0]):
        values = (own, got)[head // own.shape[0]]
        value = jnp.dot(latent[head * part : (head + 1) * part], values[head % own.shape[0]], preferred_element_type=F32)
        out[:, head * width : (head + 1) * width] = value.astype(BF)


def head_values(x, own, got):
    count, lat, width = own.shape
    rows = x.shape[0] // count // 2
    return pl.pallas_call(
        heads_kernel,
        out_shape=jax.ShapeDtypeStruct((rows, 2 * count * width), BF),
        compiler_params=pltpu.CompilerParams(vmem_limit_bytes=16 * 1024 * 1024),
        cost_estimate=pl.CostEstimate(flops=2 * x.shape[0] * lat * (width + x.shape[0]), bytes_accessed=4 * count * lat * width, transcendentals=0),
        name="head_values",
    )(x, own, got)


def first_kernel(parts, residual, first, wide):
    total = residual[...].astype(F32)
    for i in range(parts.shape[0]):
        total = total + parts[i].astype(F32)
    first[...] = total
    for i in range(parts.shape[0]):
        wide[i] = total.astype(BF)


def first_sum(parts, residual):
    return pl.pallas_call(
        first_kernel,
        out_shape=[jax.ShapeDtypeStruct(residual.shape, F32), jax.ShapeDtypeStruct(parts.shape, BF)],
        compiler_params=pltpu.CompilerParams(vmem_limit_bytes=16 * 1024 * 1024),
        cost_estimate=pl.CostEstimate(flops=parts.size, bytes_accessed=200 * parts.size, transcendentals=0),
        name="first_sum",
    )(parts, residual)


def second_kernel(parts, first, gain, second, scaled):
    total = first[...]
    for i in range(parts.shape[0]):
        total = total + parts[i].astype(F32)
    second[...] = total
    width = total.shape[1]
    scaled[:, :width] = (total * gain[...].astype(F32)).astype(BF)
    square = total * total
    lanes = square[:, :128]
    for j in range(1, width // 128):
        lanes = lanes + square[:, j * 128 : (j + 1) * 128]
    scaled[:, width:] = tail_of(lanes)


def second_sum(parts, first, gain):
    rows, width = first.shape
    return pl.pallas_call(
        second_kernel,
        out_shape=[jax.ShapeDtypeStruct(first.shape, F32), jax.ShapeDtypeStruct((rows, width + 128), BF)],
        compiler_params=pltpu.CompilerParams(vmem_limit_bytes=16 * 1024 * 1024),
        cost_estimate=pl.CostEstimate(flops=parts.size, bytes_accessed=2 * parts.size, transcendentals=0),
        name="second_sum",
    )(parts, first, gain)


def route_kernel(picks, hots, combs, *, top):
    count = picks.shape[0]
    experts = 32
    ids, gates = picks[:, :top], picks[:, top : 2 * top]
    core = picks[:1, 2 * top : 2 * top + 1]
    expert = lax.broadcasted_iota(jnp.int32, (count, experts), 1).astype(F32)
    named = jnp.zeros((count, experts), F32)
    gate = jnp.zeros((count, experts), F32)
    for k in range(top):
        hit = ids[:, k : k + 1] == expert
        named = named + jnp.where(hit, 1.0, 0.0)
        gate = gate + jnp.where(hit, gates[:, k : k + 1], 0.0)
    row, col = grid_of((count, count))
    earlier = onehot((col < row) & ((col >> 4) == (row >> 4)))
    place = jnp.dot(earlier, named.astype(BF), preferred_element_type=F32)
    token = lax.broadcasted_iota(jnp.int32, (count, experts), 0)
    place = place + jnp.where(token >= 16, 6.0, 0.0)
    place = jnp.where(named > 0.5, place, 100.0)
    across = lambda rows, chip_of, values: lax.dot_general(
        onehot(grid_of((rows, experts))[1].astype(F32) == chip_of(grid_of((rows, experts))[0]).astype(F32) * 2.0 + core),
        values.astype(BF),
        (((1,), (1,)), ((), ())),
        preferred_element_type=F32,
    )
    rows = combs.shape[2]
    at = across(rows, lambda r: r >> 3, place)
    p = lax.broadcasted_iota(jnp.int32, (rows, 1), 0) & 7
    hots[0] = onehot(at == p.astype(F32))
    hots[1] = onehot(at == (8 + (p >> 1)).astype(F32))
    high = gate.astype(BF)
    for j, part in enumerate((high, gate - high.astype(F32))):
        value = across(rows, lambda r: r >> 3, part)
        for m in range(3):
            want = p if m == 0 else jnp.where((p & 1) == m - 1, 8 + (p >> 1), -1)
            combs[j, m] = jnp.where(at == want.astype(F32), value, 0.0).astype(BF)


def route(picks, top):
    count = picks.shape[0]
    return pl.pallas_call(
        lambda *refs: route_kernel(*refs, top=top),
        out_shape=[jax.ShapeDtypeStruct((2, 128, count), BF), jax.ShapeDtypeStruct((2, 3, 128, count), BF)],
        compiler_params=pltpu.CompilerParams(vmem_limit_bytes=16 * 1024 * 1024),
        cost_estimate=pl.CostEstimate(flops=1 << 22, bytes_accessed=1 << 18, transcendentals=0),
        name="route",
    )(picks)


def combine_kernel(returned, combs, second, own, other):
    width = own.shape[1]
    half = width // 2
    sums = []
    for m in range(3):
        x = returned[:, :width] if m == 0 else returned[:, width:]
        sums.append(
            sum(lax.dot_general(combs[j, m], x, (((0,), (0,)), ((), ())), preferred_element_type=F32) for j in range(2))
        )
    rows = own.shape[0]
    for m in range(2):
        lanes = slice(m * half, (m + 1) * half)
        total = sums[0][:, lanes] + sums[1 + m]
        own[:, lanes] = second[:, lanes] + total[:rows]
        other[:, lanes] = total[rows:]


def combine(returned, combs, second):
    return pl.pallas_call(
        combine_kernel,
        out_shape=[jax.ShapeDtypeStruct(second.shape, F32)] * 2,
        compiler_params=pltpu.CompilerParams(vmem_limit_bytes=16 * 1024 * 1024),
        cost_estimate=pl.CostEstimate(flops=12 * 32 * 128 * 1792, bytes_accessed=1 << 20, transcendentals=0),
        name="combine",
    )(returned, combs, second)


def pack_kernel(x, hots, out, *, width):
    half = width // 2
    rows = out.shape[0]
    head = exact(hots[0], x[...])
    tail = exact(hots[1], x[...])
    out[:, :width] = head[:, :width]
    even = (lax.broadcasted_iota(jnp.int32, (rows, half), 0) & 1) == 0
    out[:, width : width + half] = jnp.where(even, tail[:, :half], tail[:, half:width])
    lane = lax.broadcasted_iota(jnp.int32, (rows, 128), 1)
    out[:, width + half :] = jnp.where(lane < 2, head[:, width:], tail[:, width:])


def pack(x, hots, width):
    rows = hots.shape[1]
    return pl.pallas_call(
        lambda *refs: pack_kernel(*refs, width=width),
        out_shape=jax.ShapeDtypeStruct((rows, width * 3 // 2 + 128), BF),
        compiler_params=pltpu.CompilerParams(vmem_limit_bytes=16 * 1024 * 1024),
        cost_estimate=pl.CostEstimate(flops=4 * rows * width * 32, bytes_accessed=3 * rows * width, transcendentals=0),
        name="pack",
    )(x, hots)


def params(mib=16):
    return pltpu.CompilerParams(dimension_semantics=("arbitrary",), vmem_limit_bytes=mib * 1024 * 1024)


def tail_of(squares):
    total = jnp.sum(squares, axis=1, keepdims=True)
    hi = total.astype(BF).astype(F32)
    lane = lax.broadcasted_iota(jnp.int32, (total.shape[0], 128), 1)
    return jnp.where(lane < 4, jnp.where((lane & 1) == 0, hi, total - hi), 0.0).astype(BF)


def dense_in_kernel(z_ref, x, gain, gate, gate_got, up, up_got, o0, o1, o2, o3, acc, squares, tail):
    step = pl.program_id(0)
    width = gate.shape[1]

    @pl.when(step == 0)
    def _():
        acc[...] = jnp.zeros_like(acc)
        squares[...] = jnp.zeros_like(squares)

    value = x[...].astype(F32)
    normed = (value * gain[...].astype(F32)).astype(BF)
    for j, weight in enumerate((gate, gate_got, up, up_got)):
        acc[:, j * width : (j + 1) * width] += jnp.dot(normed, weight[...], preferred_element_type=F32)
    square = value * value
    for j in range(square.shape[1] // 128):
        squares[...] += square[:, j * 128 : (j + 1) * 128]

    @pl.when(step == pl.num_programs(0) - 1)
    def _():
        z = z_ref[0]
        tail[...] = tail_of(squares[...])
        part = acc.shape[0] // NZ
        for k, out in enumerate((o0, o1, o2, o3)):
            at = pl.ds(pl.multiple_of(lax.rem(z + k, NZ) * part, part), part)
            out[:, : 4 * width] = acc[at, :].astype(BF)
            out[:, 4 * width :] = tail[at, :]


def dense_in(z, x, gain, weights):
    depth, width = weights[0].shape
    step = depth
    rows = x.shape[0]
    lanes = 4 * width + 128
    return pl.pallas_call(
        dense_in_kernel,
        grid_spec=pltpu.PrefetchScalarGridSpec(
            num_scalar_prefetch=1,
            grid=(depth // step,),
            in_specs=[
                pl.BlockSpec((rows, step), lambda i, z: (0, i)),
                pl.BlockSpec((1, step), lambda i, z: (0, i)),
            ]
            + [pl.BlockSpec((step, width), lambda i, z: (i, 0))] * 4,
            out_specs=[pl.BlockSpec((rows // NZ, lanes), lambda i, z: (0, 0))] * NZ,
            scratch_shapes=[
                pltpu.VMEM((rows, 4 * width), F32),
                pltpu.VMEM((rows, 128), F32),
                pltpu.VMEM((rows, 128), BF),
            ],
        ),
        out_shape=[jax.ShapeDtypeStruct((rows // NZ, lanes), BF)] * NZ,
        compiler_params=params(28),
        cost_estimate=pl.CostEstimate(flops=8 * rows * depth * width, bytes_accessed=2 * depth * (rows + 4 * width), transcendentals=0),
        name="dense_in",
    )(z, x, gain, *weights)


def silu(value):
    return value / (1.0 + jnp.exp(-value))


def expert_in_kernel(z_ref, *refs):
    xs, gates, ups, out = refs[:4], refs[4:8], refs[8:12], refs[12]
    rows = xs[0].shape[0]
    depth = gates[0].shape[0]
    half = depth // 2
    row, col = grid_of((rows // 2, rows))
    picks = [onehot(col == 2 * row + i) for i in range(2)]
    lane = lax.broadcasted_iota(jnp.int32, (1, 128), 1)
    gate, up, total = None, None, None
    for m in range(NZ):
        head, rest = xs[m][:, :depth], xs[m][:, depth:]
        even, odd = exact(picks[0], rest), exact(picks[1], rest[:, :half])
        x = jnp.concatenate([head, jnp.concatenate([even[:, :half], odd], axis=1)], axis=0)
        square = jnp.concatenate(
            [
                jnp.where(lane < 2, rest[:, half:].astype(F32), 0.0),
                jnp.where((lane >= 2) & (lane < 4), even[:, half:].astype(F32), 0.0),
            ],
            axis=0,
        )
        one = jnp.dot(x, gates[m][...], preferred_element_type=F32)
        two = jnp.dot(x, ups[m][...], preferred_element_type=F32)
        gate = one if gate is None else gate + one
        up = two if up is None else up + two
        total = square if total is None else total + square
    scale = lax.rsqrt(jnp.sum(total, axis=1, keepdims=True) / D + EPS)
    out[...] = (silu(gate * scale) * (up * scale)).astype(BF)


def expert_in(z, xs, gate, up):
    depth, width = gate.shape
    rows, lanes = xs[0].shape
    ws = [pl.BlockSpec((depth // NZ, width), lambda i, z, m=m: (lax.rem(z[0] + m, NZ), 0)) for m in range(NZ)]
    total = rows * 3 // 2
    return pl.pallas_call(
        expert_in_kernel,
        grid_spec=pltpu.PrefetchScalarGridSpec(
            num_scalar_prefetch=1,
            grid=(1,),
            in_specs=[pl.BlockSpec((rows, lanes), lambda i, z: (0, 0))] * NZ + ws + ws,
            out_specs=pl.BlockSpec((total, width), lambda i, z: (0, 0)),
        ),
        out_shape=jax.ShapeDtypeStruct((total, width), BF),
        compiler_params=params(28),
        cost_estimate=pl.CostEstimate(flops=4 * total * depth * width, bytes_accessed=4 * depth * width, transcendentals=0),
        name="expert_in",
    )(z, *xs, *[gate] * 4, *[up] * 4)


def expert_out_kernel(z_ref, *refs):
    hidden, weights, out, wide = refs[:4], refs[4:8], refs[8], refs[9]
    step = pl.program_id(0)
    rows = out.shape[0]

    @pl.when(step == 0)
    def _():
        row, col = grid_of((rows, rows // 2))
        order = onehot(col == row >> 1)
        for k in range(NZ):
            wide[k, :rows] = hidden[k][:rows]
            wide[k, rows:] = exact(order, hidden[k][rows:])

    half = weights[0].shape[1]
    for n in range(0, half, 256):
        tile = min(256, half - n)
        total = None
        for k in range(NZ):
            term = jnp.dot(wide[k], weights[k][:, n : n + tile], preferred_element_type=F32)
            total = term if total is None else total + term
        total = total.astype(BF)
        out[:, pl.ds(pl.multiple_of(step * half + n, 128), tile)] = total[:rows]
        lanes = slice(2 * half + n, 2 * half + n + tile)
        mine = (lax.broadcasted_iota(jnp.int32, (rows, tile), 0) & 1) == step
        out[:, lanes] = jnp.where(mine, total[rows:], out[:, lanes])


def expert_out(z, hidden, down, got):
    rows, width = hidden[0].shape
    columns = got[0].shape[1]
    steps = 2
    step = columns // steps
    whole = (rows // 12 * 8, columns + step)
    return pl.pallas_call(
        expert_out_kernel,
        grid_spec=pltpu.PrefetchScalarGridSpec(
            num_scalar_prefetch=1,
            grid=(steps,),
            in_specs=[pl.BlockSpec((rows, width), lambda i, z: (0, 0))] * NZ
            + [pl.BlockSpec((width, step), lambda i, z: (0, z[0] * steps + i))]
            + [pl.BlockSpec((width, step), lambda i, z: (0, i))] * 3,
            out_specs=pl.BlockSpec(whole, lambda i, z: (0, 0)),
            scratch_shapes=[pltpu.VMEM((NZ, 2 * whole[0], width), BF)],
        ),
        out_shape=jax.ShapeDtypeStruct(whole, BF),
        compiler_params=params(),
        cost_estimate=pl.CostEstimate(flops=16 * whole[0] * width * columns, bytes_accessed=8 * width * columns, transcendentals=0),
        name="expert_out",
    )(z, *hidden, down, *got)


def two_dots(rows, own, got, out):
    depth = own.shape[0]
    total = jnp.dot(rows[:, :depth], own[...], preferred_element_type=F32)
    total = total + jnp.dot(rows[:, depth:], got[...], preferred_element_type=F32)
    out[...] = total.astype(BF)


def dense_out_kernel(z_ref, h0, h1, h2, h3, own, got, out, held):
    @pl.when(pl.program_id(0) == 0)
    def _():
        z = z_ref[0]
        for k, ref in enumerate((h0, h1, h2, h3)):
            at = pl.multiple_of(lax.rem(z + k, NZ) * 64, 64)
            held[pl.ds(at, 64), :] = ref[...]

    two_dots(held, own, got, out)


def out_proj_kernel(z_ref, h0, h1, h2, h3, own, got, out, held):
    @pl.when(pl.program_id(0) == 0)
    def _():
        z = z_ref[0]
        row, col = grid_of((held.shape[0], h0.shape[0]))
        match = col == (row >> 4) * 4 + (row & 3)
        total = None
        for k, ref in enumerate((h0, h1, h2, h3)):
            hit = match & (((row >> 2) & 3) == lax.rem(z + k, NZ))
            term = jnp.dot(onehot(hit), ref[...], preferred_element_type=F32)
            total = term if total is None else total + term
        held[...] = total.astype(BF)

    two_dots(held, own, got, out)


def plane_dot(kernel, z, blocks, own, got, name):
    depth, columns = own.shape
    step = columns
    weight = pl.BlockSpec((depth, step), lambda i, z: (0, i))
    return pl.pallas_call(
        kernel,
        grid_spec=pltpu.PrefetchScalarGridSpec(
            num_scalar_prefetch=1,
            grid=(columns // step,),
            in_specs=[pl.BlockSpec(blocks[0].shape, lambda i, z: (0, 0))] * NZ + [weight, weight],
            out_specs=pl.BlockSpec((256, step), lambda i, z: (0, i)),
            scratch_shapes=[pltpu.VMEM((256, 2 * depth), BF)],
        ),
        out_shape=jax.ShapeDtypeStruct((256, columns), BF),
        compiler_params=params(),
        cost_estimate=pl.CostEstimate(flops=1024 * depth * columns, bytes_accessed=4 * depth * columns, transcendentals=0),
        name=name,
    )(z, *blocks, own, got)


def shards(
    queries, kv_cache, new_latent, lengths, residual, gain_first, gain_second, value_proj, out_proj,
    dense_gate, dense_up, dense_down, route_ids, route_gates, expert_gate, expert_up, expert_down,
):
    z = lax.axis_index("z")
    c = lax.axis_index("c")
    latent_dim = value_proj.shape[1]
    quarter = residual.shape[1]

    zs = z.astype(jnp.int32).reshape(1)

    def pick(w, k, axis):
        return lax.dynamic_slice_in_dim(w, lax.rem(z + k, NZ) * quarter, quarter, axis)

    def cut(w, axis, which):
        return {k: pick(w, NZ - k, axis) for k in which}

    def tied(value, *groups):
        flat = [group[k] for group in groups for k in group]
        value, *flat = lax.optimization_barrier((value, *flat))
        at = iter(flat)
        return (value, *[{k: next(at) for k in group} for group in groups])

    def fetch(group):
        return {k: zsend(group[k], NZ - k) for k in group}

    only = lambda group, *which: {k: group[k] for k in which}
    picks = jnp.concatenate([route_ids.astype(F32), route_gates], axis=1)
    picks = jnp.concatenate([picks, swap_core(picks)], axis=0)
    picks = jnp.concatenate([picks, jnp.broadcast_to(c.astype(F32), (picks.shape[0], 1))], axis=1)
    hots, combs = route(picks, route_ids.shape[1])
    gain_a, gain_b = gain_first.reshape(1, -1), gain_second.reshape(1, -1)

    latents = attend(lengths, c.astype(jnp.int32).reshape(1), queries, kv_cache, new_latent, latent_dim)
    moved = lax.all_to_all(latents.reshape(16, 32, -1), YX, 0, 0, tiled=True)
    moved, value_got = lax.optimization_barrier((moved, swap_core(value_proj)))
    moved, gain_a, gain_b, hots, combs = lax.optimization_barrier((moved, gain_a, gain_b, hots, combs))
    moved, down_cut = tied(moved, cut(expert_down[0], 1, (1, 2, 3)))
    moved, mine = lax.optimization_barrier((moved, out_proj))
    out_got = swap_core(mine)
    rows = zgather(head_values(moved.reshape(512, -1), value_proj, value_got))
    rows, out_got, *mine = lax.optimization_barrier((rows, out_got, dense_gate, dense_up, dense_down))
    dense_got = [swap_core(weight) for weight in mine]
    rows, down_cut = tied(rows, down_cut)
    down_a = fetch(only(down_cut, 1, 3))
    parts = plane_scatter(plane_dot(out_proj_kernel, zs, rows, out_proj, out_got, "out_proj"))
    parts, down_a, down_cut = tied(parts, down_a, only(down_cut, 2))
    parts, *dense_got = lax.optimization_barrier((parts, *dense_got))
    first, spread = first_sum(parts, residual)
    own = lax.all_to_all(spread, YX, 0, 0, tiled=True).reshape(256, -1)
    width = 2 * dense_gate.shape[1]

    def activate(summed):
        scale = lax.rsqrt((summed[:, 2 * width] + summed[:, 2 * width + 1]) / D + EPS)[:, None]
        gate_act = summed[:, :width] * scale
        return (jax.nn.silu(gate_act) * (summed[:, width : 2 * width] * scale)).astype(BF)

    blocks = dense_in(zs, own, gain_a, [dense_gate, dense_got[0], dense_up, dense_got[1]])
    hidden = zgather(activate(zscatter(blocks)))
    hidden, down_cut = tied(hidden, down_cut)
    down_b = fetch(down_cut)
    parts = plane_scatter(plane_dot(dense_out_kernel, zs, hidden, dense_down, dense_got[2], "dense_out"))
    parts, down_b = tied(parts, down_b)
    second, scaled = second_sum(parts, first, gain_b)

    across = lambda rows, flip: lax.ppermute(
        rows, ("c", "z"), [(c0 * NZ + z0, (c0 ^ flip) * NZ + (z0 + 2) % NZ) for c0 in range(2) for z0 in range(NZ)]
    )
    far = jnp.concatenate([across(scaled, 0), across(scaled, 1)], axis=0)
    scaled = jnp.concatenate([scaled, swap_core(scaled)], axis=0)
    spread = lambda rows: lax.all_to_all(rows.reshape(16, 8, -1), YX, 0, 0, tiled=True).reshape(128, -1)
    near, far = lax.optimization_barrier((pack(scaled, hots, quarter), far))
    near = spread(near)
    near, far = lax.optimization_barrier((near, far))
    ahead, behind = zsend(near, NZ - 1), zsend(near, 1)
    far = spread(pack(far, hots, quarter))
    expert_hidden = expert_in(zs, [near, ahead, far, behind], expert_gate[0], expert_up[0])
    result = expert_out(zs, zgather(expert_hidden), expert_down[0], [down_a[1], down_b[2], down_a[3]])
    returned = lax.all_to_all(result.reshape(16, 8, -1), YX, 0, 0, tiled=True).reshape(128, -1)
    total, theirs = combine(returned, combs, second)
    return (total + swap_core(theirs)).astype(BF)


def solution(mesh):
    grid = Mesh(mesh.devices.reshape(4, 4, 2, 4), ("y", "x", "c", "z"))
    ep = ("y", "x", "c")
    both = ("y", "x", "c", "z")
    return jax.shard_map(
        shards,
        mesh=grid,
        in_specs=(
            P(both, None, None),
            P(both, None, None),
            P(both, None),
            P(both),
            P(ep, "z"),
            P("z"),
            P("z"),
            P(ep, None, None),
            P(ep, "z"),
            P("z", ep),
            P("z", ep),
            P(ep, "z"),
            P(ep, None),
            P(ep, None),
            P(ep, None, "z"),
            P(ep, None, "z"),
            P(ep, "z", None),
        ),
        out_specs=P(ep, "z"),
        check_vma=False,
    )
```

```python
import jax
import jax.numpy as jnp
from jax import lax
from jax.experimental import pallas as pl
from jax.experimental.pallas import tpu as pltpu
from jax.sharding import Mesh, PartitionSpec as P

D = 7168
ROPE = 64
VD = 128
EPS = 1e-06
YX = ("y", "x")
NZ = 4
BF = jnp.bfloat16
F32 = jnp.float32


def zsend(values, shift):
    return lax.ppermute(values, "z", [(i, (i + shift) % NZ) for i in range(NZ)])


def swap_core(values):
    return lax.ppermute(values, "c", [(0, 1), (1, 0)])


def zgather(values):
    return [values] + [zsend(values, NZ - k) for k in (1, 2, 3)]


def zscatter(blocks):
    got = [zsend(blocks[k], k) for k in (1, 2, 3)]
    total = blocks[0].astype(F32)
    for piece in got:
        total = total + piece.astype(F32)
    return total


def plane_scatter(rows):
    return lax.all_to_all(rows.reshape(16, 16, -1), YX, 0, 0, tiled=True)


def onehot(hit):
    return jnp.where(hit, 1.0, 0.0).astype(BF)


def grid_of(shape):
    return lax.broadcasted_iota(jnp.int32, shape, 0), lax.broadcasted_iota(jnp.int32, shape, 1)


def exact(a, b):
    return jnp.dot(a, b, preferred_element_type=F32).astype(BF)


def attend_kernel(len_ref, c_ref, q_ref, kv_ref, new_ref, out, latents):
    step = pl.program_id(0)
    lat = latents.shape[2]
    new = new_ref[...].astype(F32)
    score_scale = (VD + ROPE) ** (-0.5)
    down = (((0,), (0,)), ((), ()))
    for i in range(q_ref.shape[0]):
        r = step * q_ref.shape[0] + i
        q = q_ref[i]
        fresh = jnp.sum(jnp.where(lax.broadcasted_iota(jnp.int32, new.shape, 0) == r, new, 0.0), axis=0, keepdims=True)
        scores = lax.dot_general(q, kv_ref[i], down, preferred_element_type=F32) * score_scale
        own = lax.dot_general(q, new_ref[...], (((0,), (1,)), ((), ())), preferred_element_type=F32)
        own = jnp.where(lax.broadcasted_iota(jnp.int32, own.shape, 1) == r, own, 0.0)
        self_score = jnp.sum(own, axis=1, keepdims=True) * score_scale
        live = lax.broadcasted_iota(jnp.int32, (1, scores.shape[1]), 1) < len_ref[r]
        scores = jnp.where(live, scores, -jnp.inf)
        top = jnp.maximum(jnp.max(scores, axis=1, keepdims=True), self_score)
        expo = jnp.exp(scores - top)
        self_expo = jnp.exp(self_score - top)
        total = 1.0 / (jnp.sum(expo, axis=1, keepdims=True) + self_expo)
        weights = (expo * total).astype(BF)
        self_weight = (self_expo * total).astype(BF).astype(F32)
        latent = lax.dot_general(weights, kv_ref[i, :lat, :], (((1,), (1,)), ((), ())), preferred_element_type=F32)
        latents[r] = (latent + self_weight * fresh[:, :lat]).astype(BF)

    @pl.when(step == pl.num_programs(0) - 1)
    def _():
        rows = out.shape[0]
        heads = rows // latents.shape[0]
        held = latents[...].reshape(rows, lat)
        part = rows // 2
        for i in range(2):
            row, col = grid_of((part, rows))
            row = row + i * part
            core = jnp.where((row & 16) == 0, c_ref[0], 1 - c_ref[0])
            order = onehot(col == ((row >> 2) & 3) * heads + (row >> 5) * 8 + core * 4 + (row & 3))
            out[i * part : (i + 1) * part, :] = exact(order, held)


def attend(lengths, c, queries, kv_cache, new_latent, lat):
    reqs, heads, width = queries.shape
    slots = kv_cache.shape[1]
    rows = reqs * heads
    return pl.pallas_call(
        attend_kernel,
        grid_spec=pltpu.PrefetchScalarGridSpec(
            num_scalar_prefetch=2,
            grid=(reqs // 2,),
            in_specs=[
                pl.BlockSpec((2, width, heads), lambda r, n, c: (r, 0, 0)),
                pl.BlockSpec((2, width, slots), lambda r, n, c: (r, 0, 0)),
                pl.BlockSpec((reqs, width), lambda r, n, c: (0, 0)),
            ],
            out_specs=pl.BlockSpec((rows, lat), lambda r, n, c: (0, 0)),
            scratch_shapes=[pltpu.VMEM((reqs, heads, lat), BF)],
        ),
        out_shape=jax.ShapeDtypeStruct((rows, lat), BF),
        compiler_params=params(60),
        cost_estimate=pl.CostEstimate(flops=4 * reqs * heads * slots * width, bytes_accessed=2 * reqs * slots * width, transcendentals=reqs * heads * slots),
        name="attend",
    )(lengths, c, queries.transpose(0, 2, 1), kv_cache.transpose(0, 2, 1), new_latent)


def heads_kernel(x, own, got, out):
    rows = x.shape[0]
    row, col = grid_of((rows, rows))
    head, chip, r = row >> 6, (row >> 2) & 15, row & 3
    latent = exact(onehot(col == chip * 32 + (head >> 2) * 16 + r * 4 + (head & 3)), x[...])
    part, width = out.shape[0], own.shape[2]
    for head in range(2 * own.shape[0]):
        values = (own, got)[head // own.shape[0]]
        value = jnp.dot(latent[head * part : (head + 1) * part], values[head % own.shape[0]], preferred_element_type=F32)
        out[:, head * width : (head + 1) * width] = value.astype(BF)


def head_values(x, own, got):
    count, lat, width = own.shape
    rows = x.shape[0] // count // 2
    return pl.pallas_call(
        heads_kernel,
        out_shape=jax.ShapeDtypeStruct((rows, 2 * count * width), BF),
        compiler_params=pltpu.CompilerParams(vmem_limit_bytes=16 * 1024 * 1024),
        cost_estimate=pl.CostEstimate(flops=2 * x.shape[0] * lat * (width + x.shape[0]), bytes_accessed=4 * count * lat * width, transcendentals=0),
        name="head_values",
    )(x, own, got)


def first_kernel(parts, residual, first, wide):
    total = residual[...].astype(F32)
    for i in range(parts.shape[0]):
        total = total + parts[i].astype(F32)
    first[...] = total
    for i in range(parts.shape[0]):
        wide[i] = total.astype(BF)


def first_sum(parts, residual):
    return pl.pallas_call(
        first_kernel,
        out_shape=[jax.ShapeDtypeStruct(residual.shape, F32), jax.ShapeDtypeStruct(parts.shape, BF)],
        compiler_params=pltpu.CompilerParams(vmem_limit_bytes=16 * 1024 * 1024),
        cost_estimate=pl.CostEstimate(flops=parts.size, bytes_accessed=200 * parts.size, transcendentals=0),
        name="first_sum",
    )(parts, residual)


def second_kernel(parts, first, gain, second, scaled):
    total = first[...]
    for i in range(parts.shape[0]):
        total = total + parts[i].astype(F32)
    second[...] = total
    width = total.shape[1]
    scaled[:, :width] = (total * gain[...].astype(F32)).astype(BF)
    square = total * total
    lanes = square[:, :128]
    for j in range(1, width // 128):
        lanes = lanes + square[:, j * 128 : (j + 1) * 128]
    scaled[:, width:] = tail_of(lanes)


def second_sum(parts, first, gain):
    rows, width = first.shape
    return pl.pallas_call(
        second_kernel,
        out_shape=[jax.ShapeDtypeStruct(first.shape, F32), jax.ShapeDtypeStruct((rows, width + 128), BF)],
        compiler_params=pltpu.CompilerParams(vmem_limit_bytes=16 * 1024 * 1024),
        cost_estimate=pl.CostEstimate(flops=parts.size, bytes_accessed=2 * parts.size, transcendentals=0),
        name="second_sum",
    )(parts, first, gain)


def route_kernel(picks, hots, combs, *, top):
    count = picks.shape[0]
    experts = 32
    ids, gates = picks[:, :top], picks[:, top : 2 * top]
    core = picks[:1, 2 * top : 2 * top + 1]
    expert = lax.broadcasted_iota(jnp.int32, (count, experts), 1).astype(F32)
    named = jnp.zeros((count, experts), F32)
    gate = jnp.zeros((count, experts), F32)
    for k in range(top):
        hit = ids[:, k : k + 1] == expert
        named = named + jnp.where(hit, 1.0, 0.0)
        gate = gate + jnp.where(hit, gates[:, k : k + 1], 0.0)
    row, col = grid_of((count, count))
    earlier = onehot((col < row) & ((col >> 4) == (row >> 4)))
    place = jnp.dot(earlier, named.astype(BF), preferred_element_type=F32)
    token = lax.broadcasted_iota(jnp.int32, (count, experts), 0)
    place = place + jnp.where(token >= 16, 6.0, 0.0)
    place = jnp.where(named > 0.5, place, 100.0)
    across = lambda rows, chip_of, values: lax.dot_general(
        onehot(grid_of((rows, experts))[1].astype(F32) == chip_of(grid_of((rows, experts))[0]).astype(F32) * 2.0 + core),
        values.astype(BF),
        (((1,), (1,)), ((), ())),
        preferred_element_type=F32,
    )
    rows = combs.shape[2]
    at = across(rows, lambda r: r >> 3, place)
    p = lax.broadcasted_iota(jnp.int32, (rows, 1), 0) & 7
    hots[0] = onehot(at == p.astype(F32))
    hots[1] = onehot(at == (8 + (p >> 1)).astype(F32))
    high = gate.astype(BF)
    for j, part in enumerate((high, gate - high.astype(F32))):
        value = across(rows, lambda r: r >> 3, part)
        for m in range(3):
            want = p if m == 0 else jnp.where((p & 1) == m - 1, 8 + (p >> 1), -1)
            combs[j, m] = jnp.where(at == want.astype(F32), value, 0.0).astype(BF)


def route(picks, top):
    count = picks.shape[0]
    return pl.pallas_call(
        lambda *refs: route_kernel(*refs, top=top),
        out_shape=[jax.ShapeDtypeStruct((2, 128, count), BF), jax.ShapeDtypeStruct((2, 3, 128, count), BF)],
        compiler_params=pltpu.CompilerParams(vmem_limit_bytes=16 * 1024 * 1024),
        cost_estimate=pl.CostEstimate(flops=1 << 22, bytes_accessed=1 << 18, transcendentals=0),
        name="route",
    )(picks)


def combine_kernel(returned, combs, second, own, other):
    width = own.shape[1]
    half = width // 2
    sums = []
    for m in range(3):
        x = returned[:, :width] if m == 0 else returned[:, width:]
        sums.append(
            sum(lax.dot_general(combs[j, m], x, (((0,), (0,)), ((), ())), preferred_element_type=F32) for j in range(2))
        )
    rows = own.shape[0]
    for m in range(2):
        lanes = slice(m * half, (m + 1) * half)
        total = sums[0][:, lanes] + sums[1 + m]
        own[:, lanes] = second[:, lanes] + total[:rows]
        other[:, lanes] = total[rows:]


def combine(returned, combs, second):
    return pl.pallas_call(
        combine_kernel,
        out_shape=[jax.ShapeDtypeStruct(second.shape, F32)] * 2,
        compiler_params=pltpu.CompilerParams(vmem_limit_bytes=16 * 1024 * 1024),
        cost_estimate=pl.CostEstimate(flops=12 * 32 * 128 * 1792, bytes_accessed=1 << 20, transcendentals=0),
        name="combine",
    )(returned, combs, second)


def pack_kernel(x, hots, out, *, width):
    half = width // 2
    rows = out.shape[0]
    head = exact(hots[0], x[...])
    tail = exact(hots[1], x[...])
    out[:, :width] = head[:, :width]
    even = (lax.broadcasted_iota(jnp.int32, (rows, half), 0) & 1) == 0
    out[:, width : width + half] = jnp.where(even, tail[:, :half], tail[:, half:width])
    lane = lax.broadcasted_iota(jnp.int32, (rows, 128), 1)
    out[:, width + half :] = jnp.where(lane < 2, head[:, width:], tail[:, width:])


def pack(x, hots, width):
    rows = hots.shape[1]
    return pl.pallas_call(
        lambda *refs: pack_kernel(*refs, width=width),
        out_shape=jax.ShapeDtypeStruct((rows, width * 3 // 2 + 128), BF),
        compiler_params=pltpu.CompilerParams(vmem_limit_bytes=16 * 1024 * 1024),
        cost_estimate=pl.CostEstimate(flops=4 * rows * width * 32, bytes_accessed=3 * rows * width, transcendentals=0),
        name="pack",
    )(x, hots)


def params(mib=16):
    return pltpu.CompilerParams(dimension_semantics=("arbitrary",), vmem_limit_bytes=mib * 1024 * 1024)


def tail_of(squares):
    total = jnp.sum(squares, axis=1, keepdims=True)
    hi = total.astype(BF).astype(F32)
    lane = lax.broadcasted_iota(jnp.int32, (total.shape[0], 128), 1)
    return jnp.where(lane < 4, jnp.where((lane & 1) == 0, hi, total - hi), 0.0).astype(BF)


def dense_in_kernel(z_ref, x, gain, gate, gate_got, up, up_got, o0, o1, o2, o3, acc, squares, tail):
    step = pl.program_id(0)
    width = gate.shape[1]

    @pl.when(step == 0)
    def _():
        acc[...] = jnp.zeros_like(acc)
        squares[...] = jnp.zeros_like(squares)

    value = x[...].astype(F32)
    normed = (value * gain[...].astype(F32)).astype(BF)
    for j, weight in enumerate((gate, gate_got, up, up_got)):
        acc[:, j * width : (j + 1) * width] += jnp.dot(normed, weight[...], preferred_element_type=F32)
    square = value * value
    for j in range(square.shape[1] // 128):
        squares[...] += square[:, j * 128 : (j + 1) * 128]

    @pl.when(step == pl.num_programs(0) - 1)
    def _():
        z = z_ref[0]
        tail[...] = tail_of(squares[...])
        part = acc.shape[0] // NZ
        for k, out in enumerate((o0, o1, o2, o3)):
            at = pl.ds(pl.multiple_of(lax.rem(z + k, NZ) * part, part), part)
            out[:, : 4 * width] = acc[at, :].astype(BF)
            out[:, 4 * width :] = tail[at, :]


def dense_in(z, x, gain, weights):
    depth, width = weights[0].shape
    step = depth
    rows = x.shape[0]
    lanes = 4 * width + 128
    return pl.pallas_call(
        dense_in_kernel,
        grid_spec=pltpu.PrefetchScalarGridSpec(
            num_scalar_prefetch=1,
            grid=(depth // step,),
            in_specs=[
                pl.BlockSpec((rows, step), lambda i, z: (0, i)),
                pl.BlockSpec((1, step), lambda i, z: (0, i)),
            ]
            + [pl.BlockSpec((step, width), lambda i, z: (i, 0))] * 4,
            out_specs=[pl.BlockSpec((rows // NZ, lanes), lambda i, z: (0, 0))] * NZ,
            scratch_shapes=[
                pltpu.VMEM((rows, 4 * width), F32),
                pltpu.VMEM((rows, 128), F32),
                pltpu.VMEM((rows, 128), BF),
            ],
        ),
        out_shape=[jax.ShapeDtypeStruct((rows // NZ, lanes), BF)] * NZ,
        compiler_params=params(28),
        cost_estimate=pl.CostEstimate(flops=8 * rows * depth * width, bytes_accessed=2 * depth * (rows + 4 * width), transcendentals=0),
        name="dense_in",
    )(z, x, gain, *weights)


def silu(value):
    return value / (1.0 + jnp.exp(-value))


def expert_in_kernel(z_ref, *refs):
    xs, gates, ups, out = refs[:4], refs[4:8], refs[8:12], refs[12]
    rows = xs[0].shape[0]
    depth = gates[0].shape[0]
    half = depth // 2
    row, col = grid_of((rows // 2, rows))
    picks = [onehot(col == 2 * row + i) for i in range(2)]
    lane = lax.broadcasted_iota(jnp.int32, (1, 128), 1)
    gate, up, total = None, None, None
    for m in range(NZ):
        head, rest = xs[m][:, :depth], xs[m][:, depth:]
        even, odd = exact(picks[0], rest), exact(picks[1], rest[:, :half])
        x = jnp.concatenate([head, jnp.concatenate([even[:, :half], odd], axis=1)], axis=0)
        square = jnp.concatenate(
            [
                jnp.where(lane < 2, rest[:, half:].astype(F32), 0.0),
                jnp.where((lane >= 2) & (lane < 4), even[:, half:].astype(F32), 0.0),
            ],
            axis=0,
        )
        one = jnp.dot(x, gates[m][...], preferred_element_type=F32)
        two = jnp.dot(x, ups[m][...], preferred_element_type=F32)
        gate = one if gate is None else gate + one
        up = two if up is None else up + two
        total = square if total is None else total + square
    scale = lax.rsqrt(jnp.sum(total, axis=1, keepdims=True) / D + EPS)
    out[...] = (silu(gate * scale) * (up * scale)).astype(BF)


def expert_in(z, xs, gate, up):
    depth, width = gate.shape
    rows, lanes = xs[0].shape
    ws = [pl.BlockSpec((depth // NZ, width), lambda i, z, m=m: (lax.rem(z[0] + m, NZ), 0)) for m in range(NZ)]
    total = rows * 3 // 2
    return pl.pallas_call(
        expert_in_kernel,
        grid_spec=pltpu.PrefetchScalarGridSpec(
            num_scalar_prefetch=1,
            grid=(1,),
            in_specs=[pl.BlockSpec((rows, lanes), lambda i, z: (0, 0))] * NZ + ws + ws,
            out_specs=pl.BlockSpec((total, width), lambda i, z: (0, 0)),
        ),
        out_shape=jax.ShapeDtypeStruct((total, width), BF),
        compiler_params=params(28),
        cost_estimate=pl.CostEstimate(flops=4 * total * depth * width, bytes_accessed=4 * depth * width, transcendentals=0),
        name="expert_in",
    )(z, *xs, *[gate] * 4, *[up] * 4)


def expert_out_kernel(z_ref, *refs):
    hidden, weights, out, wide = refs[:4], refs[4:8], refs[8], refs[9]
    step = pl.program_id(0)
    rows = out.shape[0]

    @pl.when(step == 0)
    def _():
        row, col = grid_of((rows, rows // 2))
        order = onehot(col == row >> 1)
        for k in range(NZ):
            wide[k, :rows] = hidden[k][:rows]
            wide[k, rows:] = exact(order, hidden[k][rows:])

    width = weights[0].shape[1]
    half = width // 2
    even = (lax.broadcasted_iota(jnp.int32, (rows, 128), 0) & 1) == 0
    for n in range(0, width, 256):
        total = None
        for k in range(NZ):
            term = jnp.dot(wide[k], weights[k][:, n : n + 256], preferred_element_type=F32)
            total = term if total is None else total + term
        total = total.astype(BF)
        out[:, n : n + 256] = total[:rows]
        for i in (0, 128):
            lane = (n + i) % half
            part = total[rows:, i : i + 128]
            lanes = slice(width + lane, width + lane + 128)
            out[:, lanes] = part if n + i < half else jnp.where(even, out[:, lanes], part)


def expert_out(z, hidden, down, got):
    rows, width = hidden[0].shape
    columns = got[0].shape[1]
    steps = 1
    step = columns
    whole = (rows // 12 * 8, columns + columns // 2)
    return pl.pallas_call(
        expert_out_kernel,
        grid_spec=pltpu.PrefetchScalarGridSpec(
            num_scalar_prefetch=1,
            grid=(steps,),
            in_specs=[pl.BlockSpec((rows, width), lambda i, z: (0, 0))] * NZ
            + [pl.BlockSpec((width, step), lambda i, z: (0, z[0] * steps + i))]
            + [pl.BlockSpec((width, step), lambda i, z: (0, i))] * 3,
            out_specs=pl.BlockSpec(whole, lambda i, z: (0, 0)),
            scratch_shapes=[pltpu.VMEM((NZ, 2 * whole[0], width), BF)],
        ),
        out_shape=jax.ShapeDtypeStruct(whole, BF),
        compiler_params=params(),
        cost_estimate=pl.CostEstimate(flops=16 * whole[0] * width * columns, bytes_accessed=8 * width * columns, transcendentals=0),
        name="expert_out",
    )(z, *hidden, down, *got)


def two_dots(rows, own, got, out):
    depth = own.shape[0]
    total = jnp.dot(rows[:, :depth], own[...], preferred_element_type=F32)
    total = total + jnp.dot(rows[:, depth:], got[...], preferred_element_type=F32)
    out[...] = total.astype(BF)


def dense_out_kernel(z_ref, h0, h1, h2, h3, own, got, out, held):
    @pl.when(pl.program_id(0) == 0)
    def _():
        z = z_ref[0]
        for k, ref in enumerate((h0, h1, h2, h3)):
            at = pl.multiple_of(lax.rem(z + k, NZ) * 64, 64)
            held[pl.ds(at, 64), :] = ref[...]

    two_dots(held, own, got, out)


def out_proj_kernel(z_ref, h0, h1, h2, h3, own, got, out, held):
    @pl.when(pl.program_id(0) == 0)
    def _():
        z = z_ref[0]
        row, col = grid_of((held.shape[0], h0.shape[0]))
        match = col == (row >> 4) * 4 + (row & 3)
        total = None
        for k, ref in enumerate((h0, h1, h2, h3)):
            hit = match & (((row >> 2) & 3) == lax.rem(z + k, NZ))
            term = jnp.dot(onehot(hit), ref[...], preferred_element_type=F32)
            total = term if total is None else total + term
        held[...] = total.astype(BF)

    two_dots(held, own, got, out)


def plane_dot(kernel, z, blocks, own, got, name):
    depth, columns = own.shape
    step = columns
    weight = pl.BlockSpec((depth, step), lambda i, z: (0, i))
    return pl.pallas_call(
        kernel,
        grid_spec=pltpu.PrefetchScalarGridSpec(
            num_scalar_prefetch=1,
            grid=(columns // step,),
            in_specs=[pl.BlockSpec(blocks[0].shape, lambda i, z: (0, 0))] * NZ + [weight, weight],
            out_specs=pl.BlockSpec((256, step), lambda i, z: (0, i)),
            scratch_shapes=[pltpu.VMEM((256, 2 * depth), BF)],
        ),
        out_shape=jax.ShapeDtypeStruct((256, columns), BF),
        compiler_params=params(),
        cost_estimate=pl.CostEstimate(flops=1024 * depth * columns, bytes_accessed=4 * depth * columns, transcendentals=0),
        name=name,
    )(z, *blocks, own, got)


def shards(
    queries, kv_cache, new_latent, lengths, residual, gain_first, gain_second, value_proj, out_proj,
    dense_gate, dense_up, dense_down, route_ids, route_gates, expert_gate, expert_up, expert_down,
):
    z = lax.axis_index("z")
    c = lax.axis_index("c")
    latent_dim = value_proj.shape[1]
    quarter = residual.shape[1]

    zs = z.astype(jnp.int32).reshape(1)

    def pick(w, k, axis):
        return lax.dynamic_slice_in_dim(w, lax.rem(z + k, NZ) * quarter, quarter, axis)

    def cut(w, axis, which):
        return {k: pick(w, NZ - k, axis) for k in which}

    def tied(value, *groups):
        flat = [group[k] for group in groups for k in group]
        value, *flat = lax.optimization_barrier((value, *flat))
        at = iter(flat)
        return (value, *[{k: next(at) for k in group} for group in groups])

    def fetch(group):
        return {k: zsend(group[k], NZ - k) for k in group}

    only = lambda group, *which: {k: group[k] for k in which}
    picks = jnp.concatenate([route_ids.astype(F32), route_gates], axis=1)
    picks = jnp.concatenate([picks, swap_core(picks)], axis=0)
    picks = jnp.concatenate([picks, jnp.broadcast_to(c.astype(F32), (picks.shape[0], 1))], axis=1)
    hots, combs = route(picks, route_ids.shape[1])
    gain_a, gain_b = gain_first.reshape(1, -1), gain_second.reshape(1, -1)

    latents = attend(lengths, c.astype(jnp.int32).reshape(1), queries, kv_cache, new_latent, latent_dim)
    moved = lax.all_to_all(latents.reshape(16, 32, -1), YX, 0, 0, tiled=True)
    moved, value_got = lax.optimization_barrier((moved, swap_core(value_proj)))
    moved, gain_a, gain_b, hots, combs = lax.optimization_barrier((moved, gain_a, gain_b, hots, combs))
    moved, down_cut = tied(moved, cut(expert_down[0], 1, (1, 2, 3)))
    moved, mine = lax.optimization_barrier((moved, out_proj))
    out_got = swap_core(mine)
    rows = zgather(head_values(moved.reshape(512, -1), value_proj, value_got))
    rows, out_got, *mine = lax.optimization_barrier((rows, out_got, dense_gate, dense_up, dense_down))
    dense_got = [swap_core(weight) for weight in mine]
    rows, down_cut = tied(rows, down_cut)
    down_a = fetch(only(down_cut, 1, 3))
    parts = plane_scatter(plane_dot(out_proj_kernel, zs, rows, out_proj, out_got, "out_proj"))
    parts, down_a, down_cut = tied(parts, down_a, only(down_cut, 2))
    parts, *dense_got = lax.optimization_barrier((parts, *dense_got))
    first, spread = first_sum(parts, residual)
    own = lax.all_to_all(spread, YX, 0, 0, tiled=True).reshape(256, -1)
    width = 2 * dense_gate.shape[1]

    def activate(summed):
        scale = lax.rsqrt((summed[:, 2 * width] + summed[:, 2 * width + 1]) / D + EPS)[:, None]
        gate_act = summed[:, :width] * scale
        return (jax.nn.silu(gate_act) * (summed[:, width : 2 * width] * scale)).astype(BF)

    blocks = dense_in(zs, own, gain_a, [dense_gate, dense_got[0], dense_up, dense_got[1]])
    hidden = zgather(activate(zscatter(blocks)))
    hidden, down_cut = tied(hidden, down_cut)
    down_b = fetch(down_cut)
    parts = plane_scatter(plane_dot(dense_out_kernel, zs, hidden, dense_down, dense_got[2], "dense_out"))
    parts, down_b = tied(parts, down_b)
    second, scaled = second_sum(parts, first, gain_b)

    across = lambda rows, flip: lax.ppermute(
        rows, ("c", "z"), [(c0 * NZ + z0, (c0 ^ flip) * NZ + (z0 + 2) % NZ) for c0 in range(2) for z0 in range(NZ)]
    )
    far = jnp.concatenate([across(scaled, 0), across(scaled, 1)], axis=0)
    scaled = jnp.concatenate([scaled, swap_core(scaled)], axis=0)
    spread = lambda rows: lax.all_to_all(rows.reshape(16, 8, -1), YX, 0, 0, tiled=True).reshape(128, -1)
    near, far = lax.optimization_barrier((pack(scaled, hots, quarter), far))
    near = spread(near)
    near, far = lax.optimization_barrier((near, far))
    ahead, behind = zsend(near, NZ - 1), zsend(near, 1)
    far = spread(pack(far, hots, quarter))
    expert_hidden = expert_in(zs, [near, ahead, far, behind], expert_gate[0], expert_up[0])
    result = expert_out(zs, zgather(expert_hidden), expert_down[0], [down_a[1], down_b[2], down_a[3]])
    returned = lax.all_to_all(result.reshape(16, 8, -1), YX, 0, 0, tiled=True).reshape(128, -1)
    total, theirs = combine(returned, combs, second)
    return (total + swap_core(theirs)).astype(BF)


def solution(mesh):
    grid = Mesh(mesh.devices.reshape(4, 4, 2, 4), ("y", "x", "c", "z"))
    ep = ("y", "x", "c")
    both = ("y", "x", "c", "z")
    return jax.shard_map(
        shards,
        mesh=grid,
        in_specs=(
            P(both, None, None),
            P(both, None, None),
            P(both, None),
            P(both),
            P(ep, "z"),
            P("z"),
            P("z"),
            P(ep, None, None),
            P(ep, "z"),
            P("z", ep),
            P("z", ep),
            P(ep, "z"),
            P(ep, None),
            P(ep, None),
            P(ep, None, "z"),
            P(ep, None, "z"),
            P(ep, "z", None),
        ),
        out_specs=P(ep, "z"),
        check_vma=False,
    )
```
